32 devices in a mesh: groups: 2 (over x), blk: 16 (over z, y, core).
Axes of the slice: x: 2, y: 2, z: 4, core: 2. Of those that a mesh axis runs over, the one named last changes fastest.
Arguments:
- projections: bfloat16 [2, 512, 8192], P(None, ('groups', 'blk')), parts along dimension 1, may hold values from -12 to 12
- images: bfloat16 [64, 8192], P(('groups', 'blk')), parts along dimension 0, may hold values from -16 to 16, as said below
- ctf_group: int32 [64], P(('groups', 'blk')), parts along dimension 0, may hold values from 0 to 15
- shift_offsets: int32 [64, 9, 2], P(('groups', 'blk')), parts along dimension 0, may hold values from -8 to 8
- shell_limit: int32 [64], P(('groups', 'blk')), parts along dimension 0, may hold values from 16 to 63
- ctf_table: float32 [32, 4096], P('groups'), parts along dimension 0, may hold values from -1 to 1
- noise_weight: float32 [32, 4096], P('groups'), parts along dimension 0, may hold values from 0.25 to 4
Outputs:
- slices: float32 [2, 512, 8192], P(None, ('groups', 'blk')), parts along dimension 1
- best_posterior: float32 [64], P(('groups', 'blk')), parts along dimension 0
- log_total: float32 [64], P(('groups', 'blk')), parts along dimension 0
The draws below stay inside these ranges and needn't reach their ends.
There are 2 independent parts, one for each index of `groups`. The reference program is written for one: setup_inputs(seed, part) draws one part's arguments, and reference() takes and returns one part's arrays. A program takes and returns all parts, laid end to end along the dimension named above; each array names one. Nothing has to cross between parts.
Inputs may be any that keep to these rules, and one draw needn't show every extreme that they name: `images`: image coefficients.
All inputs are finite; a program needn't handle non-finite values.
Results may differ from the reference program's by a relative error of at most 0.006.
Values may be sent and summed in bfloat16 or wider, within the bound.
No kernel may reach another device: no remote copies, remote signals or barrier semaphores. Data moves between devices by JAX's collectives and lax.ppermute only.
A program may use at most 128 MiB of HBM per device.

```python
import math
import jax
import jax.numpy as jnp
from jax import lax

F = 4096
KY = 64
IMG = 256
S = 9
BATCHES = 2
G = 16
P_SIZE = 32
ORIENT = 256


def group_values(key):
    return jax.random.randint(jax.random.fold_in(key, 11), (P_SIZE,), 0, G, dtype=jnp.int32)


def offset_values(key):
    return jax.random.randint(jax.random.fold_in(key, 12), (P_SIZE, S, 2), -8, 9, dtype=jnp.int32)


def ctf_values(key):
    drawn = jax.random.uniform(jax.random.fold_in(key, 13), (G, F), jnp.float32, -1.0, 1.0)
    return drawn


def projection_values(key):
    row_total = BATCHES * ORIENT
    drawn = jax.random.normal(jax.random.fold_in(key, 14), (row_total, 2 * F), jnp.float32)
    return jnp.clip(drawn, -6.0, 6.0)


def draw_projections(key, part):
    values = projection_values(key)
    return values.reshape(BATCHES, ORIENT, 2 * F).astype(jnp.bfloat16)


def draw_ctf_group(key, part):
    return group_values(key)


def draw_shift_offsets(key, part):
    return offset_values(key)


def draw_ctf_table(key, part):
    values = ctf_values(key)
    return values.astype(jnp.float32)


def draw_images(key, part):
    drawn = jnp.clip(jax.random.normal(jax.random.fold_in(key, 31), (P_SIZE, 2 * F), jnp.float32), -6.0, 6.0)
    return drawn.astype(jnp.bfloat16)


def set_ends(values, stream_key, low, high):
    spot = [jax.random.randint(jax.random.fold_in(stream_key, axis), (), 0, length) for axis, length in enumerate(values.shape)]
    main_axis = values.shape.index(max(values.shape))
    next_to = spot[:main_axis] + [(spot[main_axis] + 1) % values.shape[main_axis]] + spot[main_axis + 1:]
    return values.at[tuple(spot)].set(low).at[tuple(next_to)].set(high)


def setup_inputs(seed: int = 0, part: int = 0) -> dict:
    splits = jax.random.split(jax.random.key(seed), 8)
    own_keys = jax.random.split(jax.random.fold_in(splits[7], part), 8)
    return {
        "projections": draw_projections(jax.random.fold_in(jax.random.fold_in(splits[7], part), 71), part),
        "images": draw_images(jax.random.fold_in(jax.random.fold_in(splits[7], part), 71), part),
        "ctf_group": draw_ctf_group(jax.random.fold_in(jax.random.fold_in(splits[7], part), 71), part),
        "shift_offsets": draw_shift_offsets(jax.random.fold_in(jax.random.fold_in(splits[7], part), 71), part),
        "shell_limit": set_ends(jax.random.randint(own_keys[4], (P_SIZE,), KY // 4, KY // 2 + F // KY // 2), jax.random.fold_in(own_keys[4], 1), KY // 4, (KY // 2 + F // KY // 2) - 1).astype(jnp.int32),
        "ctf_table": draw_ctf_table(jax.random.fold_in(jax.random.fold_in(splits[7], part), 71), part),
        "noise_weight": jnp.clip(jnp.exp(jax.random.uniform(own_keys[6], (G, F), jnp.float32, math.log(0.25), math.log(4.0))), 0.25, 4.0),
    }


def frequencies(half_width):
    positions = jnp.arange(half_width, dtype=jnp.int32)
    return (positions // KY, positions % KY - KY // 2)

def shift_factors(offsets, half_width):
    row_count = offsets.shape[0]
    shift_count = offsets.shape[1]
    row_freq = jnp.arange(half_width // KY, dtype=jnp.int32)
    col_freq = jnp.arange(KY, dtype=jnp.int32) - KY // 2
    turns_x = row_freq[None, None, :] * offsets[:, :, 0:1] % IMG
    turns_y = col_freq[None, None, :] * offsets[:, :, 1:2] % IMG
    angle_x = turns_x.astype(jnp.float32) * (2.0 * math.pi / IMG)
    angle_y = turns_y.astype(jnp.float32) * (2.0 * math.pi / IMG)
    cosine_x = jnp.cos(angle_x)[:, :, :, None]
    sine_x = jnp.sin(angle_x)[:, :, :, None]
    cosine_y = jnp.cos(angle_y)[:, :, None, :]
    sine_y = jnp.sin(angle_y)[:, :, None, :]
    cosine = cosine_x * cosine_y - sine_x * sine_y
    sine_part = sine_x * cosine_y + cosine_x * sine_y
    return (cosine.reshape(row_count, shift_count, half_width), sine_part.reshape(row_count, shift_count, half_width))

def particle_terms(image_rows, ctf_rows, weight_rows, offsets, limits, freq_x, freq_y):
    half_width = image_rows.shape[1] // 2
    image_real = image_rows[:, :half_width].astype(jnp.float32)
    image_imag = image_rows[:, half_width:].astype(jnp.float32)
    radius_sq = freq_x * freq_x + freq_y * freq_y
    inside = (radius_sq[None, :] < (limits * limits)[:, None]).astype(jnp.float32)
    masked_weight = inside * weight_rows
    ctf_weight = masked_weight * ctf_rows
    norm_term = lax.optimization_barrier(jnp.sum(masked_weight * (image_real * image_real + image_imag * image_imag), axis=1))
    quad_weight = ctf_weight * ctf_rows
    cosine, sine_part = shift_factors(offsets, half_width)
    shift_real = image_real[:, None, :] * cosine + image_imag[:, None, :] * sine_part
    shift_imag = image_imag[:, None, :] * cosine - image_real[:, None, :] * sine_part
    weighted = jnp.concatenate([ctf_weight[:, None, :] * shift_real, ctf_weight[:, None, :] * shift_imag], axis=2).astype(jnp.bfloat16)
    return (weighted, norm_term, quad_weight)

def reference(projections, images, ctf_group, shift_offsets, shell_limit, ctf_table, noise_weight):
    full_width = images.shape[1]
    half_width = full_width // 2
    candidates = BATCHES * ORIENT
    flat_proj = projections.reshape(candidates, full_width)
    proj_real = flat_proj[:, :half_width].astype(jnp.float32)
    proj_imag = flat_proj[:, half_width:].astype(jnp.float32)
    proj_power = proj_real * proj_real + proj_imag * proj_imag
    flat_wide = flat_proj.astype(jnp.float32)
    freq_x, freq_y = frequencies(half_width)
    score_scale = 0.5 / math.sqrt(half_width)
    block_rows = 16
    block_count = P_SIZE // block_rows

    def split_rows(source):
        return source.reshape((block_count, block_rows) + source.shape[1:])

    def block_terms(members):
        image_rows, groups, offsets, limits = members
        return particle_terms(image_rows, ctf_table[groups], noise_weight[groups], offsets, limits, freq_x, freq_y)

    def score_block(members):
        weighted, norm_term, quad_weight = block_terms(members)
        cross_term = lax.dot_general(weighted.astype(jnp.float32), flat_wide, (((2,), (1,)), ((), ())))
        quad_term = lax.dot_general(quad_weight, proj_power, (((1,), (1,)), ((), ())), precision=lax.Precision.HIGHEST)
        return -(norm_term[:, None, None] - 2.0 * cross_term + quad_term[:, None, :]) * score_scale
    members = (split_rows(images), split_rows(ctf_group), split_rows(shift_offsets), split_rows(shell_limit))
    scores = lax.map(score_block, members).reshape(P_SIZE, S, candidates)
    score_top = lax.optimization_barrier(jnp.max(scores, axis=(1, 2)))
    exp_total = lax.optimization_barrier(jnp.sum(jnp.exp(scores - score_top[:, None, None]), axis=(1, 2)))
    log_total = score_top + jnp.log(exp_total)
    best_posterior = jnp.exp(score_top - log_total)

    def add_block(carry, packed):
        member_block, score_values, log_block = packed
        weighted = block_terms(member_block)[0]
        posterior = jnp.exp(score_values - log_block[:, None, None]).astype(jnp.bfloat16)
        contrib = lax.dot_general(posterior.astype(jnp.float32), weighted.astype(jnp.float32), (((0, 1), (0, 1)), ((), ())))
        return (carry + contrib, None)
    zero_slices = jnp.zeros((candidates, full_width), jnp.float32)
    summed, unused_out = lax.scan(add_block, zero_slices, (members, split_rows(scores), split_rows(log_total)))
    slices = (summed * (BATCHES * ORIENT / P_SIZE)).reshape(BATCHES, ORIENT, full_width)
    return (slices, best_posterior, log_total)
```

```python
import functools
import math

import jax
import jax.numpy as jnp
from jax import lax
from jax.experimental import pallas as pl
from jax.experimental.pallas import tpu as pltpu
from jax.sharding import PartitionSpec as P

KY = 64
IMG = 256
LANES = 128
ROWS = 16
LIMIT_AT = 1
X_AT = 16
Y_AT = 48

VMEM = pl.BlockSpec(memory_space=pltpu.VMEM)
SMEM = pl.BlockSpec(memory_space=pltpu.SMEM)
NT = (((1,), (1,)), ((), ()))


def sin_cos(turns):
    quarter = IMG // 4
    wrapped = (turns + quarter // 2) & (IMG - 1)
    quadrant = wrapped >> int(math.log2(quarter))
    angle = (wrapped - quadrant * quarter - quarter // 2).astype(jnp.float32) * (
        2.0 * math.pi / IMG
    )
    square = angle * angle
    even = 1.0 + square * (
        -1.0 / 2 + square * (1.0 / 24 + square * (-1.0 / 720 + square * (1.0 / 40320)))
    )
    odd = angle * (
        1.0
        + square
        * (-1.0 / 6 + square * (1.0 / 120 + square * (-1.0 / 5040 + square * (1.0 / 362880))))
    )
    swapped = (quadrant & 1) == 1
    cosine = jnp.where(swapped, odd, even)
    sine = jnp.where(swapped, even, odd)
    cosine = jnp.where((quadrant == 1) | (quadrant == 2), -cosine, cosine)
    sine = jnp.where(quadrant >= 2, -sine, sine)
    return cosine, sine


def split_halves(value):
    high = value.astype(jnp.bfloat16)
    return high, (value - high.astype(jnp.float32)).astype(jnp.bfloat16)


def power_kernel(own_ref, other_ref, both_ref, high_ref, low_ref):
    rows, full = own_ref.shape
    half = full // 2
    for place, ref in enumerate((own_ref, other_ref)):
        at = pl.ds(place * rows, rows)
        both_ref[at, :] = ref[...]
        real = ref[:, :half].astype(jnp.float32)
        imag = ref[:, half:].astype(jnp.float32)
        high, low = split_halves(real * real + imag * imag)
        high_ref[at, :] = high
        low_ref[at, :] = low


def score_kernel(
    pieces_count,
    shifts,
    order_ref,
    *refs,
):
    pieces = refs[:pieces_count]
    both_ref, high_ref, low_ref, ctf_ref, noise_ref = refs[pieces_count : pieces_count + 5]
    weighted_ref, exps_ref, stats_ref = refs[pieces_count + 5 : pieces_count + 8]
    image_ref, real_ref, imag_ref, cross_ref, square_ref = refs[pieces_count + 8 :]
    half = ctf_ref.shape[1]
    full = 2 * half
    groups = ctf_ref.shape[0]
    candidates = both_ref.shape[0]
    particles = image_ref.shape[0]
    per_device = pieces[0].shape[1]
    scale = 0.5 / math.sqrt(half)
    place = 0
    for piece in pieces:
        for row in range(piece.shape[0]):
            start = order_ref[place] * per_device
            values = piece[row].astype(jnp.float32)
            for sub in range(per_device):
                image_ref[pl.ds(start + sub, 1), :] = values[sub : sub + 1]
            place += 1

    lane = lax.broadcasted_iota(jnp.int32, (ROWS, LANES), 1)
    block_rows = shifts * ROWS

    def block(index, carry):
        rows = pl.ds(pl.multiple_of(index * ROWS, ROWS), ROWS)
        first = pl.multiple_of(index * block_rows, ROWS)
        numbers = image_ref[rows, full:]
        one_hot = (
            numbers[:, :1].astype(jnp.int32)
            == lax.broadcasted_iota(jnp.int32, (ROWS, groups), 1)
        ).astype(jnp.float32)
        ctf = jnp.dot(
            one_hot,
            ctf_ref[...],
            precision=lax.Precision.HIGHEST,
            preferred_element_type=jnp.float32,
        )
        noise = jnp.dot(
            one_hot,
            noise_ref[...],
            precision=lax.Precision.HIGHEST,
            preferred_element_type=jnp.float32,
        )
        limit = numbers[:, LIMIT_AT : LIMIT_AT + 1].astype(jnp.int32)
        position = lax.broadcasted_iota(jnp.int32, (1, half), 1)
        freq_x = position // KY
        freq_y = position % KY - KY // 2
        weight = jnp.where(freq_x * freq_x + freq_y * freq_y < limit * limit, noise, 0.0)
        ctf_weight = weight * ctf
        real = image_ref[rows, :half]
        imag = image_ref[rows, half:full]
        norm = jnp.sum(weight * (real * real + imag * imag), axis=1, keepdims=True)
        real_ref[...] = ctf_weight * real
        imag_ref[...] = ctf_weight * imag
        quad_high, quad_low = split_halves(ctf_weight * ctf)
        quad_weight = jnp.concatenate([quad_high, quad_low], axis=0)
        quad = lax.dot_general(
            quad_weight, high_ref[...], NT, preferred_element_type=jnp.float32
        ) + lax.dot_general(quad_weight, low_ref[...], NT, preferred_element_type=jnp.float32)
        quad = quad[:ROWS] + quad[ROWS:]

        numbers_int = numbers.astype(jnp.int32)
        step_cos, step_sin = sin_cos(numbers_int * (LANES // KY))
        for shift in range(shifts):
            turns = (
                (lane // KY) * numbers_int[:, X_AT + shift : X_AT + shift + 1]
                + (lane % KY - KY // 2) * numbers_int[:, Y_AT + shift : Y_AT + shift + 1]
            )
            cosine, sine = sin_cos(turns)
            turn_cos = step_cos[:, X_AT + shift : X_AT + shift + 1]
            turn_sin = step_sin[:, X_AT + shift : X_AT + shift + 1]
            cosine_before = cosine * turn_cos + sine * turn_sin
            sine_before = sine * turn_cos - cosine * turn_sin
            double = jnp.broadcast_to(2.0 * turn_cos, (ROWS, LANES))
            out_rows = pl.ds(first + shift * ROWS, ROWS)
            for chunk in range(half // LANES):
                at = pl.ds(chunk * LANES, LANES)
                real = real_ref[:, at]
                imag = imag_ref[:, at]
                weighted_ref[out_rows, at] = (real * cosine + imag * sine).astype(jnp.bfloat16)
                weighted_ref[out_rows, pl.ds(half + chunk * LANES, LANES)] = (
                    imag * cosine - real * sine
                ).astype(jnp.bfloat16)
                cosine, cosine_before = double * cosine - cosine_before, cosine
                sine, sine_before = double * sine - sine_before, sine

        cross_ref[...] = lax.dot_general(
            weighted_ref[pl.ds(first, block_rows), :],
            both_ref[...],
            NT,
            preferred_element_type=jnp.float32,
        )
        base = norm + quad
        scores = [
            -(base - 2.0 * cross_ref[pl.ds(shift * ROWS, ROWS), :]) * scale
            for shift in range(shifts)
        ]
        top = jnp.max(functools.reduce(jnp.maximum, scores), axis=1, keepdims=True)
        exps = [jnp.exp(score - top) for score in scores]
        total = jnp.sum(functools.reduce(jnp.add, exps), axis=1, keepdims=True)
        top_wide = jnp.broadcast_to(top, (ROWS, LANES - candidates))
        total_wide = jnp.broadcast_to(total, (ROWS, LANES - candidates))
        spare = lax.broadcasted_iota(jnp.int32, top_wide.shape, 1)
        tail = jnp.where(spare == 0, top_wide, total_wide)
        for shift in range(shifts):
            square_ref[pl.ds(shift * ROWS, ROWS), :] = jnp.concatenate(
                [exps[shift], tail], axis=1
            )
        turned = square_ref[...].T
        exps_ref[index] = turned[:candidates, :block_rows]
        for target in range(stats_ref.shape[0]):
            stats_ref[target, index] = turned[candidates : candidates + 2, :block_rows]
        return carry

    lax.fori_loop(0, particles // ROWS, block, 0)


def slice_kernel(
    scale,
    own_ref,
    stats_ref,
    mine_ref,
    exps_ref,
    weighted_ref,
    keep_ref,
    send_ref,
    best_ref,
    log_ref,
    posterior_ref,
):
    blocks, candidates, block_rows = exps_ref.shape
    half_rows = candidates // 2
    per_device = best_ref.shape[0]
    for block in range(blocks):
        tops = stats_ref[:, block, 0, :]
        top = jnp.max(tops, axis=0, keepdims=True)
        total = jnp.sum(stats_ref[:, block, 1, :] * jnp.exp(tops - top), axis=0, keepdims=True)
        log_total = top + jnp.log(total)
        factor = jnp.exp(mine_ref[0, block, 0:1, :] - log_total)
        posterior_ref[block] = (exps_ref[block] * factor).astype(jnp.bfloat16)
        best = jnp.exp(top - log_total)
        column = lax.broadcasted_iota(jnp.int32, (1, block_rows), 1)
        for row in range(per_device):
            particle = own_ref[0] * per_device + row

            @pl.when(particle // ROWS == block)
            def _():
                chosen = column == particle % ROWS
                best_ref[row] = jnp.sum(jnp.where(chosen, best, 0.0))
                log_ref[row] = jnp.sum(jnp.where(chosen, log_total, 0.0))

    width = 1024
    for start in range(0, weighted_ref.shape[1], width):
        at = pl.ds(start, width)
        summed = jnp.zeros((candidates, width), jnp.float32)
        for block in range(blocks):
            summed = summed + jnp.dot(
                posterior_ref[block],
                weighted_ref[pl.ds(block * block_rows, block_rows), at],
                preferred_element_type=jnp.float32,
            )
        summed = summed * scale
        keep_ref[:, at] = summed[:half_rows]
        send_ref[:, at] = summed[half_rows:].astype(send_ref.dtype)


def local(
    axis_size, projections, images, ctf_group, shift_offsets, shell_limit, ctf_table, noise_weight
):
    batch_count, orient_dev, full = projections.shape
    half = full // 2
    own_rows = batch_count * orient_dev
    candidates = 2 * own_rows
    per_device = images.shape[0]
    shifts = shift_offsets.shape[1]
    chips = axis_size // 2
    particles = chips * per_device
    blocks = particles // ROWS
    block_rows = shifts * ROWS
    chip = lax.axis_index("blk") // 2
    params = pltpu.CompilerParams(vmem_limit_bytes=48 * 1024 * 1024)

    def swap(value, mask):
        return lax.ppermute(value, "blk", [(i, i ^ mask) for i in range(axis_size)])

    offsets = shift_offsets.astype(jnp.bfloat16)

    def at_column(value, column):
        return jnp.pad(value, ((0, 0), (column, LANES - column - value.shape[1])))

    numbers = (
        at_column(ctf_group[:, None].astype(jnp.bfloat16), 0)
        + at_column(shell_limit[:, None].astype(jnp.bfloat16), LIMIT_AT)
        + at_column(offsets[:, :, 0], X_AT)
        + at_column(offsets[:, :, 1], Y_AT)
    )
    packed = jnp.concatenate([images, numbers], axis=1)[None]
    if chips <= 8:
        pair = jnp.concatenate([packed, swap(packed, 2)], axis=0) if chips > 1 else packed
        pieces = [pair] + [swap(pair, mask) for mask in range(4, axis_size, 4)]
        order = jnp.arange(chips, dtype=jnp.int32) ^ chip
    else:
        same_core = [[2 * c + core for c in range(chips)] for core in range(2)]
        pieces = [
            lax.all_gather(packed, "blk", axis=0, tiled=True, axis_index_groups=same_core)
        ]
        order = jnp.arange(chips, dtype=jnp.int32)

    flat = projections.reshape(own_rows, full)
    other = swap(flat, 1)
    both, high, low = pl.pallas_call(
        power_kernel,
        out_shape=(
            jax.ShapeDtypeStruct((candidates, full), jnp.bfloat16),
            jax.ShapeDtypeStruct((candidates, half), jnp.bfloat16),
            jax.ShapeDtypeStruct((candidates, half), jnp.bfloat16),
        ),
        in_specs=[VMEM] * 2,
        out_specs=(VMEM,) * 3,
        compiler_params=params,
        cost_estimate=pl.CostEstimate(
            flops=8 * candidates * full, bytes_accessed=4 * candidates * full, transcendentals=0
        ),
        name="power",
    )(flat, other)

    weighted, exps, stats = pl.pallas_call(
        functools.partial(score_kernel, len(pieces), shifts),
        out_shape=(
            jax.ShapeDtypeStruct((blocks * block_rows, full), jnp.bfloat16),
            jax.ShapeDtypeStruct((blocks, candidates, block_rows), jnp.float32),
            jax.ShapeDtypeStruct((chips, blocks, 2, block_rows), jnp.float32),
        ),
        in_specs=[SMEM] + [VMEM] * (len(pieces) + 5),
        out_specs=(VMEM,) * 3,
        scratch_shapes=[
            pltpu.VMEM((particles, full + LANES), jnp.float32),
            pltpu.VMEM((ROWS, half), jnp.float32),
            pltpu.VMEM((ROWS, half), jnp.float32),
            pltpu.VMEM((block_rows, candidates), jnp.float32),
            pltpu.VMEM((-(-block_rows // LANES) * LANES, LANES), jnp.float32),
        ],
        compiler_params=params,
        name="scores",
    )(order, *pieces, both, high, low, ctf_table, noise_weight)

    same_core = [[2 * c + core for c in range(chips)] for core in range(2)]
    gathered = lax.all_to_all(stats, "blk", 0, 0, axis_index_groups=same_core)

    keep, send, best_posterior, log_total = pl.pallas_call(
        functools.partial(slice_kernel, own_rows / per_device),
        out_shape=(
            jax.ShapeDtypeStruct((own_rows, full), jnp.float32),
            jax.ShapeDtypeStruct((own_rows, full), jnp.float32),
            jax.ShapeDtypeStruct((per_device,), jnp.float32),
            jax.ShapeDtypeStruct((per_device,), jnp.float32),
        ),
        in_specs=[SMEM] + [VMEM] * 4,
        out_specs=(VMEM, VMEM, SMEM, SMEM),
        scratch_shapes=[pltpu.VMEM((blocks, candidates, block_rows), jnp.bfloat16)],
        compiler_params=params,
        name="slices",
    )(chip.reshape(1).astype(jnp.int32), gathered, stats, exps, weighted)

    slices = (keep + swap(send, 1)).reshape(batch_count, orient_dev, full)
    return (slices, best_posterior, log_total)


def solution(mesh):
    in_specs = (
        P(None, ("groups", "blk"), None),
        P(("groups", "blk"), None),
        P(("groups", "blk")),
        P(("groups", "blk"), None, None),
        P(("groups", "blk")),
        P("groups", None),
        P("groups", None),
    )
    out_specs = (P(None, ("groups", "blk"), None), P(("groups", "blk")), P(("groups", "blk")))
    return jax.shard_map(
        functools.partial(local, mesh.shape["blk"]),
        mesh=mesh,
        in_specs=in_specs,
        out_specs=out_specs,
        check_vma=False,
    )
```

```python
import functools
import math

import jax
import jax.numpy as jnp
from jax import lax
from jax.experimental import pallas as pl
from jax.experimental.pallas import tpu as pltpu
from jax.sharding import PartitionSpec as P

KY = 64
IMG = 256
LANES = 128
ROWS = 16
LIMIT_AT = 1
X_AT = 16
Y_AT = 48

VMEM = pl.BlockSpec(memory_space=pltpu.VMEM)
HBM = pl.BlockSpec(memory_space=pltpu.HBM)
SMEM = pl.BlockSpec(memory_space=pltpu.SMEM)
NT = (((1,), (1,)), ((), ()))


def sin_cos(turns):
    quarter = IMG // 4
    wrapped = (turns + quarter // 2) & (IMG - 1)
    quadrant = wrapped >> int(math.log2(quarter))
    angle = (wrapped - quadrant * quarter - quarter // 2).astype(jnp.float32) * (
        2.0 * math.pi / IMG
    )
    square = angle * angle
    even = 1.0 + square * (
        -1.0 / 2 + square * (1.0 / 24 + square * (-1.0 / 720 + square * (1.0 / 40320)))
    )
    odd = angle * (
        1.0
        + square
        * (-1.0 / 6 + square * (1.0 / 120 + square * (-1.0 / 5040 + square * (1.0 / 362880))))
    )
    swapped = (quadrant & 1) == 1
    cosine = jnp.where(swapped, odd, even)
    sine = jnp.where(swapped, even, odd)
    cosine = jnp.where((quadrant == 1) | (quadrant == 2), -cosine, cosine)
    sine = jnp.where(quadrant >= 2, -sine, sine)
    return cosine, sine


def split_halves(value):
    high = value.astype(jnp.bfloat16)
    return high, (value - high.astype(jnp.float32)).astype(jnp.bfloat16)


def pack_kernel(images_hbm, group_hbm, limit_hbm, offsets_hbm, packed_ref, group, limit, offsets, sems):
    per_device, full = images_hbm.shape
    shifts = offsets_hbm.shape[2]
    copies = [
        pltpu.make_async_copy(images_hbm, packed_ref.at[0, :, pl.ds(0, full)], sems.at[0]),
        pltpu.make_async_copy(group_hbm, group, sems.at[1]),
        pltpu.make_async_copy(limit_hbm, limit, sems.at[2]),
        pltpu.make_async_copy(offsets_hbm, offsets, sems.at[3]),
    ]
    for copy in copies:
        copy.start()
    for copy in copies[1:]:
        copy.wait()
    row = lax.broadcasted_iota(jnp.int32, (per_device, LANES), 0)
    lane = lax.broadcasted_iota(jnp.int32, (per_device, LANES), 1)
    numbers = jnp.zeros((per_device, LANES), jnp.int32)
    for particle in range(per_device):
        line = jnp.zeros((per_device, LANES), jnp.int32)
        line = jnp.where(lane == 0, group[particle], line)
        line = jnp.where(lane == LIMIT_AT, limit[particle], line)
        for shift in range(shifts):
            line = jnp.where(lane == X_AT + shift, offsets[particle, 0, shift], line)
            line = jnp.where(lane == Y_AT + shift, offsets[particle, 1, shift], line)
        numbers = jnp.where(row == particle, line, numbers)
    packed_ref[0, :, pl.ds(full, LANES)] = numbers.astype(jnp.float32).astype(jnp.bfloat16)
    copies[0].wait()


def split_thirds(value):
    high = value.astype(jnp.bfloat16)
    rest = value - high.astype(jnp.float32)
    middle = rest.astype(jnp.bfloat16)
    return high, middle, (rest - middle.astype(jnp.float32)).astype(jnp.bfloat16)


def power_kernel(
    own_hbm,
    other_ref,
    ctf_hbm,
    noise_hbm,
    both_ref,
    high_ref,
    low_ref,
    table_ref,
    ctf_ref,
    noise_ref,
    sems,
):
    rows, full = other_ref.shape
    half = full // 2
    groups = ctf_ref.shape[0]
    copies = [
        pltpu.make_async_copy(own_hbm, both_ref.at[pl.ds(0, rows)], sems.at[0]),
        pltpu.make_async_copy(ctf_hbm, ctf_ref, sems.at[1]),
        pltpu.make_async_copy(noise_hbm, noise_ref, sems.at[2]),
    ]
    for copy in copies:
        copy.start()
    both_ref[pl.ds(rows, rows), :] = other_ref[...]
    for place in (1, 0):
        at = pl.ds(place * rows, rows)
        if place == 0:
            copies[0].wait()
        real = both_ref[at, :half].astype(jnp.float32)
        imag = both_ref[at, half:].astype(jnp.float32)
        high, low = split_halves(real * real + imag * imag)
        high_ref[at, :] = high
        low_ref[at, :] = low
    for place, ref in enumerate((ctf_ref, noise_ref)):
        copies[1 + place].wait()
        for third, part in enumerate(split_thirds(ref[...])):
            table_ref[pl.ds(third * groups, groups), pl.ds(place * half, half)] = part


def score_kernel(pieces_count, shifts, by_distance, place_ref, *refs):
    pieces = refs[:pieces_count]
    both_ref, high_ref, low_ref, table_ref = refs[pieces_count : pieces_count + 4]
    weighted_ref, exps_ref, exps_other_ref, stats_ref = refs[pieces_count + 4 : pieces_count + 8]
    image_ref, real_ref, imag_ref, cross_ref, square_ref = refs[pieces_count + 8 :]
    full = both_ref.shape[1]
    half = full // 2
    groups = table_ref.shape[0] // 3
    candidates = both_ref.shape[0]
    particles = image_ref.shape[0]
    per_device = pieces[0].shape[1]
    scale = 0.5 / math.sqrt(half)
    place = 0
    for piece in pieces:
        for row in range(piece.shape[0]):
            source = place_ref[0] ^ place if by_distance else place
            start = source * per_device
            values = piece[row].astype(jnp.float32)
            for sub in range(per_device):
                image_ref[pl.ds(start + sub, 1), :] = values[sub : sub + 1]
            place += 1

    lane = lax.broadcasted_iota(jnp.int32, (ROWS, LANES), 1)
    block_rows = shifts * ROWS

    def block(index, carry):
        rows = pl.ds(pl.multiple_of(index * ROWS, ROWS), ROWS)
        first = pl.multiple_of(index * block_rows, ROWS)
        numbers = image_ref[rows, full:]
        column = lax.broadcasted_iota(jnp.int32, (ROWS, 3 * groups), 1) % groups
        one_hot = (numbers[:, :1].astype(jnp.int32) == column).astype(jnp.bfloat16)
        tables = jnp.dot(one_hot, table_ref[...], preferred_element_type=jnp.float32)
        ctf = tables[:, :half]
        noise = tables[:, half:]
        limit = numbers[:, LIMIT_AT : LIMIT_AT + 1].astype(jnp.int32)
        position = lax.broadcasted_iota(jnp.int32, (1, half), 1)
        freq_x = position // KY
        freq_y = position % KY - KY // 2
        weight = jnp.where(freq_x * freq_x + freq_y * freq_y < limit * limit, noise, 0.0)
        ctf_weight = weight * ctf
        real = image_ref[rows, :half]
        imag = image_ref[rows, half:full]
        norm = jnp.sum(weight * (real * real + imag * imag), axis=1, keepdims=True)
        real_ref[...] = ctf_weight * real
        imag_ref[...] = ctf_weight * imag
        quad_high, quad_low = split_halves(ctf_weight * ctf)
        quad_weight = jnp.concatenate([quad_high, quad_low], axis=0)
        quad = lax.dot_general(
            quad_weight, high_ref[...], NT, preferred_element_type=jnp.float32
        ) + lax.dot_general(quad_weight, low_ref[...], NT, preferred_element_type=jnp.float32)
        quad = quad[:ROWS] + quad[ROWS:]

        numbers_int = numbers.astype(jnp.int32)
        step_cos, step_sin = sin_cos(numbers_int * (LANES // KY))
        for shift in range(shifts):
            turns = (
                (lane // KY) * numbers_int[:, X_AT + shift : X_AT + shift + 1]
                + (lane % KY - KY // 2) * numbers_int[:, Y_AT + shift : Y_AT + shift + 1]
            )
            cosine, sine = sin_cos(turns)
            turn_cos = step_cos[:, X_AT + shift : X_AT + shift + 1]
            turn_sin = step_sin[:, X_AT + shift : X_AT + shift + 1]
            cosine_before = cosine * turn_cos + sine * turn_sin
            sine_before = sine * turn_cos - cosine * turn_sin
            double = jnp.broadcast_to(2.0 * turn_cos, (ROWS, LANES))
            out_rows = pl.ds(first + shift * ROWS, ROWS)
            for chunk in range(half // LANES):
                at = pl.ds(chunk * LANES, LANES)
                real = real_ref[:, at]
                imag = imag_ref[:, at]
                weighted_ref[out_rows, at] = (real * cosine + imag * sine).astype(jnp.bfloat16)
                weighted_ref[out_rows, pl.ds(half + chunk * LANES, LANES)] = (
                    imag * cosine - real * sine
                ).astype(jnp.bfloat16)
                cosine, cosine_before = double * cosine - cosine_before, cosine
                sine, sine_before = double * sine - sine_before, sine

        cross_ref[...] = lax.dot_general(
            weighted_ref[pl.ds(first, block_rows), :],
            both_ref[...],
            NT,
            preferred_element_type=jnp.float32,
        )
        base = norm + quad
        scores = [
            -(base - 2.0 * cross_ref[pl.ds(shift * ROWS, ROWS), :]) * scale
            for shift in range(shifts)
        ]
        top = jnp.max(functools.reduce(jnp.maximum, scores), axis=1, keepdims=True)
        exps = [jnp.exp(score - top) for score in scores]
        total = jnp.sum(functools.reduce(jnp.add, exps), axis=1, keepdims=True)
        top_wide = jnp.broadcast_to(top, (ROWS, LANES - candidates))
        total_wide = jnp.broadcast_to(total, (ROWS, LANES - candidates))
        spare = lax.broadcasted_iota(jnp.int32, top_wide.shape, 1)
        tail = jnp.where(spare == 0, top_wide, total_wide)
        for shift in range(shifts):
            square_ref[pl.ds(shift * ROWS, ROWS), :] = jnp.concatenate(
                [exps[shift], tail], axis=1
            )
        turned = square_ref[...].T
        exps_ref[index] = turned[: candidates // 2, :block_rows]
        exps_other_ref[index] = turned[candidates // 2 : candidates, :block_rows]
        for target in range(stats_ref.shape[0]):
            stats_ref[target, index] = turned[candidates : candidates + 2, :block_rows]
        return carry

    lax.fori_loop(0, particles // ROWS, block, 0)


def slice_kernel(
    scale,
    place_ref,
    stats_ref,
    exps_own_ref,
    exps_other_ref,
    weighted_own_ref,
    weighted_other_ref,
    out_hbm,
    best_ref,
    log_ref,
    posterior_ref,
    summed_ref,
    sems,
):
    blocks, rows, block_rows = exps_own_ref.shape
    chips = stats_ref.shape[0]
    per_device = best_ref.shape[0]
    full = out_hbm.shape[1]
    for side, exps_ref in enumerate((exps_own_ref, exps_other_ref)):
        core = place_ref[1] if side == 0 else 1 - place_ref[1]
        for block in range(blocks):
            tops = [stats_ref[source, core, block, 0:1, :] for source in range(chips)]
            totals = [stats_ref[source, core, block, 1:2, :] for source in range(chips)]
            top = functools.reduce(jnp.maximum, tops)
            total = functools.reduce(
                jnp.add, [part * jnp.exp(high - top) for high, part in zip(tops, totals)]
            )
            log_total = top + jnp.log(total)
            factor = jnp.exp(stats_ref[place_ref[0], core, block, 0:1, :] - log_total)
            posterior_ref[side, block] = (exps_ref[block] * factor).astype(jnp.bfloat16)
            if side == 0:
                best = jnp.exp(top - log_total)
                column = lax.broadcasted_iota(jnp.int32, (1, block_rows), 1)
                for row in range(per_device):
                    particle = place_ref[0] * per_device + row

                    @pl.when(particle // ROWS == block)
                    def _():
                        chosen = column == particle % ROWS
                        best_ref[row] = jnp.sum(jnp.where(chosen, best, 0.0))
                        log_ref[row] = jnp.sum(jnp.where(chosen, log_total, 0.0))

    width = 1024
    copies = []
    for number, start in enumerate(range(0, full, width)):
        at = pl.ds(start, width)
        summed = jnp.zeros((rows, width), jnp.float32)
        for side, weighted_ref in enumerate((weighted_own_ref, weighted_other_ref)):
            for block in range(blocks):
                summed = summed + jnp.dot(
                    posterior_ref[side, block],
                    weighted_ref[pl.ds(block * block_rows, block_rows), at],
                    preferred_element_type=jnp.float32,
                )
        summed_ref[:, at] = summed * scale
        copy = pltpu.make_async_copy(summed_ref.at[:, at], out_hbm.at[:, at], sems.at[number])
        copy.start()
        copies.append(copy)
    for copy in copies:
        copy.wait()


def local(
    axis_size, projections, images, ctf_group, shift_offsets, shell_limit, ctf_table, noise_weight
):
    batch_count, orient_dev, full = projections.shape
    half = full // 2
    own_rows = batch_count * orient_dev
    candidates = 2 * own_rows
    per_device = images.shape[0]
    shifts = shift_offsets.shape[1]
    chips = axis_size // 2
    particles = chips * per_device
    blocks = particles // ROWS
    block_rows = shifts * ROWS
    index = lax.axis_index("blk")
    place = jnp.stack([index >> 1, index & 1])
    megabytes = 12 + -(-2 * blocks * block_rows * full * 2 // 2**20)
    params = pltpu.CompilerParams(vmem_limit_bytes=megabytes * 2**20)

    def swap(value, mask):
        return lax.ppermute(value, "blk", [(i, i ^ mask) for i in range(axis_size)])

    packed = pl.pallas_call(
        pack_kernel,
        out_shape=jax.ShapeDtypeStruct((1, per_device, full + LANES), jnp.bfloat16),
        in_specs=[HBM] * 4,
        out_specs=VMEM,
        scratch_shapes=[
            pltpu.SMEM((per_device,), jnp.int32),
            pltpu.SMEM((per_device,), jnp.int32),
            pltpu.SMEM((per_device, 2, shifts), jnp.int32),
            pltpu.SemaphoreType.DMA((4,)),
        ],
        compiler_params=pltpu.CompilerParams(vmem_limit_bytes=60 * 2**20),
        name="pack",
    )(images, ctf_group, shell_limit, shift_offsets.transpose(0, 2, 1))
    by_distance = chips <= 8
    if by_distance:
        pair = jnp.concatenate([packed, swap(packed, 2)], axis=0) if chips > 1 else packed
        pieces = [pair] + [swap(pair, mask) for mask in range(4, axis_size, 4)]
    else:
        same_core = [[2 * c + core for c in range(chips)] for core in range(2)]
        pieces = [
            lax.all_gather(packed, "blk", axis=0, tiled=True, axis_index_groups=same_core)
        ]

    flat = projections.reshape(own_rows, full)
    other = swap(flat, 1)
    groups = ctf_table.shape[0]
    both, high, low, tables = pl.pallas_call(
        power_kernel,
        out_shape=(
            jax.ShapeDtypeStruct((candidates, full), jnp.bfloat16),
            jax.ShapeDtypeStruct((candidates, half), jnp.bfloat16),
            jax.ShapeDtypeStruct((candidates, half), jnp.bfloat16),
            jax.ShapeDtypeStruct((3 * groups, full), jnp.bfloat16),
        ),
        in_specs=[HBM, VMEM, HBM, HBM],
        out_specs=(VMEM,) * 4,
        scratch_shapes=[
            pltpu.VMEM((groups, half), jnp.float32),
            pltpu.VMEM((groups, half), jnp.float32),
            pltpu.SemaphoreType.DMA((3,)),
        ],
        compiler_params=params,
        cost_estimate=pl.CostEstimate(
            flops=8 * candidates * full, bytes_accessed=4 * candidates * full, transcendentals=0
        ),
        name="power",
    )(flat, other, ctf_table, noise_weight)

    weighted, exps, exps_other, stats = pl.pallas_call(
        functools.partial(score_kernel, len(pieces), shifts, by_distance),
        out_shape=(
            jax.ShapeDtypeStruct((blocks * block_rows, full), jnp.bfloat16),
            jax.ShapeDtypeStruct((blocks, own_rows, block_rows), jnp.float32),
            jax.ShapeDtypeStruct((blocks, own_rows, block_rows), jnp.float32),
            jax.ShapeDtypeStruct((axis_size, blocks, 2, block_rows), jnp.float32),
        ),
        in_specs=[SMEM] + [VMEM] * (len(pieces) + 4),
        out_specs=(VMEM,) * 4,
        scratch_shapes=[
            pltpu.VMEM((particles, full + LANES), jnp.float32),
            pltpu.VMEM((ROWS, half), jnp.float32),
            pltpu.VMEM((ROWS, half), jnp.float32),
            pltpu.VMEM((block_rows, candidates), jnp.float32),
            pltpu.VMEM((-(-block_rows // LANES) * LANES, LANES), jnp.float32),
        ],
        compiler_params=params,
        name="scores",
    )(place, *pieces, both, high, low, tables)

    weighted_other = swap(weighted, 1)
    exps_in = swap(exps_other, 1)
    gathered = lax.all_to_all(stats, "blk", 0, 0)
    gathered = gathered.reshape((chips, 2) + gathered.shape[1:])

    slices, best_posterior, log_total = pl.pallas_call(
        functools.partial(slice_kernel, own_rows / per_device),
        out_shape=(
            jax.ShapeDtypeStruct((own_rows, full), jnp.float32),
            jax.ShapeDtypeStruct((per_device,), jnp.float32),
            jax.ShapeDtypeStruct((per_device,), jnp.float32),
        ),
        in_specs=[SMEM] + [VMEM] * 5,
        out_specs=(HBM, SMEM, SMEM),
        scratch_shapes=[
            pltpu.VMEM((2, blocks, own_rows, block_rows), jnp.bfloat16),
            pltpu.VMEM((own_rows, full), jnp.float32),
            pltpu.SemaphoreType.DMA((full // 1024,)),
        ],
        compiler_params=params,
        name="slices",
    )(place, gathered, exps, exps_in, weighted, weighted_other)
    return (slices.reshape(batch_count, orient_dev, full), best_posterior, log_total)


def solution(mesh):
    in_specs = (
        P(None, ("groups", "blk"), None),
        P(("groups", "blk"), None),
        P(("groups", "blk")),
        P(("groups", "blk"), None, None),
        P(("groups", "blk")),
        P("groups", None),
        P("groups", None),
    )
    out_specs = (P(None, ("groups", "blk"), None), P(("groups", "blk")), P(("groups", "blk")))
    return jax.shard_map(
        functools.partial(local, mesh.shape["blk"]),
        mesh=mesh,
        in_specs=in_specs,
        out_specs=out_specs,
        check_vma=False,
    )
```

```python
import functools
import math

import jax
import jax.numpy as jnp
from jax import lax
from jax.experimental import pallas as pl
from jax.experimental.pallas import tpu as pltpu
from jax.sharding import PartitionSpec as P

KY = 64
IMG = 256
LANES = 128
ROWS = 16
LIMIT_AT = 1
X_AT = 16
Y_AT = 48

VMEM = pl.BlockSpec(memory_space=pltpu.VMEM)
HBM = pl.BlockSpec(memory_space=pltpu.HBM)
NT = (((1,), (1,)), ((), ()))


def sin_cos(turns):
    quarter = IMG // 4
    wrapped = (turns + quarter // 2) & (IMG - 1)
    quadrant = wrapped >> int(math.log2(quarter))
    angle = (wrapped - quadrant * quarter - quarter // 2).astype(jnp.float32) * (
        2.0 * math.pi / IMG
    )
    square = angle * angle
    even = 1.0 + square * (
        -1.0 / 2 + square * (1.0 / 24 + square * (-1.0 / 720 + square * (1.0 / 40320)))
    )
    odd = angle * (
        1.0
        + square
        * (-1.0 / 6 + square * (1.0 / 120 + square * (-1.0 / 5040 + square * (1.0 / 362880))))
    )
    swapped = (quadrant & 1) == 1
    cosine = jnp.where(swapped, odd, even)
    sine = jnp.where(swapped, even, odd)
    cosine = jnp.where((quadrant == 1) | (quadrant == 2), -cosine, cosine)
    sine = jnp.where(quadrant >= 2, -sine, sine)
    return cosine, sine


def split_halves(value):
    high = value.astype(jnp.bfloat16)
    return high, (value - high.astype(jnp.float32)).astype(jnp.bfloat16)


def pack_kernel(images_hbm, group_hbm, limit_hbm, offsets_hbm, packed_ref, group, limit, offsets, sems):
    per_device, full = images_hbm.shape
    shifts = offsets_hbm.shape[2]
    copies = [
        pltpu.make_async_copy(images_hbm, packed_ref.at[0, :, pl.ds(0, full)], sems.at[0]),
        pltpu.make_async_copy(group_hbm, group, sems.at[1]),
        pltpu.make_async_copy(limit_hbm, limit, sems.at[2]),
        pltpu.make_async_copy(offsets_hbm, offsets, sems.at[3]),
    ]
    for copy in copies:
        copy.start()
    for copy in copies[1:]:
        copy.wait()
    row = lax.broadcasted_iota(jnp.int32, (per_device, LANES), 0)
    lane = lax.broadcasted_iota(jnp.int32, (per_device, LANES), 1)
    numbers = jnp.zeros((per_device, LANES), jnp.int32)
    for particle in range(per_device):
        line = jnp.zeros((per_device, LANES), jnp.int32)
        line = jnp.where(lane == 0, group[particle], line)
        line = jnp.where(lane == LIMIT_AT, limit[particle], line)
        for shift in range(shifts):
            line = jnp.where(lane == X_AT + shift, offsets[particle, 0, shift], line)
            line = jnp.where(lane == Y_AT + shift, offsets[particle, 1, shift], line)
        numbers = jnp.where(row == particle, line, numbers)
    packed_ref[0, :, pl.ds(full, LANES)] = numbers.astype(jnp.float32).astype(jnp.bfloat16)
    copies[0].wait()


def split_thirds(value):
    high = value.astype(jnp.bfloat16)
    rest = value - high.astype(jnp.float32)
    middle = rest.astype(jnp.bfloat16)
    return high, middle, (rest - middle.astype(jnp.float32)).astype(jnp.bfloat16)


def power_kernel(
    own_hbm,
    other_ref,
    ctf_hbm,
    noise_hbm,
    both_ref,
    high_ref,
    low_ref,
    table_ref,
    ctf_ref,
    noise_ref,
    sems,
):
    rows, full = other_ref.shape
    half = full // 2
    groups = ctf_ref.shape[0]
    copies = [
        pltpu.make_async_copy(own_hbm, both_ref.at[pl.ds(0, rows)], sems.at[0]),
        pltpu.make_async_copy(ctf_hbm, ctf_ref, sems.at[1]),
        pltpu.make_async_copy(noise_hbm, noise_ref, sems.at[2]),
    ]
    for copy in copies:
        copy.start()
    both_ref[pl.ds(rows, rows), :] = other_ref[...]
    for place in (1, 0):
        at = pl.ds(place * rows, rows)
        if place == 0:
            copies[0].wait()
        real = both_ref[at, :half].astype(jnp.float32)
        imag = both_ref[at, half:].astype(jnp.float32)
        high, low = split_halves(real * real + imag * imag)
        high_ref[at, :] = high
        low_ref[at, :] = low
    for place, ref in enumerate((ctf_ref, noise_ref)):
        copies[1 + place].wait()
        for third, part in enumerate(split_thirds(ref[...])):
            table_ref[pl.ds(third * groups, groups), pl.ds(place * half, half)] = part


def score_kernel(pieces_count, shifts, by_distance, *refs):
    pieces = refs[:pieces_count]
    both_ref, high_ref, low_ref, table_ref = refs[pieces_count : pieces_count + 4]
    weighted_ref, exps_ref, exps_other_ref, stats_ref = refs[pieces_count + 4 : pieces_count + 8]
    image_ref, real_ref, imag_ref, cross_ref, square_ref = refs[pieces_count + 8 :]
    full = both_ref.shape[1]
    half = full // 2
    groups = table_ref.shape[0] // 3
    candidates = both_ref.shape[0]
    particles = image_ref.shape[0]
    per_device = pieces[0].shape[1]
    scale = 0.5 / math.sqrt(half)
    chip = lax.axis_index("blk") >> 1
    place = 0
    for piece in pieces:
        for row in range(piece.shape[0]):
            source = chip ^ place if by_distance else place
            start = source * per_device
            values = piece[row].astype(jnp.float32)
            for sub in range(per_device):
                image_ref[pl.ds(start + sub, 1), :] = values[sub : sub + 1]
            place += 1

    lane = lax.broadcasted_iota(jnp.int32, (ROWS, LANES), 1)
    block_rows = shifts * ROWS

    def block(index, carry):
        rows = pl.ds(pl.multiple_of(index * ROWS, ROWS), ROWS)
        first = pl.multiple_of(index * block_rows, ROWS)
        numbers = image_ref[rows, full:]
        column = lax.broadcasted_iota(jnp.int32, (ROWS, 3 * groups), 1) % groups
        one_hot = (numbers[:, :1].astype(jnp.int32) == column).astype(jnp.bfloat16)
        tables = jnp.dot(one_hot, table_ref[...], preferred_element_type=jnp.float32)
        ctf = tables[:, :half]
        noise = tables[:, half:]
        limit = numbers[:, LIMIT_AT : LIMIT_AT + 1].astype(jnp.int32)
        position = lax.broadcasted_iota(jnp.int32, (1, half), 1)
        freq_x = position // KY
        freq_y = position % KY - KY // 2
        weight = jnp.where(freq_x * freq_x + freq_y * freq_y < limit * limit, noise, 0.0)
        ctf_weight = weight * ctf
        real = image_ref[rows, :half]
        imag = image_ref[rows, half:full]
        norm = jnp.sum(weight * (real * real + imag * imag), axis=1, keepdims=True)
        real_ref[...] = ctf_weight * real
        imag_ref[...] = ctf_weight * imag
        quad_high, quad_low = split_halves(ctf_weight * ctf)
        quad_weight = jnp.concatenate([quad_high, quad_low], axis=0)
        quad = lax.dot_general(
            quad_weight, high_ref[...], NT, preferred_element_type=jnp.float32
        ) + lax.dot_general(quad_weight, low_ref[...], NT, preferred_element_type=jnp.float32)
        quad = quad[:ROWS] + quad[ROWS:]

        numbers_int = numbers.astype(jnp.int32)
        step_cos, step_sin = sin_cos(numbers_int * (LANES // KY))
        for shift in range(shifts):
            turns = (
                (lane // KY) * numbers_int[:, X_AT + shift : X_AT + shift + 1]
                + (lane % KY - KY // 2) * numbers_int[:, Y_AT + shift : Y_AT + shift + 1]
            )
            cosine, sine = sin_cos(turns)
            turn_cos = step_cos[:, X_AT + shift : X_AT + shift + 1]
            turn_sin = step_sin[:, X_AT + shift : X_AT + shift + 1]
            cosine_before = cosine * turn_cos + sine * turn_sin
            sine_before = sine * turn_cos - cosine * turn_sin
            double = jnp.broadcast_to(2.0 * turn_cos, (ROWS, LANES))
            out_rows = pl.ds(first + shift * ROWS, ROWS)
            for chunk in range(half // LANES):
                at = pl.ds(chunk * LANES, LANES)
                real = real_ref[:, at]
                imag = imag_ref[:, at]
                weighted_ref[out_rows, at] = (real * cosine + imag * sine).astype(jnp.bfloat16)
                weighted_ref[out_rows, pl.ds(half + chunk * LANES, LANES)] = (
                    imag * cosine - real * sine
                ).astype(jnp.bfloat16)
                cosine, cosine_before = double * cosine - cosine_before, cosine
                sine, sine_before = double * sine - sine_before, sine

        cross_ref[...] = lax.dot_general(
            weighted_ref[pl.ds(first, block_rows), :],
            both_ref[...],
            NT,
            preferred_element_type=jnp.float32,
        )
        base = norm + quad
        scores = [
            -(base - 2.0 * cross_ref[pl.ds(shift * ROWS, ROWS), :]) * scale
            for shift in range(shifts)
        ]
        top = jnp.max(functools.reduce(jnp.maximum, scores), axis=1, keepdims=True)
        exps = [jnp.exp(score - top) for score in scores]
        total = jnp.sum(functools.reduce(jnp.add, exps), axis=1, keepdims=True)
        for shift in range(shifts):
            square_ref[pl.ds(shift * ROWS, ROWS), :candidates] = exps[shift]
        turned = square_ref[...].T
        exps_ref[index] = turned[: candidates // 2, :block_rows]
        exps_other_ref[index] = turned[candidates // 2 : candidates, :block_rows]
        row = lax.broadcasted_iota(jnp.int32, (ROWS, LANES), 0)
        both_stats = jnp.where(lane == row, top, jnp.where(lane == row + ROWS, total, 0.0))
        line = jnp.sum(both_stats, axis=0, keepdims=True)
        for target in range(stats_ref.shape[0]):
            stats_ref[target, pl.ds(index, 1), :] = line
        return carry

    lax.fori_loop(0, particles // ROWS, block, 0)


def slice_kernel(
    scale,
    stats_ref,
    exps_own_ref,
    exps_other_ref,
    weighted_own_ref,
    weighted_other_ref,
    out_hbm,
    best_hbm,
    log_hbm,
    best_ref,
    log_ref,
    posterior_ref,
    summed_ref,
    sems,
    number_sems,
):
    blocks, rows, block_rows = exps_own_ref.shape
    chips = stats_ref.shape[0]
    per_device = best_ref.shape[0]
    full = out_hbm.shape[1]
    index = lax.axis_index("blk")
    chip = index >> 1
    lane = lax.broadcasted_iota(jnp.int32, (1, LANES), 1)
    for side, exps_ref in enumerate((exps_own_ref, exps_other_ref)):
        core = (index & 1) ^ side
        for block in range(blocks):
            at = pl.ds(block, 1)
            lines = [stats_ref[source, core, at, :] for source in range(chips)]
            top = functools.reduce(jnp.maximum, lines)
            total = functools.reduce(
                jnp.add,
                [pltpu.roll(line, LANES - ROWS, 1) * jnp.exp(line - top) for line in lines],
            )
            log_total = top + jnp.log(total)
            factor = jnp.exp(stats_ref[chip, core, at, :] - log_total)
            factor = jnp.where(lane < ROWS, factor, 0.0)
            filled = ROWS
            while filled < LANES:
                factor = factor + pltpu.roll(factor, filled, 1)
                filled *= 2
            factor = jnp.concatenate([factor] * -(-block_rows // LANES), axis=1)[:, :block_rows]
            posterior_ref[side, block] = (exps_ref[block] * factor).astype(jnp.bfloat16)
            if side == 0:
                best = jnp.exp(top - log_total)
                for row in range(per_device):
                    particle = chip * per_device + row

                    @pl.when(particle // ROWS == block)
                    def _():
                        chosen = lane == particle % ROWS
                        best_ref[row] = jnp.sum(jnp.where(chosen, best, 0.0))
                        log_ref[row] = jnp.sum(jnp.where(chosen, log_total, 0.0))

    width = 1024
    copies = [
        pltpu.make_async_copy(best_ref, best_hbm, number_sems.at[0]),
        pltpu.make_async_copy(log_ref, log_hbm, number_sems.at[1]),
    ]
    for copy in copies:
        copy.start()
    for number, start in enumerate(range(0, full, width)):
        at = pl.ds(start, width)
        summed = jnp.zeros((rows, width), jnp.float32)
        for side, weighted_ref in enumerate((weighted_own_ref, weighted_other_ref)):
            for block in range(blocks):
                summed = summed + jnp.dot(
                    posterior_ref[side, block],
                    weighted_ref[pl.ds(block * block_rows, block_rows), at],
                    preferred_element_type=jnp.float32,
                )
        summed_ref[:, at] = summed * scale
        copy = pltpu.make_async_copy(summed_ref.at[:, at], out_hbm.at[:, at], sems.at[number])
        copy.start()
        copies.append(copy)
    for copy in copies:
        copy.wait()


def local(
    axis_size, projections, images, ctf_group, shift_offsets, shell_limit, ctf_table, noise_weight
):
    batch_count, orient_dev, full = projections.shape
    half = full // 2
    own_rows = batch_count * orient_dev
    candidates = 2 * own_rows
    per_device = images.shape[0]
    shifts = shift_offsets.shape[1]
    chips = axis_size // 2
    particles = chips * per_device
    blocks = particles // ROWS
    block_rows = shifts * ROWS
    megabytes = 12 + -(-2 * blocks * block_rows * full * 2 // 2**20)
    params = pltpu.CompilerParams(vmem_limit_bytes=megabytes * 2**20)

    def swap(value, mask):
        return lax.ppermute(value, "blk", [(i, i ^ mask) for i in range(axis_size)])

    packed = pl.pallas_call(
        pack_kernel,
        out_shape=jax.ShapeDtypeStruct((1, per_device, full + LANES), jnp.bfloat16),
        in_specs=[HBM] * 4,
        out_specs=VMEM,
        scratch_shapes=[
            pltpu.SMEM((per_device,), jnp.int32),
            pltpu.SMEM((per_device,), jnp.int32),
            pltpu.SMEM((per_device, 2, shifts), jnp.int32),
            pltpu.SemaphoreType.DMA((4,)),
        ],
        compiler_params=pltpu.CompilerParams(vmem_limit_bytes=60 * 2**20),
        name="pack",
    )(images, ctf_group, shell_limit, shift_offsets.transpose(0, 2, 1))
    by_distance = chips <= 8
    if by_distance:
        pair = jnp.concatenate([packed, swap(packed, 2)], axis=0) if chips > 1 else packed
        pieces = [pair] + [swap(pair, mask) for mask in range(4, axis_size, 4)]
    else:
        same_core = [[2 * c + core for c in range(chips)] for core in range(2)]
        pieces = [
            lax.all_gather(packed, "blk", axis=0, tiled=True, axis_index_groups=same_core)
        ]

    flat = projections.reshape(own_rows, full)
    other = swap(flat, 1)
    groups = ctf_table.shape[0]
    both, high, low, tables = pl.pallas_call(
        power_kernel,
        out_shape=(
            jax.ShapeDtypeStruct((candidates, full), jnp.bfloat16),
            jax.ShapeDtypeStruct((candidates, half), jnp.bfloat16),
            jax.ShapeDtypeStruct((candidates, half), jnp.bfloat16),
            jax.ShapeDtypeStruct((3 * groups, full), jnp.bfloat16),
        ),
        in_specs=[HBM, VMEM, HBM, HBM],
        out_specs=(VMEM,) * 4,
        scratch_shapes=[
            pltpu.VMEM((groups, half), jnp.float32),
            pltpu.VMEM((groups, half), jnp.float32),
            pltpu.SemaphoreType.DMA((3,)),
        ],
        compiler_params=params,
        cost_estimate=pl.CostEstimate(
            flops=8 * candidates * full, bytes_accessed=4 * candidates * full, transcendentals=0
        ),
        name="power",
    )(flat, other, ctf_table, noise_weight)

    weighted, exps, exps_other, stats = pl.pallas_call(
        functools.partial(score_kernel, len(pieces), shifts, by_distance),
        out_shape=(
            jax.ShapeDtypeStruct((blocks * block_rows, full), jnp.bfloat16),
            jax.ShapeDtypeStruct((blocks, own_rows, block_rows), jnp.float32),
            jax.ShapeDtypeStruct((blocks, own_rows, block_rows), jnp.float32),
            jax.ShapeDtypeStruct((axis_size, blocks, LANES), jnp.float32),
        ),
        in_specs=[VMEM] * (len(pieces) + 4),
        out_specs=(VMEM,) * 4,
        scratch_shapes=[
            pltpu.VMEM((particles, full + LANES), jnp.float32),
            pltpu.VMEM((ROWS, half), jnp.float32),
            pltpu.VMEM((ROWS, half), jnp.float32),
            pltpu.VMEM((block_rows, candidates), jnp.float32),
            pltpu.VMEM((-(-block_rows // LANES) * LANES, LANES), jnp.float32),
        ],
        compiler_params=params,
        name="scores",
    )(*pieces, both, high, low, tables)

    weighted_other = swap(weighted, 1)
    exps_in = swap(exps_other, 1)
    gathered = lax.all_to_all(stats, "blk", 0, 0)
    gathered = gathered.reshape((chips, 2) + gathered.shape[1:])

    slices, best_posterior, log_total = pl.pallas_call(
        functools.partial(slice_kernel, own_rows / per_device),
        out_shape=(
            jax.ShapeDtypeStruct((own_rows, full), jnp.float32),
            jax.ShapeDtypeStruct((per_device,), jnp.float32),
            jax.ShapeDtypeStruct((per_device,), jnp.float32),
        ),
        in_specs=[VMEM] * 5,
        out_specs=(HBM, HBM, HBM),
        scratch_shapes=[
            pltpu.SMEM((per_device,), jnp.float32),
            pltpu.SMEM((per_device,), jnp.float32),
            pltpu.VMEM((2, blocks, own_rows, block_rows), jnp.bfloat16),
            pltpu.VMEM((own_rows, full), jnp.float32),
            pltpu.SemaphoreType.DMA((full // 1024,)),
            pltpu.SemaphoreType.DMA((2,)),
        ],
        compiler_params=params,
        name="slices",
    )(gathered, exps, exps_in, weighted, weighted_other)
    return (slices.reshape(batch_count, orient_dev, full), best_posterior, log_total)


def solution(mesh):
    in_specs = (
        P(None, ("groups", "blk"), None),
        P(("groups", "blk"), None),
        P(("groups", "blk")),
        P(("groups", "blk"), None, None),
        P(("groups", "blk")),
        P("groups", None),
        P("groups", None),
    )
    out_specs = (P(None, ("groups", "blk"), None), P(("groups", "blk")), P(("groups", "blk")))
    return jax.shard_map(
        functools.partial(local, mesh.shape["blk"]),
        mesh=mesh,
        in_specs=in_specs,
        out_specs=out_specs,
        check_vma=False,
    )
```

```python
import functools
import math

import jax
import jax.numpy as jnp
from jax import lax
from jax.experimental import pallas as pl
from jax.experimental.pallas import tpu as pltpu
from jax.sharding import PartitionSpec as P

KY = 64
IMG = 256
LANES = 128
ROWS = 16
LIMIT_AT = 1
X_AT = 16
Y_AT = 48

VMEM = pl.BlockSpec(memory_space=pltpu.VMEM)
HBM = pl.BlockSpec(memory_space=pltpu.HBM)
NT = (((1,), (1,)), ((), ()))


def sin_cos(turns):
    quarter = IMG // 4
    wrapped = (turns + quarter // 2) & (IMG - 1)
    quadrant = wrapped >> int(math.log2(quarter))
    angle = (wrapped - quadrant * quarter - quarter // 2).astype(jnp.float32) * (
        2.0 * math.pi / IMG
    )
    square = angle * angle
    even = 1.0 + square * (
        -1.0 / 2 + square * (1.0 / 24 + square * (-1.0 / 720 + square * (1.0 / 40320)))
    )
    odd = angle * (
        1.0
        + square
        * (-1.0 / 6 + square * (1.0 / 120 + square * (-1.0 / 5040 + square * (1.0 / 362880))))
    )
    swapped = (quadrant & 1) == 1
    cosine = jnp.where(swapped, odd, even)
    sine = jnp.where(swapped, even, odd)
    cosine = jnp.where((quadrant == 1) | (quadrant == 2), -cosine, cosine)
    sine = jnp.where(quadrant >= 2, -sine, sine)
    return cosine, sine


def split_halves(value):
    high = value.astype(jnp.bfloat16)
    return high, (value - high.astype(jnp.float32)).astype(jnp.bfloat16)


def pack_kernel(
    images_hbm,
    group_hbm,
    limit_hbm,
    offsets_hbm,
    packed_hbm,
    numbers_ref,
    group,
    limit,
    offsets,
    sems,
):
    per_device, full = images_hbm.shape
    shifts = offsets_hbm.shape[2]
    copies = [
        pltpu.make_async_copy(group_hbm, group, sems.at[0]),
        pltpu.make_async_copy(limit_hbm, limit, sems.at[1]),
        pltpu.make_async_copy(offsets_hbm, offsets, sems.at[2]),
        pltpu.make_async_copy(images_hbm, packed_hbm.at[0, :, pl.ds(0, full)], sems.at[3]),
        pltpu.make_async_copy(numbers_ref, packed_hbm.at[0, :, pl.ds(full, LANES)], sems.at[4]),
    ]
    for copy in copies[:4]:
        copy.start()
    for copy in copies[:3]:
        copy.wait()
    row = lax.broadcasted_iota(jnp.int32, (per_device, LANES), 0)
    lane = lax.broadcasted_iota(jnp.int32, (per_device, LANES), 1)
    numbers = jnp.zeros((per_device, LANES), jnp.int32)
    for particle in range(per_device):
        line = jnp.zeros((per_device, LANES), jnp.int32)
        line = jnp.where(lane == 0, group[particle], line)
        line = jnp.where(lane == LIMIT_AT, limit[particle], line)
        for shift in range(shifts):
            line = jnp.where(lane == X_AT + shift, offsets[particle, 0, shift], line)
            line = jnp.where(lane == Y_AT + shift, offsets[particle, 1, shift], line)
        numbers = jnp.where(row == particle, line, numbers)
    numbers_ref[...] = numbers.astype(jnp.float32).astype(jnp.bfloat16)
    copies[4].start()
    copies[3].wait()
    copies[4].wait()


def split_thirds(value):
    high = value.astype(jnp.bfloat16)
    rest = value - high.astype(jnp.float32)
    middle = rest.astype(jnp.bfloat16)
    return high, middle, (rest - middle.astype(jnp.float32)).astype(jnp.bfloat16)


def power_kernel(own_ref, other_ref, both_ref, high_ref, low_ref):
    rows, full = own_ref.shape
    half = full // 2
    for place, ref in enumerate((own_ref, other_ref)):
        at = pl.ds(place * rows, rows)
        both_ref[at, :] = ref[...]
        real = ref[:, :half].astype(jnp.float32)
        imag = ref[:, half:].astype(jnp.float32)
        high, low = split_halves(real * real + imag * imag)
        high_ref[at, :] = high
        low_ref[at, :] = low


def table_kernel(ctf_ref, noise_ref, table_ref):
    groups, half = ctf_ref.shape
    for place, ref in enumerate((ctf_ref, noise_ref)):
        for third, part in enumerate(split_thirds(ref[...])):
            table_ref[pl.ds(third * groups, groups), pl.ds(place * half, half)] = part


def score_kernel(pieces_count, shifts, by_distance, *refs):
    pieces = refs[:pieces_count]
    both_ref, high_ref, low_ref, table_ref = refs[pieces_count : pieces_count + 4]
    weighted_ref, exps_ref, exps_other_ref, stats_ref = refs[pieces_count + 4 : pieces_count + 8]
    image_ref, real_ref, imag_ref, cross_ref, square_ref = refs[pieces_count + 8 :]
    full = both_ref.shape[1]
    half = full // 2
    groups = table_ref.shape[0] // 3
    candidates = both_ref.shape[0]
    particles = image_ref.shape[0]
    per_device = pieces[0].shape[1]
    scale = 0.5 / math.sqrt(half)
    chip = lax.axis_index("blk") >> 1
    place = 0
    for piece in pieces:
        for row in range(piece.shape[0]):
            source = chip ^ place if by_distance else place
            start = source * per_device
            values = piece[row].astype(jnp.float32)
            for sub in range(per_device):
                image_ref[pl.ds(start + sub, 1), :] = values[sub : sub + 1]
            place += 1

    lane = lax.broadcasted_iota(jnp.int32, (ROWS, LANES), 1)
    block_rows = shifts * ROWS

    def block(index, carry):
        rows = pl.ds(pl.multiple_of(index * ROWS, ROWS), ROWS)
        first = pl.multiple_of(index * block_rows, ROWS)
        numbers = image_ref[rows, full:]
        column = lax.broadcasted_iota(jnp.int32, (ROWS, 3 * groups), 1) % groups
        one_hot = (numbers[:, :1].astype(jnp.int32) == column).astype(jnp.bfloat16)
        tables = jnp.dot(one_hot, table_ref[...], preferred_element_type=jnp.float32)
        ctf = tables[:, :half]
        noise = tables[:, half:]
        limit = numbers[:, LIMIT_AT : LIMIT_AT + 1].astype(jnp.int32)
        position = lax.broadcasted_iota(jnp.int32, (1, half), 1)
        freq_x = position // KY
        freq_y = position % KY - KY // 2
        weight = jnp.where(freq_x * freq_x + freq_y * freq_y < limit * limit, noise, 0.0)
        ctf_weight = weight * ctf
        real = image_ref[rows, :half]
        imag = image_ref[rows, half:full]
        norm = jnp.sum(weight * (real * real + imag * imag), axis=1, keepdims=True)
        real_ref[...] = ctf_weight * real
        imag_ref[...] = ctf_weight * imag
        quad_high, quad_low = split_halves(ctf_weight * ctf)
        quad_weight = jnp.concatenate([quad_high, quad_low], axis=0)
        quad = lax.dot_general(
            quad_weight, high_ref[...], NT, preferred_element_type=jnp.float32
        ) + lax.dot_general(quad_weight, low_ref[...], NT, preferred_element_type=jnp.float32)
        quad = quad[:ROWS] + quad[ROWS:]

        numbers_int = numbers.astype(jnp.int32)
        step_cos, step_sin = sin_cos(numbers_int * (LANES // KY))
        for shift in range(shifts):
            turns = (
                (lane // KY) * numbers_int[:, X_AT + shift : X_AT + shift + 1]
                + (lane % KY - KY // 2) * numbers_int[:, Y_AT + shift : Y_AT + shift + 1]
            )
            cosine, sine = sin_cos(turns)
            turn_cos = step_cos[:, X_AT + shift : X_AT + shift + 1]
            turn_sin = step_sin[:, X_AT + shift : X_AT + shift + 1]
            cosine_before = cosine * turn_cos + sine * turn_sin
            sine_before = sine * turn_cos - cosine * turn_sin
            double = jnp.broadcast_to(2.0 * turn_cos, (ROWS, LANES))
            out_rows = pl.ds(first + shift * ROWS, ROWS)
            for chunk in range(half // LANES):
                at = pl.ds(chunk * LANES, LANES)
                real = real_ref[:, at]
                imag = imag_ref[:, at]
                weighted_ref[out_rows, at] = (real * cosine + imag * sine).astype(jnp.bfloat16)
                weighted_ref[out_rows, pl.ds(half + chunk * LANES, LANES)] = (
                    imag * cosine - real * sine
                ).astype(jnp.bfloat16)
                cosine, cosine_before = double * cosine - cosine_before, cosine
                sine, sine_before = double * sine - sine_before, sine

        cross_ref[...] = lax.dot_general(
            weighted_ref[pl.ds(first, block_rows), :],
            both_ref[...],
            NT,
            preferred_element_type=jnp.float32,
        )
        base = norm + quad
        scores = [
            -(base - 2.0 * cross_ref[pl.ds(shift * ROWS, ROWS), :]) * scale
            for shift in range(shifts)
        ]
        top = jnp.max(functools.reduce(jnp.maximum, scores), axis=1, keepdims=True)
        exps = [jnp.exp(score - top) for score in scores]
        total = jnp.sum(functools.reduce(jnp.add, exps), axis=1, keepdims=True)
        for shift in range(shifts):
            square_ref[pl.ds(shift * ROWS, ROWS), :candidates] = exps[shift]
        turned = square_ref[...].T
        exps_ref[index] = turned[: candidates // 2, :block_rows]
        exps_other_ref[index] = turned[candidates // 2 : candidates, :block_rows]
        row = lax.broadcasted_iota(jnp.int32, (ROWS, LANES), 0)
        both_stats = jnp.where(lane == row, top, jnp.where(lane == row + ROWS, total, 0.0))
        line = jnp.sum(both_stats, axis=0, keepdims=True)
        for target in range(stats_ref.shape[0]):
            stats_ref[target, pl.ds(index, 1), :] = line
        return carry

    lax.fori_loop(0, particles // ROWS, block, 0)


def multiply_slices(scale, posterior_ref, weighted_ref, out_ref):
    blocks, rows, block_rows = posterior_ref.shape
    width = 1024
    for start in range(0, weighted_ref.shape[1], width):
        at = pl.ds(start, width)
        summed = functools.reduce(
            jnp.add,
            [
                jnp.dot(
                    posterior_ref[block],
                    weighted_ref[pl.ds(block * block_rows, block_rows), at],
                    preferred_element_type=jnp.float32,
                )
                for block in range(blocks)
            ],
        )
        out_ref[:, at] = (summed * scale).astype(out_ref.dtype)


def send_kernel(
    scale,
    stats_ref,
    exps_own_ref,
    exps_other_ref,
    weighted_ref,
    send_ref,
    posterior_ref,
    best_hbm,
    log_hbm,
    posterior_other_ref,
    best_ref,
    log_ref,
    sems,
):
    blocks, rows, block_rows = exps_own_ref.shape
    chips = stats_ref.shape[0]
    per_device = best_ref.shape[0]
    chip = lax.axis_index("blk") >> 1
    lane = lax.broadcasted_iota(jnp.int32, (1, LANES), 1)
    for block in range(blocks):
        at = pl.ds(block, 1)
        lines = [stats_ref[source, at, :] for source in range(chips)]
        top = functools.reduce(jnp.maximum, lines)
        total = functools.reduce(
            jnp.add,
            [pltpu.roll(line, LANES - ROWS, 1) * jnp.exp(line - top) for line in lines],
        )
        log_total = top + jnp.log(total)
        factor = jnp.exp(stats_ref[chip, at, :] - log_total)
        factor = jnp.where(lane < ROWS, factor, 0.0)
        filled = ROWS
        while filled < LANES:
            factor = factor + pltpu.roll(factor, filled, 1)
            filled *= 2
        factor = jnp.concatenate([factor] * -(-block_rows // LANES), axis=1)[:, :block_rows]
        posterior_other_ref[block] = (exps_other_ref[block] * factor).astype(jnp.bfloat16)
        posterior_ref[block] = (exps_own_ref[block] * factor).astype(jnp.bfloat16)
        best = jnp.exp(top - log_total)
        for row in range(per_device):
            particle = chip * per_device + row

            @pl.when(particle // ROWS == block)
            def _():
                chosen = lane == particle % ROWS
                best_ref[row] = jnp.sum(jnp.where(chosen, best, 0.0))
                log_ref[row] = jnp.sum(jnp.where(chosen, log_total, 0.0))

    copies = [
        pltpu.make_async_copy(best_ref, best_hbm, sems.at[0]),
        pltpu.make_async_copy(log_ref, log_hbm, sems.at[1]),
    ]
    for copy in copies:
        copy.start()
    multiply_slices(scale, posterior_other_ref, weighted_ref, send_ref)
    for copy in copies:
        copy.wait()


def add_kernel(keep_ref, received_ref, out_hbm, summed_ref, sems):
    width = summed_ref.shape[1] // sems.shape[0]
    copies = []
    for number in range(sems.shape[0]):
        at = pl.ds(number * width, width)
        summed_ref[:, at] = keep_ref[:, at] + received_ref[:, at].astype(jnp.float32)
        copy = pltpu.make_async_copy(summed_ref.at[:, at], out_hbm.at[:, at], sems.at[number])
        copy.start()
        copies.append(copy)
    for copy in copies:
        copy.wait()


def local(
    axis_size, projections, images, ctf_group, shift_offsets, shell_limit, ctf_table, noise_weight
):
    batch_count, orient_dev, full = projections.shape
    half = full // 2
    own_rows = batch_count * orient_dev
    candidates = 2 * own_rows
    per_device = images.shape[0]
    shifts = shift_offsets.shape[1]
    chips = axis_size // 2
    particles = chips * per_device
    blocks = particles // ROWS
    block_rows = shifts * ROWS
    megabytes = 12 + -(-2 * blocks * block_rows * full * 2 // 2**20)
    params = pltpu.CompilerParams(vmem_limit_bytes=megabytes * 2**20)

    def swap(value, mask):
        return lax.ppermute(value, "blk", [(i, i ^ mask) for i in range(axis_size)])

    packed = pl.pallas_call(
        pack_kernel,
        out_shape=jax.ShapeDtypeStruct((1, per_device, full + LANES), jnp.bfloat16),
        in_specs=[HBM] * 4,
        out_specs=HBM,
        scratch_shapes=[
            pltpu.VMEM((per_device, LANES), jnp.bfloat16),
            pltpu.SMEM((per_device,), jnp.int32),
            pltpu.SMEM((per_device,), jnp.int32),
            pltpu.SMEM((per_device, 2, shifts), jnp.int32),
            pltpu.SemaphoreType.DMA((5,)),
        ],
        compiler_params=pltpu.CompilerParams(vmem_limit_bytes=60 * 2**20),
        name="pack",
    )(images, ctf_group, shell_limit, shift_offsets.transpose(0, 2, 1))
    received = swap(packed, 2) if 1 < chips <= 8 else packed
    flat = projections.reshape(own_rows, full)
    other = swap(flat, 1)
    groups = ctf_table.shape[0]
    both, high, low = pl.pallas_call(
        power_kernel,
        out_shape=(
            jax.ShapeDtypeStruct((candidates, full), jnp.bfloat16),
            jax.ShapeDtypeStruct((candidates, half), jnp.bfloat16),
            jax.ShapeDtypeStruct((candidates, half), jnp.bfloat16),
        ),
        in_specs=[VMEM] * 2,
        out_specs=(VMEM,) * 3,
        compiler_params=params,
        cost_estimate=pl.CostEstimate(
            flops=8 * candidates * full, bytes_accessed=4 * candidates * full, transcendentals=0
        ),
        name="power",
    )(flat, other)
    tables = pl.pallas_call(
        table_kernel,
        out_shape=jax.ShapeDtypeStruct((3 * groups, full), jnp.bfloat16),
        in_specs=[VMEM] * 2,
        out_specs=VMEM,
        compiler_params=params,
        cost_estimate=pl.CostEstimate(
            flops=6 * groups * full, bytes_accessed=10 * groups * full, transcendentals=0
        ),
        name="tables",
    )(ctf_table, noise_weight)
    by_distance = 1 < chips <= 8
    same_core = [[2 * c + core for c in range(chips)] for core in range(2)]
    if by_distance:
        pair = jnp.zeros((2,) + packed.shape[1:], packed.dtype)
        pair = lax.dynamic_update_slice(pair, packed, (0, 0, 0))
        pair, received, both, high, low = lax.optimization_barrier(
            (pair, received, both, high, low)
        )
        pair = lax.dynamic_update_slice(pair, received, (1, 0, 0))
        pieces = [pair] + [swap(pair, mask) for mask in range(4, axis_size, 4)]
    else:
        pieces = [
            lax.all_gather(packed, "blk", axis=0, tiled=True, axis_index_groups=same_core)
        ]

    weighted, exps, exps_other, stats = pl.pallas_call(
        functools.partial(score_kernel, len(pieces), shifts, by_distance),
        out_shape=(
            jax.ShapeDtypeStruct((blocks * block_rows, full), jnp.bfloat16),
            jax.ShapeDtypeStruct((blocks, own_rows, block_rows), jnp.float32),
            jax.ShapeDtypeStruct((blocks, own_rows, block_rows), jnp.float32),
            jax.ShapeDtypeStruct((chips, blocks, LANES), jnp.float32),
        ),
        in_specs=[VMEM] * (len(pieces) + 4),
        out_specs=(VMEM,) * 4,
        scratch_shapes=[
            pltpu.VMEM((particles, full + LANES), jnp.float32),
            pltpu.VMEM((ROWS, half), jnp.float32),
            pltpu.VMEM((ROWS, half), jnp.float32),
            pltpu.VMEM((block_rows, candidates), jnp.float32),
            pltpu.VMEM((-(-block_rows // LANES) * LANES, LANES), jnp.float32),
        ],
        compiler_params=params,
        name="scores",
    )(*pieces, both, high, low, tables)

    gathered = lax.all_to_all(stats, "blk", 0, 0, axis_index_groups=same_core)

    scale = own_rows / per_device
    send, posterior, best_posterior, log_total = pl.pallas_call(
        functools.partial(send_kernel, scale),
        out_shape=(
            jax.ShapeDtypeStruct((own_rows, full), jnp.bfloat16),
            jax.ShapeDtypeStruct((blocks, own_rows, block_rows), jnp.bfloat16),
            jax.ShapeDtypeStruct((per_device,), jnp.float32),
            jax.ShapeDtypeStruct((per_device,), jnp.float32),
        ),
        in_specs=[VMEM] * 4,
        out_specs=(VMEM, VMEM, HBM, HBM),
        scratch_shapes=[
            pltpu.VMEM((blocks, own_rows, block_rows), jnp.bfloat16),
            pltpu.SMEM((per_device,), jnp.float32),
            pltpu.SMEM((per_device,), jnp.float32),
            pltpu.SemaphoreType.DMA((2,)),
        ],
        compiler_params=params,
        name="send",
    )(gathered, exps, exps_other, weighted)
    received = swap(send, 1)
    keep = pl.pallas_call(
        functools.partial(multiply_slices, scale),
        out_shape=jax.ShapeDtypeStruct((own_rows, full), jnp.float32),
        in_specs=[VMEM] * 2,
        out_specs=VMEM,
        compiler_params=params,
        cost_estimate=pl.CostEstimate(
            flops=2 * own_rows * full * blocks * block_rows,
            bytes_accessed=4 * own_rows * full,
            transcendentals=0,
        ),
        name="keep",
    )(posterior, weighted)
    slices = pl.pallas_call(
        add_kernel,
        out_shape=jax.ShapeDtypeStruct((own_rows, full), jnp.float32),
        in_specs=[VMEM] * 2,
        out_specs=HBM,
        scratch_shapes=[
            pltpu.VMEM((own_rows, full), jnp.float32),
            pltpu.SemaphoreType.DMA((8,)),
        ],
        compiler_params=params,
        name="add",
    )(keep, received)
    return (slices.reshape(batch_count, orient_dev, full), best_posterior, log_total)


def solution(mesh):
    in_specs = (
        P(None, ("groups", "blk"), None),
        P(("groups", "blk"), None),
        P(("groups", "blk")),
        P(("groups", "blk"), None, None),
        P(("groups", "blk")),
        P("groups", None),
        P("groups", None),
    )
    out_specs = (P(None, ("groups", "blk"), None), P(("groups", "blk")), P(("groups", "blk")))
    return jax.shard_map(
        functools.partial(local, mesh.shape["blk"]),
        mesh=mesh,
        in_specs=in_specs,
        out_specs=out_specs,
        check_vma=False,
    )
```

```python
import functools
import math

import jax
import jax.numpy as jnp
from jax import lax
from jax.experimental import pallas as pl
from jax.experimental.pallas import tpu as pltpu
from jax.sharding import PartitionSpec as P

KY = 64
IMG = 256
LANES = 128
ROWS = 8
NEAR = 4
LIMIT_AT = 1
X_AT = 16
Y_AT = 48

VMEM = pl.BlockSpec(memory_space=pltpu.VMEM)
HBM = pl.BlockSpec(memory_space=pltpu.HBM)
NT = (((1,), (1,)), ((), ()))


def sin_cos(turns):
    quarter = IMG // 4
    wrapped = (turns + quarter // 2) & (IMG - 1)
    quadrant = wrapped >> int(math.log2(quarter))
    angle = (wrapped - quadrant * quarter - quarter // 2).astype(jnp.float32) * (
        2.0 * math.pi / IMG
    )
    square = angle * angle
    even = 1.0 + square * (
        -1.0 / 2 + square * (1.0 / 24 + square * (-1.0 / 720 + square * (1.0 / 40320)))
    )
    odd = angle * (
        1.0
        + square
        * (-1.0 / 6 + square * (1.0 / 120 + square * (-1.0 / 5040 + square * (1.0 / 362880))))
    )
    swapped = (quadrant & 1) == 1
    cosine = jnp.where(swapped, odd, even)
    sine = jnp.where(swapped, even, odd)
    cosine = jnp.where((quadrant == 1) | (quadrant == 2), -cosine, cosine)
    sine = jnp.where(quadrant >= 2, -sine, sine)
    return cosine, sine


def split_halves(value):
    high = value.astype(jnp.bfloat16)
    return high, (value - high.astype(jnp.float32)).astype(jnp.bfloat16)


def pack_kernel(images_hbm, group_hbm, limit_hbm, offsets_hbm, packed_ref, group, limit, offsets, sems):
    per_device, full = images_hbm.shape
    shifts = offsets_hbm.shape[2]
    copies = [
        pltpu.make_async_copy(images_hbm, packed_ref.at[0, :, pl.ds(0, full)], sems.at[0]),
        pltpu.make_async_copy(group_hbm, group, sems.at[1]),
        pltpu.make_async_copy(limit_hbm, limit, sems.at[2]),
        pltpu.make_async_copy(offsets_hbm, offsets, sems.at[3]),
    ]
    for copy in copies:
        copy.start()
    for copy in copies[1:]:
        copy.wait()
    row = lax.broadcasted_iota(jnp.int32, (per_device, LANES), 0)
    lane = lax.broadcasted_iota(jnp.int32, (per_device, LANES), 1)
    numbers = jnp.zeros((per_device, LANES), jnp.int32)
    for particle in range(per_device):
        line = jnp.zeros((per_device, LANES), jnp.int32)
        line = jnp.where(lane == 0, group[particle], line)
        line = jnp.where(lane == LIMIT_AT, limit[particle], line)
        for shift in range(shifts):
            line = jnp.where(lane == X_AT + shift, offsets[particle, 0, shift], line)
            line = jnp.where(lane == Y_AT + shift, offsets[particle, 1, shift], line)
        numbers = jnp.where(row == particle, line, numbers)
    packed_ref[0, :, pl.ds(full, LANES)] = numbers.astype(jnp.float32).astype(jnp.bfloat16)
    copies[0].wait()


def split_thirds(value):
    high = value.astype(jnp.bfloat16)
    rest = value - high.astype(jnp.float32)
    middle = rest.astype(jnp.bfloat16)
    return high, middle, (rest - middle.astype(jnp.float32)).astype(jnp.bfloat16)


def power_kernel(own_ref, other_ref, both_ref, high_ref, low_ref):
    rows, full = own_ref.shape
    half = full // 2
    for place, ref in enumerate((own_ref, other_ref)):
        at = pl.ds(place * rows, rows)
        both_ref[at, :] = ref[...]
        real = ref[:, :half].astype(jnp.float32)
        imag = ref[:, half:].astype(jnp.float32)
        high, low = split_halves(real * real + imag * imag)
        high_ref[at, :] = high
        low_ref[at, :] = low


def table_kernel(ctf_ref, noise_ref, table_ref):
    groups, half = ctf_ref.shape
    for place, ref in enumerate((ctf_ref, noise_ref)):
        for third, part in enumerate(split_thirds(ref[...])):
            table_ref[pl.ds(third * groups, groups), pl.ds(place * half, half)] = part


def score_kernel(sources, by_distance, shifts, has_earlier, *refs):
    pieces = refs[: len(sources)]
    refs = refs[len(sources) :]
    both_ref, high_ref, low_ref, table_ref = refs[:4]
    refs = refs[4:]
    if has_earlier:
        earlier_own_ref, earlier_other_ref, earlier_stats_ref = refs[:3]
        refs = refs[3:]
    weighted_ref, exps_ref, exps_other_ref, stats_ref = refs[:4]
    image_ref, real_ref, imag_ref, cross_ref, square_ref = refs[4:]
    full = both_ref.shape[1]
    half = full // 2
    groups = table_ref.shape[0] // 3
    candidates = both_ref.shape[0]
    rows_total = image_ref.shape[0]
    per_device = pieces[0].shape[1]
    scale = 0.5 / math.sqrt(half)
    chip = lax.axis_index("blk") >> 1
    for piece, places in zip(pieces, sources):
        for row, place in enumerate(places):
            if by_distance:
                place = (chip ^ place) & (NEAR - 1)
            values = piece[row].astype(jnp.float32)
            for sub in range(per_device):
                image_ref[pl.ds(place * per_device + sub, 1), :] = values[sub : sub + 1]

    block_rows = shifts * ROWS
    slot = 1 if has_earlier else 0
    if has_earlier:
        exps_ref[0] = earlier_own_ref[0]
        exps_other_ref[0] = earlier_other_ref[0]

    def block(index, carry):
        rows = pl.ds(pl.multiple_of(index * ROWS, ROWS), ROWS)
        first = pl.multiple_of(index * block_rows, ROWS)
        numbers = image_ref[rows, full:]
        column = lax.broadcasted_iota(jnp.int32, (ROWS, 3 * groups), 1) % groups
        one_hot = (numbers[:, :1].astype(jnp.int32) == column).astype(jnp.bfloat16)
        tables = jnp.dot(one_hot, table_ref[...], preferred_element_type=jnp.float32)
        ctf = tables[:, :half]
        noise = tables[:, half:]
        limit = numbers[:, LIMIT_AT : LIMIT_AT + 1].astype(jnp.int32)
        position = lax.broadcasted_iota(jnp.int32, (ROWS, half), 1)
        freq_x = position >> int(math.log2(KY))
        freq_y = (position & (KY - 1)) - KY // 2
        weight = jnp.where(freq_x * freq_x + freq_y * freq_y < limit * limit, noise, 0.0)
        ctf_weight = weight * ctf
        real = image_ref[rows, :half]
        imag = image_ref[rows, half:full]
        norm = jnp.sum(weight * (real * real + imag * imag), axis=1, keepdims=True)
        real_ref[...] = ctf_weight * real
        imag_ref[...] = ctf_weight * imag
        quad_high, quad_low = split_halves(ctf_weight * ctf)
        quad_weight = jnp.concatenate([quad_high, quad_low], axis=0)
        quad = lax.dot_general(
            quad_weight, high_ref[...], NT, preferred_element_type=jnp.float32
        ) + lax.dot_general(quad_weight, low_ref[...], NT, preferred_element_type=jnp.float32)
        quad = quad[:ROWS] + quad[ROWS:]

        numbers_int = numbers.astype(jnp.int32)
        step_cos, step_sin = sin_cos(numbers_int * (LANES // KY))
        for start in range(0, shifts, 2):
            members = range(start, min(start + 2, shifts))

            def stacked(value, base):
                return jnp.concatenate(
                    [value[:, base + shift : base + shift + 1] for shift in members], axis=0
                )

            height = len(members) * ROWS
            lane = lax.broadcasted_iota(jnp.int32, (height, LANES), 1)
            turns = (lane >> int(math.log2(KY))) * stacked(numbers_int, X_AT) + (
                (lane & (KY - 1)) - KY // 2
            ) * stacked(numbers_int, Y_AT)
            cosine, sine = sin_cos(turns)
            turn_cos = stacked(step_cos, X_AT)
            turn_sin = stacked(step_sin, X_AT)
            cosine_before = cosine * turn_cos + sine * turn_sin
            sine_before = sine * turn_cos - cosine * turn_sin
            double = jnp.broadcast_to(2.0 * turn_cos, (height, LANES))
            out_rows = pl.ds(first + start * ROWS, height)
            for chunk in range(half // LANES):
                at = pl.ds(chunk * LANES, LANES)
                real = jnp.concatenate([real_ref[:, at]] * len(members), axis=0)
                imag = jnp.concatenate([imag_ref[:, at]] * len(members), axis=0)
                weighted_ref[out_rows, at] = (real * cosine + imag * sine).astype(jnp.bfloat16)
                weighted_ref[out_rows, pl.ds(half + chunk * LANES, LANES)] = (
                    imag * cosine - real * sine
                ).astype(jnp.bfloat16)
                cosine, cosine_before = double * cosine - cosine_before, cosine
                sine, sine_before = double * sine - sine_before, sine

        cross_ref[...] = lax.dot_general(
            weighted_ref[pl.ds(first, block_rows), :],
            both_ref[...],
            NT,
            preferred_element_type=jnp.float32,
        )
        base = norm + quad
        scores = [
            -(base - 2.0 * cross_ref[pl.ds(shift * ROWS, ROWS), :]) * scale
            for shift in range(shifts)
        ]
        top = jnp.max(functools.reduce(jnp.maximum, scores), axis=1, keepdims=True)
        exps = [jnp.exp(score - top) for score in scores]
        total = jnp.sum(functools.reduce(jnp.add, exps), axis=1, keepdims=True)
        for shift in range(shifts):
            square_ref[pl.ds(shift * ROWS, ROWS), :candidates] = exps[shift]
        turned = square_ref[...].T
        exps_ref[index + slot] = turned[: candidates // 2, :block_rows]
        exps_other_ref[index + slot] = turned[candidates // 2 : candidates, :block_rows]
        row = lax.broadcasted_iota(jnp.int32, (ROWS, LANES), 0)
        lane = lax.broadcasted_iota(jnp.int32, (ROWS, LANES), 1)
        line = jnp.sum(
            jnp.where(lane == row, top, jnp.where(lane == row + LANES // 2, total, 0.0)),
            axis=0,
            keepdims=True,
        )
        if has_earlier:
            first_half = chip // NEAR == 0
            before = earlier_stats_ref[0]
            line = jnp.where(first_half, before, line) + pltpu.roll(
                jnp.where(first_half, line, before), ROWS, 1
            )
        for target in range(stats_ref.shape[0]):
            stats_ref[target, pl.ds(index, 1), :] = line
        return carry

    lax.fori_loop(0, rows_total // ROWS, block, 0)


def slice_kernel(scale, calls, by_distance, *refs):
    stats_ref, exps_own_ref, exps_other_ref = refs[:3]
    weighted_refs = (refs[3 : 3 + calls], refs[3 + calls : 3 + 2 * calls])
    out_hbm, best_hbm, log_hbm = refs[3 + 2 * calls : 6 + 2 * calls]
    best_ref, log_ref, posterior_ref, summed_ref, sems, number_sems = refs[6 + 2 * calls :]
    blocks, rows, block_rows = exps_own_ref.shape
    chips = stats_ref.shape[0]
    per_device = best_ref.shape[0]
    full = out_hbm.shape[1]
    index = lax.axis_index("blk")
    chip = index >> 1
    lane = lax.broadcasted_iota(jnp.int32, (1, LANES), 1)

    def combined(core, row):
        lines = [stats_ref[source, core, pl.ds(row, 1), :] for source in range(chips)]
        top = functools.reduce(jnp.maximum, lines)
        total = functools.reduce(
            jnp.add,
            [pltpu.roll(line, LANES // 2, 1) * jnp.exp(line - top) for line in lines],
        )
        log_total = top + jnp.log(total)
        return top, log_total, stats_ref[chip, core, pl.ds(row, 1), :]

    for side, exps_ref in enumerate((exps_own_ref, exps_other_ref)):
        core = (index & 1) ^ side
        for block in range(blocks):
            if block == 0 or not by_distance:
                top, log_total, mine = combined(core, block)
                line = jnp.exp(mine - log_total)
            factor = line
            if by_distance:
                first_half = chip // NEAR == block
                factor = jnp.where(first_half, line, pltpu.roll(line, LANES - ROWS, 1))
            factor = jnp.where(lane < ROWS, factor, 0.0)
            filled = ROWS
            while filled < LANES:
                factor = factor + pltpu.roll(factor, filled, 1)
                filled *= 2
            posterior_ref[side, block] = (exps_ref[block] * factor[:, :block_rows]).astype(
                jnp.bfloat16
            )

    width = 1024
    copies = []
    for number, start in enumerate(range(0, full, width)):
        at = pl.ds(start, width)
        products = []
        for side in range(2):
            for block in range(blocks):
                call, place = divmod(block, blocks // calls)
                products.append(
                    jnp.dot(
                        posterior_ref[side, block],
                        weighted_refs[side][call][pl.ds(place * block_rows, block_rows), at],
                        preferred_element_type=jnp.float32,
                    )
                )
        summed_ref[:, at] = functools.reduce(jnp.add, products) * scale
        copy = pltpu.make_async_copy(summed_ref.at[:, at], out_hbm.at[:, at], sems.at[number])
        copy.start()
        copies.append(copy)
        if number == 0:
            for row in range(per_device):
                particle = chip * per_device + row
                if by_distance:
                    top, log_total, mine = combined(index & 1, 0)
                    chosen = lane == particle
                else:
                    top, log_total, mine = combined(index & 1, particle // ROWS)
                    chosen = lane == particle % ROWS
                best_ref[row] = jnp.sum(jnp.where(chosen, jnp.exp(top - log_total), 0.0))
                log_ref[row] = jnp.sum(jnp.where(chosen, log_total, 0.0))
            copies.append(pltpu.make_async_copy(best_ref, best_hbm, number_sems.at[0]))
            copies.append(pltpu.make_async_copy(log_ref, log_hbm, number_sems.at[1]))
            copies[-2].start()
            copies[-1].start()
    for copy in copies:
        copy.wait()


def local(
    axis_size, projections, images, ctf_group, shift_offsets, shell_limit, ctf_table, noise_weight
):
    batch_count, orient_dev, full = projections.shape
    half = full // 2
    own_rows = batch_count * orient_dev
    candidates = 2 * own_rows
    per_device = images.shape[0]
    shifts = shift_offsets.shape[1]
    chips = axis_size // 2
    particles = chips * per_device
    blocks = particles // ROWS
    block_rows = shifts * ROWS
    megabytes = 12 + -(-2 * blocks * block_rows * full * 2 // 2**20)
    params = pltpu.CompilerParams(vmem_limit_bytes=megabytes * 2**20)

    def swap(value, mask):
        return lax.ppermute(value, "blk", [(i, i ^ mask) for i in range(axis_size)])

    packed = pl.pallas_call(
        pack_kernel,
        out_shape=jax.ShapeDtypeStruct((1, per_device, full + LANES), jnp.bfloat16),
        in_specs=[HBM] * 4,
        out_specs=VMEM,
        scratch_shapes=[
            pltpu.SMEM((per_device,), jnp.int32),
            pltpu.SMEM((per_device,), jnp.int32),
            pltpu.SMEM((per_device, 2, shifts), jnp.int32),
            pltpu.SemaphoreType.DMA((4,)),
        ],
        compiler_params=pltpu.CompilerParams(vmem_limit_bytes=60 * 2**20),
        name="pack",
    )(images, ctf_group, shell_limit, shift_offsets.transpose(0, 2, 1))
    by_distance = chips == 2 * NEAR and per_device * NEAR == ROWS
    received = swap(packed, 2) if by_distance else packed
    flat = projections.reshape(own_rows, full)
    other = swap(flat, 1)
    groups = ctf_table.shape[0]
    both, high, low = pl.pallas_call(
        power_kernel,
        out_shape=(
            jax.ShapeDtypeStruct((candidates, full), jnp.bfloat16),
            jax.ShapeDtypeStruct((candidates, half), jnp.bfloat16),
            jax.ShapeDtypeStruct((candidates, half), jnp.bfloat16),
        ),
        in_specs=[VMEM] * 2,
        out_specs=(VMEM,) * 3,
        compiler_params=params,
        cost_estimate=pl.CostEstimate(
            flops=8 * candidates * full, bytes_accessed=4 * candidates * full, transcendentals=0
        ),
        name="power",
    )(flat, other)
    tables = pl.pallas_call(
        table_kernel,
        out_shape=jax.ShapeDtypeStruct((3 * groups, full), jnp.bfloat16),
        in_specs=[VMEM] * 2,
        out_specs=VMEM,
        compiler_params=params,
        cost_estimate=pl.CostEstimate(
            flops=6 * groups * full, bytes_accessed=10 * groups * full, transcendentals=0
        ),
        name="tables",
    )(ctf_table, noise_weight)
    if by_distance:
        pair = jnp.zeros((2,) + packed.shape[1:], packed.dtype)
        pair = lax.dynamic_update_slice(pair, packed, (0, 0, 0))
        pair, received, both, high, low = lax.optimization_barrier(
            (pair, received, both, high, low)
        )
        pair = lax.dynamic_update_slice(pair, received, (1, 0, 0))
        pieces = [pair] + [swap(pair, mask) for mask in range(4, axis_size, 4)]
        parts = [(pieces[:2], ((0, 1), (2, 3))), (pieces[2:], ((4, 5), (6, 7)))]
    else:
        same_core = [[2 * c + core for c in range(chips)] for core in range(2)]
        gathered = lax.all_gather(
            packed, "blk", axis=0, tiled=True, axis_index_groups=same_core
        )
        parts = [([gathered], (tuple(range(chips)),))]

    all_weighted = []
    earlier = ()
    for pieces, sources in parts:
        last = len(all_weighted) == len(parts) - 1
        own_blocks = blocks // len(parts)
        seen = blocks if last else own_blocks
        weighted, *earlier = pl.pallas_call(
            functools.partial(score_kernel, sources, by_distance, shifts, bool(earlier)),
            out_shape=(
                jax.ShapeDtypeStruct((own_blocks * block_rows, full), jnp.bfloat16),
                jax.ShapeDtypeStruct((seen, own_rows, block_rows), jnp.float32),
                jax.ShapeDtypeStruct((seen, own_rows, block_rows), jnp.float32),
                jax.ShapeDtypeStruct(
                    (axis_size if last else 1, 1 if by_distance else blocks, LANES), jnp.float32
                ),
            ),
            in_specs=[VMEM] * (len(pieces) + 4 + len(earlier)),
            out_specs=(VMEM,) * 4,
            scratch_shapes=[
                pltpu.VMEM((own_blocks * ROWS, full + LANES), jnp.float32),
                pltpu.VMEM((ROWS, half), jnp.float32),
                pltpu.VMEM((ROWS, half), jnp.float32),
                pltpu.VMEM((block_rows, candidates), jnp.float32),
                pltpu.VMEM((-(-block_rows // LANES) * LANES, LANES), jnp.float32),
            ],
            compiler_params=params,
            cost_estimate=pl.CostEstimate(
                flops=2 * own_blocks * block_rows * full * (candidates + 8),
                bytes_accessed=2 * own_blocks * block_rows * full,
                transcendentals=0,
            ),
            name="scores",
        )(*pieces, both, high, low, tables, *earlier)
        all_weighted.append(weighted)
    exps, exps_other, stats = earlier

    exchanged = [swap(weighted, 1) for weighted in all_weighted]
    exps_in = swap(exps_other, 1)
    gathered = lax.all_to_all(stats, "blk", 0, 0)
    gathered = gathered.reshape((chips, 2) + gathered.shape[1:])

    slices, best_posterior, log_total = pl.pallas_call(
        functools.partial(
            slice_kernel, own_rows / per_device, len(all_weighted), by_distance
        ),
        out_shape=(
            jax.ShapeDtypeStruct((own_rows, full), jnp.float32),
            jax.ShapeDtypeStruct((per_device,), jnp.float32),
            jax.ShapeDtypeStruct((per_device,), jnp.float32),
        ),
        in_specs=[VMEM] * (3 + 2 * len(all_weighted)),
        out_specs=(HBM, HBM, HBM),
        scratch_shapes=[
            pltpu.SMEM((per_device,), jnp.float32),
            pltpu.SMEM((per_device,), jnp.float32),
            pltpu.VMEM((2, blocks, own_rows, block_rows), jnp.bfloat16),
            pltpu.VMEM((own_rows, full), jnp.float32),
            pltpu.SemaphoreType.DMA((full // 1024,)),
            pltpu.SemaphoreType.DMA((2,)),
        ],
        compiler_params=params,
        name="slices",
    )(gathered, exps, exps_in, *all_weighted, *exchanged)
    return (slices.reshape(batch_count, orient_dev, full), best_posterior, log_total)


def solution(mesh):
    in_specs = (
        P(None, ("groups", "blk"), None),
        P(("groups", "blk"), None),
        P(("groups", "blk")),
        P(("groups", "blk"), None, None),
        P(("groups", "blk")),
        P("groups", None),
        P("groups", None),
    )
    out_specs = (P(None, ("groups", "blk"), None), P(("groups", "blk")), P(("groups", "blk")))
    return jax.shard_map(
        functools.partial(local, mesh.shape["blk"]),
        mesh=mesh,
        in_specs=in_specs,
        out_specs=out_specs,
        check_vma=False,
    )
```

```python
import functools
import math

import jax
import jax.numpy as jnp
from jax import lax
from jax.experimental import pallas as pl
from jax.experimental.pallas import tpu as pltpu
from jax.sharding import PartitionSpec as P

KY = 64
IMG = 256
LANES = 128
ROWS = 8
NEAR = 4
GROUP = 1024
LIMIT_AT = 1
X_AT = 16
Y_AT = 48

VMEM = pl.BlockSpec(memory_space=pltpu.VMEM)
HBM = pl.BlockSpec(memory_space=pltpu.HBM)
NT = (((1,), (1,)), ((), ()))


def sin_cos(turns):
    quarter = IMG // 4
    wrapped = (turns + quarter // 2) & (IMG - 1)
    quadrant = wrapped >> int(math.log2(quarter))
    angle = (wrapped - quadrant * quarter - quarter // 2).astype(jnp.float32) * (
        2.0 * math.pi / IMG
    )
    square = angle * angle
    even = 1.0 + square * (
        -1.0 / 2 + square * (1.0 / 24 + square * (-1.0 / 720 + square * (1.0 / 40320)))
    )
    odd = angle * (
        1.0
        + square
        * (-1.0 / 6 + square * (1.0 / 120 + square * (-1.0 / 5040 + square * (1.0 / 362880))))
    )
    swapped = (quadrant & 1) == 1
    cosine = jnp.where(swapped, odd, even)
    sine = jnp.where(swapped, even, odd)
    cosine = jnp.where((quadrant == 1) | (quadrant == 2), -cosine, cosine)
    sine = jnp.where(quadrant >= 2, -sine, sine)
    return cosine, sine


def split_halves(value):
    high = value.astype(jnp.bfloat16)
    return high, (value - high.astype(jnp.float32)).astype(jnp.bfloat16)


def pack_kernel(images_hbm, group_hbm, limit_hbm, offsets_hbm, packed_ref, group, limit, offsets, sems):
    per_device, full = images_hbm.shape
    shifts = offsets_hbm.shape[2]
    copies = [
        pltpu.make_async_copy(images_hbm, packed_ref.at[0, :, pl.ds(0, full)], sems.at[0]),
        pltpu.make_async_copy(group_hbm, group, sems.at[1]),
        pltpu.make_async_copy(limit_hbm, limit, sems.at[2]),
        pltpu.make_async_copy(offsets_hbm, offsets, sems.at[3]),
    ]
    for copy in copies:
        copy.start()
    for copy in copies[1:]:
        copy.wait()
    row = lax.broadcasted_iota(jnp.int32, (per_device, LANES), 0)
    lane = lax.broadcasted_iota(jnp.int32, (per_device, LANES), 1)
    numbers = jnp.zeros((per_device, LANES), jnp.int32)
    for particle in range(per_device):
        line = jnp.zeros((per_device, LANES), jnp.int32)
        line = jnp.where(lane == 0, group[particle], line)
        line = jnp.where(lane == LIMIT_AT, limit[particle], line)
        for shift in range(shifts):
            line = jnp.where(lane == X_AT + shift, offsets[particle, 0, shift], line)
            line = jnp.where(lane == Y_AT + shift, offsets[particle, 1, shift], line)
        numbers = jnp.where(row == particle, line, numbers)
    packed_ref[0, :, pl.ds(full, LANES)] = numbers.astype(jnp.float32).astype(jnp.bfloat16)
    copies[0].wait()


def split_thirds(value):
    high = value.astype(jnp.bfloat16)
    rest = value - high.astype(jnp.float32)
    middle = rest.astype(jnp.bfloat16)
    return high, middle, (rest - middle.astype(jnp.float32)).astype(jnp.bfloat16)


def power_kernel(own_ref, other_ref, both_ref, high_ref, low_ref):
    rows, full = own_ref.shape
    half = full // 2
    for place, ref in enumerate((own_ref, other_ref)):
        at = pl.ds(place * rows, rows)
        both_ref[at, :] = ref[...]
        real = ref[:, :half].astype(jnp.float32)
        imag = ref[:, half:].astype(jnp.float32)
        high, low = split_halves(real * real + imag * imag)
        high_ref[at, :] = high
        low_ref[at, :] = low


def table_kernel(ctf_ref, noise_ref, table_ref):
    groups, half = ctf_ref.shape
    for place, ref in enumerate((ctf_ref, noise_ref)):
        for third, part in enumerate(split_thirds(ref[...])):
            table_ref[pl.ds(third * groups, groups), pl.ds(place * half, half)] = part


def score_kernel(sources, by_distance, shifts, has_earlier, *refs):
    pieces = refs[: len(sources)]
    refs = refs[len(sources) :]
    both_ref, high_ref, low_ref, table_ref = refs[:4]
    refs = refs[4:]
    if has_earlier:
        earlier_own_ref, earlier_other_ref, earlier_stats_ref = refs[:3]
        refs = refs[3:]
    weighted_ref, exps_ref, exps_other_ref, stats_ref = refs[:4]
    image_ref, real_ref, imag_ref, cross_ref, square_ref = refs[4:]
    full = both_ref.shape[1]
    half = full // 2
    groups = table_ref.shape[0] // 3
    candidates = both_ref.shape[0]
    rows_total = image_ref.shape[0]
    per_device = pieces[0].shape[1]
    scale = 0.5 / math.sqrt(half)
    chip = lax.axis_index("blk") >> 1
    for piece, places in zip(pieces, sources):
        for row, place in enumerate(places):
            if by_distance:
                place = (chip ^ place) & (NEAR - 1)
            values = piece[row].astype(jnp.float32)
            for sub in range(per_device):
                image_ref[pl.ds(place * per_device + sub, 1), :] = values[sub : sub + 1]

    block_rows = shifts * ROWS
    slot = 1 if has_earlier else 0
    if has_earlier:
        exps_ref[0] = earlier_own_ref[0]
        exps_other_ref[0] = earlier_other_ref[0]

    def block(index, carry):
        rows = pl.ds(pl.multiple_of(index * ROWS, ROWS), ROWS)
        first = pl.multiple_of(index * block_rows, ROWS)
        numbers = image_ref[rows, full:]
        column = lax.broadcasted_iota(jnp.int32, (ROWS, 3 * groups), 1) % groups
        one_hot = (numbers[:, :1].astype(jnp.int32) == column).astype(jnp.bfloat16)
        tables = jnp.dot(one_hot, table_ref[...], preferred_element_type=jnp.float32)
        ctf = tables[:, :half]
        noise = tables[:, half:]
        limit = numbers[:, LIMIT_AT : LIMIT_AT + 1].astype(jnp.int32)
        position = lax.broadcasted_iota(jnp.int32, (ROWS, half), 1)
        freq_x = position >> int(math.log2(KY))
        freq_y = (position & (KY - 1)) - KY // 2
        weight = jnp.where(freq_x * freq_x + freq_y * freq_y < limit * limit, noise, 0.0)
        ctf_weight = weight * ctf
        real = image_ref[rows, :half]
        imag = image_ref[rows, half:full]
        norm = jnp.sum(weight * (real * real + imag * imag), axis=1, keepdims=True)
        real_ref[...] = ctf_weight * real
        imag_ref[...] = ctf_weight * imag
        quad_high, quad_low = split_halves(ctf_weight * ctf)
        quad_weight = jnp.concatenate([quad_high, quad_low], axis=0)
        quad = lax.dot_general(
            quad_weight, high_ref[...], NT, preferred_element_type=jnp.float32
        ) + lax.dot_general(quad_weight, low_ref[...], NT, preferred_element_type=jnp.float32)
        quad = quad[:ROWS] + quad[ROWS:]

        numbers_int = numbers.astype(jnp.int32)
        step_cos, step_sin = sin_cos(numbers_int * (LANES // KY))
        phases = []
        for start in range(0, shifts, 2):
            members = range(start, min(start + 2, shifts))

            def stacked(value, base):
                return jnp.concatenate(
                    [value[:, base + shift : base + shift + 1] for shift in members], axis=0
                )

            height = len(members) * ROWS
            lane = lax.broadcasted_iota(jnp.int32, (height, LANES), 1)
            turns = (lane >> int(math.log2(KY))) * stacked(numbers_int, X_AT) + (
                (lane & (KY - 1)) - KY // 2
            ) * stacked(numbers_int, Y_AT)
            cosine, sine = sin_cos(turns)
            turn_cos = stacked(step_cos, X_AT)
            turn_sin = stacked(step_sin, X_AT)
            cosine_before = cosine * turn_cos + sine * turn_sin
            sine_before = sine * turn_cos - cosine * turn_sin
            double = jnp.broadcast_to(2.0 * turn_cos, (height, LANES))
            phases.append((cosine, cosine_before, sine, sine_before, double))

        cross = jnp.zeros(cross_ref.shape, jnp.float32)
        for group in range(0, half, GROUP):
            for number, phase in enumerate(phases):
                cosine, cosine_before, sine, sine_before, double = phase
                height = double.shape[0]
                out_rows = pl.ds(first + 2 * number * ROWS, height)
                for start in range(group, group + GROUP, LANES):
                    at = pl.ds(start, LANES)
                    real = jnp.concatenate([real_ref[:, at]] * (height // ROWS), axis=0)
                    imag = jnp.concatenate([imag_ref[:, at]] * (height // ROWS), axis=0)
                    weighted_ref[out_rows, at] = (real * cosine + imag * sine).astype(
                        jnp.bfloat16
                    )
                    weighted_ref[out_rows, pl.ds(half + start, LANES)] = (
                        imag * cosine - real * sine
                    ).astype(jnp.bfloat16)
                    cosine, cosine_before = double * cosine - cosine_before, cosine
                    sine, sine_before = double * sine - sine_before, sine
                phases[number] = (cosine, cosine_before, sine, sine_before, double)
            for base in (group, half + group):
                at = pl.ds(base, GROUP)
                cross = cross + lax.dot_general(
                    weighted_ref[pl.ds(first, block_rows), at],
                    both_ref[:, at],
                    NT,
                    preferred_element_type=jnp.float32,
                )
        cross_ref[...] = cross
        base = norm + quad
        scores = [
            -(base - 2.0 * cross_ref[pl.ds(shift * ROWS, ROWS), :]) * scale
            for shift in range(shifts)
        ]
        top = jnp.max(functools.reduce(jnp.maximum, scores), axis=1, keepdims=True)
        exps = [jnp.exp(score - top) for score in scores]
        total = jnp.sum(functools.reduce(jnp.add, exps), axis=1, keepdims=True)
        for shift in range(shifts):
            square_ref[pl.ds(shift * ROWS, ROWS), :candidates] = exps[shift]
        turned = square_ref[...].T
        exps_ref[index + slot] = turned[: candidates // 2, :block_rows]
        exps_other_ref[index + slot] = turned[candidates // 2 : candidates, :block_rows]
        row = lax.broadcasted_iota(jnp.int32, (ROWS, LANES), 0)
        lane = lax.broadcasted_iota(jnp.int32, (ROWS, LANES), 1)
        half_at = chip // NEAR ^ slot if by_distance else 0
        here = (lane & (2 * ROWS - 1)) == row + half_at * ROWS
        line = jnp.sum(
            jnp.where(here, jnp.where(lane < LANES // 2, top, total), 0.0),
            axis=0,
            keepdims=True,
        )
        if has_earlier:
            line = line + earlier_stats_ref[0]
        for target in range(stats_ref.shape[0]):
            stats_ref[target, pl.ds(index, 1), :] = line
        return carry

    lax.fori_loop(0, rows_total // ROWS, block, 0)


def slice_kernel(scale, calls, by_distance, *refs):
    stats_ref, exps_own_ref, exps_other_ref = refs[:3]
    weighted_refs = (refs[3 : 3 + calls], refs[3 + calls : 3 + 2 * calls])
    out_hbm, best_hbm, log_hbm = refs[3 + 2 * calls : 6 + 2 * calls]
    best_ref, log_ref, posterior_ref, summed_ref, sems, number_sems = refs[6 + 2 * calls :]
    blocks, rows, block_rows = exps_own_ref.shape
    chips = stats_ref.shape[0]
    per_device = best_ref.shape[0]
    full = out_hbm.shape[1]
    index = lax.axis_index("blk")
    chip = index >> 1
    lane = lax.broadcasted_iota(jnp.int32, (1, LANES), 1)

    def combined(core, row):
        at = pl.ds(row, 1)
        lower = lane < LANES // 2
        lines = [stats_ref[source, core, at, :] for source in range(chips)]
        lines.append(stats_ref[chip, core, at, :])
        turned = [pltpu.roll(line, LANES // 2, 1) for line in lines]
        tops = [jnp.where(lower, one, two) for one, two in zip(lines, turned)]
        totals = [jnp.where(lower, two, one) for one, two in zip(lines, turned)]
        top = functools.reduce(jnp.maximum, tops)
        total = functools.reduce(
            jnp.add, [part * jnp.exp(high - top) for high, part in zip(tops[:-1], totals)]
        )
        return top, top + jnp.log(total), tops[-1]

    upper = (lane & ROWS) != 0
    for side, exps_ref in enumerate((exps_own_ref, exps_other_ref)):
        core = (index & 1) ^ side
        for block in range(blocks):
            if block == 0 or not by_distance:
                top, log_total, mine = combined(core, block)
                line = jnp.exp(mine - log_total)
                crossed = pltpu.roll(line, ROWS, 1)
            wanted = (chip // NEAR ^ block) != 0 if by_distance else False
            factor = jnp.where(upper == wanted, line, crossed)
            posterior_ref[side, block] = (exps_ref[block] * factor[:, :block_rows]).astype(
                jnp.bfloat16
            )

    width = 1024
    copies = []
    for number, start in enumerate(range(0, full, width)):
        at = pl.ds(start, width)
        products = []
        for side in range(2):
            for block in range(blocks):
                call, place = divmod(block, blocks // calls)
                products.append(
                    jnp.dot(
                        posterior_ref[side, block],
                        weighted_refs[side][call][pl.ds(place * block_rows, block_rows), at],
                        preferred_element_type=jnp.float32,
                    )
                )
        summed_ref[:, at] = functools.reduce(jnp.add, products) * scale
        copy = pltpu.make_async_copy(summed_ref.at[:, at], out_hbm.at[:, at], sems.at[number])
        copy.start()
        copies.append(copy)
        if number == 0:
            for row in range(per_device):
                particle = chip * per_device + row
                if by_distance:
                    top, log_total, mine = combined(index & 1, 0)
                    chosen = lane == particle
                else:
                    top, log_total, mine = combined(index & 1, particle // ROWS)
                    chosen = lane == particle % ROWS
                best_ref[row] = jnp.sum(jnp.where(chosen, jnp.exp(top - log_total), 0.0))
                log_ref[row] = jnp.sum(jnp.where(chosen, log_total, 0.0))
            copies.append(pltpu.make_async_copy(best_ref, best_hbm, number_sems.at[0]))
            copies.append(pltpu.make_async_copy(log_ref, log_hbm, number_sems.at[1]))
            copies[-2].start()
            copies[-1].start()
    for copy in copies:
        copy.wait()


def local(
    axis_size, projections, images, ctf_group, shift_offsets, shell_limit, ctf_table, noise_weight
):
    batch_count, orient_dev, full = projections.shape
    half = full // 2
    own_rows = batch_count * orient_dev
    candidates = 2 * own_rows
    per_device = images.shape[0]
    shifts = shift_offsets.shape[1]
    chips = axis_size // 2
    particles = chips * per_device
    blocks = particles // ROWS
    block_rows = shifts * ROWS
    megabytes = 12 + -(-2 * blocks * block_rows * full * 2 // 2**20)
    params = pltpu.CompilerParams(vmem_limit_bytes=megabytes * 2**20)

    def swap(value, mask):
        return lax.ppermute(value, "blk", [(i, i ^ mask) for i in range(axis_size)])

    packed = pl.pallas_call(
        pack_kernel,
        out_shape=jax.ShapeDtypeStruct((1, per_device, full + LANES), jnp.bfloat16),
        in_specs=[HBM] * 4,
        out_specs=VMEM,
        scratch_shapes=[
            pltpu.SMEM((per_device,), jnp.int32),
            pltpu.SMEM((per_device,), jnp.int32),
            pltpu.SMEM((per_device, 2, shifts), jnp.int32),
            pltpu.SemaphoreType.DMA((4,)),
        ],
        compiler_params=pltpu.CompilerParams(vmem_limit_bytes=60 * 2**20),
        name="pack",
    )(images, ctf_group, shell_limit, shift_offsets.transpose(0, 2, 1))
    by_distance = chips == 2 * NEAR and per_device * NEAR == ROWS
    received = swap(packed, 2) if by_distance else packed
    flat = projections.reshape(own_rows, full)
    other = swap(flat, 1)
    groups = ctf_table.shape[0]
    both, high, low = pl.pallas_call(
        power_kernel,
        out_shape=(
            jax.ShapeDtypeStruct((candidates, full), jnp.bfloat16),
            jax.ShapeDtypeStruct((candidates, half), jnp.bfloat16),
            jax.ShapeDtypeStruct((candidates, half), jnp.bfloat16),
        ),
        in_specs=[VMEM] * 2,
        out_specs=(VMEM,) * 3,
        compiler_params=params,
        cost_estimate=pl.CostEstimate(
            flops=8 * candidates * full, bytes_accessed=4 * candidates * full, transcendentals=0
        ),
        name="power",
    )(flat, other)
    tables = pl.pallas_call(
        table_kernel,
        out_shape=jax.ShapeDtypeStruct((3 * groups, full), jnp.bfloat16),
        in_specs=[VMEM] * 2,
        out_specs=VMEM,
        compiler_params=params,
        cost_estimate=pl.CostEstimate(
            flops=6 * groups * full, bytes_accessed=10 * groups * full, transcendentals=0
        ),
        name="tables",
    )(ctf_table, noise_weight)
    if by_distance:
        pair = jnp.zeros((2,) + packed.shape[1:], packed.dtype)
        pair = lax.dynamic_update_slice(pair, packed, (0, 0, 0))
        pair, received, both, high, low = lax.optimization_barrier(
            (pair, received, both, high, low)
        )
        pair = lax.dynamic_update_slice(pair, received, (1, 0, 0))
        pieces = [pair] + [swap(pair, mask) for mask in range(4, axis_size, 4)]
        parts = [(pieces[:2], ((0, 1), (2, 3))), (pieces[2:], ((4, 5), (6, 7)))]
    else:
        same_core = [[2 * c + core for c in range(chips)] for core in range(2)]
        gathered = lax.all_gather(
            packed, "blk", axis=0, tiled=True, axis_index_groups=same_core
        )
        parts = [([gathered], (tuple(range(chips)),))]

    all_weighted = []
    earlier = ()
    for pieces, sources in parts:
        last = len(all_weighted) == len(parts) - 1
        own_blocks = blocks // len(parts)
        seen = blocks if last else own_blocks
        weighted, *earlier = pl.pallas_call(
            functools.partial(score_kernel, sources, by_distance, shifts, bool(earlier)),
            out_shape=(
                jax.ShapeDtypeStruct((own_blocks * block_rows, full), jnp.bfloat16),
                jax.ShapeDtypeStruct((seen, own_rows, block_rows), jnp.float32),
                jax.ShapeDtypeStruct((seen, own_rows, block_rows), jnp.float32),
                jax.ShapeDtypeStruct(
                    (axis_size if last else 1, 1 if by_distance else blocks, LANES), jnp.float32
                ),
            ),
            in_specs=[VMEM] * (len(pieces) + 4 + len(earlier)),
            out_specs=(VMEM,) * 4,
            scratch_shapes=[
                pltpu.VMEM((own_blocks * ROWS, full + LANES), jnp.float32),
                pltpu.VMEM((ROWS, half), jnp.float32),
                pltpu.VMEM((ROWS, half), jnp.float32),
                pltpu.VMEM((block_rows, candidates), jnp.float32),
                pltpu.VMEM((-(-block_rows // LANES) * LANES, LANES), jnp.float32),
            ],
            compiler_params=params,
            cost_estimate=pl.CostEstimate(
                flops=2 * own_blocks * block_rows * full * (candidates + 8),
                bytes_accessed=2 * own_blocks * block_rows * full,
                transcendentals=0,
            ),
            name="scores",
        )(*pieces, both, high, low, tables, *earlier)
        all_weighted.append(weighted)
    exps, exps_other, stats = earlier

    exchanged = [swap(weighted, 1) for weighted in all_weighted]
    exps_in = swap(exps_other, 1)
    gathered = lax.all_to_all(stats, "blk", 0, 0)
    gathered = gathered.reshape((chips, 2) + gathered.shape[1:])

    slices, best_posterior, log_total = pl.pallas_call(
        functools.partial(
            slice_kernel, own_rows / per_device, len(all_weighted), by_distance
        ),
        out_shape=(
            jax.ShapeDtypeStruct((own_rows, full), jnp.float32),
            jax.ShapeDtypeStruct((per_device,), jnp.float32),
            jax.ShapeDtypeStruct((per_device,), jnp.float32),
        ),
        in_specs=[VMEM] * (3 + 2 * len(all_weighted)),
        out_specs=(HBM, HBM, HBM),
        scratch_shapes=[
            pltpu.SMEM((per_device,), jnp.float32),
            pltpu.SMEM((per_device,), jnp.float32),
            pltpu.VMEM((2, blocks, own_rows, block_rows), jnp.bfloat16),
            pltpu.VMEM((own_rows, full), jnp.float32),
            pltpu.SemaphoreType.DMA((full // 1024,)),
            pltpu.SemaphoreType.DMA((2,)),
        ],
        compiler_params=params,
        name="slices",
    )(gathered, exps, exps_in, *all_weighted, *exchanged)
    return (slices.reshape(batch_count, orient_dev, full), best_posterior, log_total)


def solution(mesh):
    in_specs = (
        P(None, ("groups", "blk"), None),
        P(("groups", "blk"), None),
        P(("groups", "blk")),
        P(("groups", "blk"), None, None),
        P(("groups", "blk")),
        P("groups", None),
        P("groups", None),
    )
    out_specs = (P(None, ("groups", "blk"), None), P(("groups", "blk")), P(("groups", "blk")))
    return jax.shard_map(
        functools.partial(local, mesh.shape["blk"]),
        mesh=mesh,
        in_specs=in_specs,
        out_specs=out_specs,
        check_vma=False,
    )
```

```python
import functools
import math

import jax
import jax.numpy as jnp
from jax import lax
from jax.experimental import pallas as pl
from jax.experimental.pallas import tpu as pltpu
from jax.sharding import PartitionSpec as P

KY = 64
IMG = 256
LANES = 128
ROWS = 8
NEAR = 4
GROUP = 1024
LIMIT_AT = 1
X_AT = 16
Y_AT = 48

VMEM = pl.BlockSpec(memory_space=pltpu.VMEM)
HBM = pl.BlockSpec(memory_space=pltpu.HBM)
NT = (((1,), (1,)), ((), ()))


def sin_cos(turns):
    quarter = IMG // 4
    wrapped = (turns + quarter // 2) & (IMG - 1)
    quadrant = wrapped >> int(math.log2(quarter))
    angle = (wrapped - quadrant * quarter - quarter // 2).astype(jnp.float32) * (
        2.0 * math.pi / IMG
    )
    square = angle * angle
    even = 1.0 + square * (
        -1.0 / 2 + square * (1.0 / 24 + square * (-1.0 / 720 + square * (1.0 / 40320)))
    )
    odd = angle * (
        1.0
        + square
        * (-1.0 / 6 + square * (1.0 / 120 + square * (-1.0 / 5040 + square * (1.0 / 362880))))
    )
    swapped = (quadrant & 1) == 1
    cosine = jnp.where(swapped, odd, even)
    sine = jnp.where(swapped, even, odd)
    cosine = jnp.where((quadrant == 1) | (quadrant == 2), -cosine, cosine)
    sine = jnp.where(quadrant >= 2, -sine, sine)
    return cosine, sine


def split_halves(value):
    high = value.astype(jnp.bfloat16)
    return high, (value - high.astype(jnp.float32)).astype(jnp.bfloat16)


def pack_kernel(group_hbm, limit_hbm, offsets_hbm, packed_ref, group, limit, offsets, sems):
    per_device, _, shifts = offsets_hbm.shape
    copies = [
        pltpu.make_async_copy(group_hbm, group, sems.at[0]),
        pltpu.make_async_copy(limit_hbm, limit, sems.at[1]),
        pltpu.make_async_copy(offsets_hbm, offsets, sems.at[2]),
    ]
    for copy in copies:
        copy.start()
    for copy in copies:
        copy.wait()
    row = lax.broadcasted_iota(jnp.int32, (per_device, LANES), 0)
    lane = lax.broadcasted_iota(jnp.int32, (per_device, LANES), 1)
    numbers = jnp.zeros((per_device, LANES), jnp.int32)
    for particle in range(per_device):
        line = jnp.zeros((per_device, LANES), jnp.int32)
        line = jnp.where(lane == 0, group[particle], line)
        line = jnp.where(lane == LIMIT_AT, limit[particle], line)
        for shift in range(shifts):
            line = jnp.where(lane == X_AT + shift, offsets[particle, 0, shift], line)
            line = jnp.where(lane == Y_AT + shift, offsets[particle, 1, shift], line)
        numbers = jnp.where(row == particle, line, numbers)
    packed_ref[0] = numbers.astype(jnp.float32).astype(jnp.bfloat16)


def split_thirds(value):
    high = value.astype(jnp.bfloat16)
    rest = value - high.astype(jnp.float32)
    middle = rest.astype(jnp.bfloat16)
    return high, middle, (rest - middle.astype(jnp.float32)).astype(jnp.bfloat16)


def power_kernel(own_ref, other_ref, both_ref, high_ref, low_ref):
    rows, full = own_ref.shape
    half = full // 2
    for place, ref in enumerate((own_ref, other_ref)):
        at = pl.ds(place * rows, rows)
        both_ref[at, :] = ref[...]
        real = ref[:, :half].astype(jnp.float32)
        imag = ref[:, half:].astype(jnp.float32)
        high, low = split_halves(real * real + imag * imag)
        high_ref[at, :] = high
        low_ref[at, :] = low


def table_kernel(ctf_ref, noise_ref, table_ref):
    groups, half = ctf_ref.shape
    for place, ref in enumerate((ctf_ref, noise_ref)):
        for third, part in enumerate(split_thirds(ref[...])):
            table_ref[pl.ds(third * groups, groups), pl.ds(place * half, half)] = part


def score_kernel(sources, by_distance, shifts, has_earlier, *refs):
    pieces = refs[: len(sources)]
    refs = refs[len(sources) :]
    both_ref, high_ref, low_ref, table_ref = refs[:4]
    refs = refs[4:]
    if has_earlier:
        earlier_own_ref, earlier_other_ref, earlier_stats_ref = refs[:3]
        refs = refs[3:]
    weighted_ref, exps_ref, exps_other_ref, stats_ref = refs[:4]
    image_ref, real_ref, imag_ref, cross_ref, square_ref = refs[4:]
    full = both_ref.shape[1]
    half = full // 2
    groups = table_ref.shape[0] // 3
    candidates = both_ref.shape[0]
    rows_total = image_ref.shape[0]
    per_device = pieces[0].shape[1]
    scale = 0.5 / math.sqrt(half)
    chip = lax.axis_index("blk") >> 1
    for piece, places in zip(pieces, sources):
        for row, place in enumerate(places):
            if by_distance:
                place = (chip ^ place) & (NEAR - 1)
            values = piece[row].astype(jnp.float32)
            for sub in range(per_device):
                image_ref[pl.ds(place * per_device + sub, 1), :] = values[sub : sub + 1]

    block_rows = shifts * ROWS
    slot = 1 if has_earlier else 0
    if has_earlier:
        exps_ref[0] = earlier_own_ref[0]
        exps_other_ref[0] = earlier_other_ref[0]

    def block(index, carry):
        rows = pl.ds(pl.multiple_of(index * ROWS, ROWS), ROWS)
        first = pl.multiple_of(index * block_rows, ROWS)
        numbers = image_ref[rows, full:]
        column = lax.broadcasted_iota(jnp.int32, (ROWS, 3 * groups), 1) % groups
        one_hot = (numbers[:, :1].astype(jnp.int32) == column).astype(jnp.bfloat16)
        tables = jnp.dot(one_hot, table_ref[...], preferred_element_type=jnp.float32)
        ctf = tables[:, :half]
        noise = tables[:, half:]
        limit = numbers[:, LIMIT_AT : LIMIT_AT + 1].astype(jnp.int32)
        position = lax.broadcasted_iota(jnp.int32, (ROWS, half), 1)
        freq_x = position >> int(math.log2(KY))
        freq_y = (position & (KY - 1)) - KY // 2
        weight = jnp.where(freq_x * freq_x + freq_y * freq_y < limit * limit, noise, 0.0)
        ctf_weight = weight * ctf
        real = image_ref[rows, :half]
        imag = image_ref[rows, half:full]
        norm = jnp.sum(weight * (real * real + imag * imag), axis=1, keepdims=True)
        real_ref[...] = ctf_weight * real
        imag_ref[...] = ctf_weight * imag
        quad_high, quad_low = split_halves(ctf_weight * ctf)
        quad_weight = jnp.concatenate([quad_high, quad_low], axis=0)
        quad = lax.dot_general(
            quad_weight, high_ref[...], NT, preferred_element_type=jnp.float32
        ) + lax.dot_general(quad_weight, low_ref[...], NT, preferred_element_type=jnp.float32)
        quad = quad[:ROWS] + quad[ROWS:]

        numbers_int = numbers.astype(jnp.int32)
        step_cos, step_sin = sin_cos(numbers_int * (LANES // KY))
        phases = []
        for start in range(0, shifts, 2):
            members = range(start, min(start + 2, shifts))

            def stacked(value, base):
                return jnp.concatenate(
                    [value[:, base + shift : base + shift + 1] for shift in members], axis=0
                )

            height = len(members) * ROWS
            lane = lax.broadcasted_iota(jnp.int32, (height, LANES), 1)
            turns = (lane >> int(math.log2(KY))) * stacked(numbers_int, X_AT) + (
                (lane & (KY - 1)) - KY // 2
            ) * stacked(numbers_int, Y_AT)
            cosine, sine = sin_cos(turns)
            turn_cos = stacked(step_cos, X_AT)
            turn_sin = stacked(step_sin, X_AT)
            cosine_before = cosine * turn_cos + sine * turn_sin
            sine_before = sine * turn_cos - cosine * turn_sin
            double = jnp.broadcast_to(2.0 * turn_cos, (height, LANES))
            phases.append((cosine, cosine_before, sine, sine_before, double))

        cross = jnp.zeros(cross_ref.shape, jnp.float32)
        for group in range(0, half, GROUP):
            for number, phase in enumerate(phases):
                cosine, cosine_before, sine, sine_before, double = phase
                height = double.shape[0]
                out_rows = pl.ds(first + 2 * number * ROWS, height)
                for start in range(group, group + GROUP, LANES):
                    at = pl.ds(start, LANES)
                    real = jnp.concatenate([real_ref[:, at]] * (height // ROWS), axis=0)
                    imag = jnp.concatenate([imag_ref[:, at]] * (height // ROWS), axis=0)
                    weighted_ref[out_rows, at] = (real * cosine + imag * sine).astype(
                        jnp.bfloat16
                    )
                    weighted_ref[out_rows, pl.ds(half + start, LANES)] = (
                        imag * cosine - real * sine
                    ).astype(jnp.bfloat16)
                    cosine, cosine_before = double * cosine - cosine_before, cosine
                    sine, sine_before = double * sine - sine_before, sine
                phases[number] = (cosine, cosine_before, sine, sine_before, double)
            for base in (group, half + group):
                at = pl.ds(base, GROUP)
                cross = cross + lax.dot_general(
                    weighted_ref[pl.ds(first, block_rows), at],
                    both_ref[:, at],
                    NT,
                    preferred_element_type=jnp.float32,
                )
        cross_ref[...] = cross
        base = norm + quad
        scores = [
            -(base - 2.0 * cross_ref[pl.ds(shift * ROWS, ROWS), :]) * scale
            for shift in range(shifts)
        ]
        top = jnp.max(functools.reduce(jnp.maximum, scores), axis=1, keepdims=True)
        exps = [jnp.exp(score - top) for score in scores]
        total = jnp.sum(functools.reduce(jnp.add, exps), axis=1, keepdims=True)
        for shift in range(shifts):
            square_ref[pl.ds(shift * ROWS, ROWS), :candidates] = exps[shift]
        turned = square_ref[...].T
        exps_ref[index + slot] = turned[: candidates // 2, :block_rows]
        exps_other_ref[index + slot] = turned[candidates // 2 : candidates, :block_rows]
        row = lax.broadcasted_iota(jnp.int32, (ROWS, LANES), 0)
        lane = lax.broadcasted_iota(jnp.int32, (ROWS, LANES), 1)
        half_at = chip // NEAR ^ slot if by_distance else 0
        here = (lane & (2 * ROWS - 1)) == row + half_at * ROWS
        line = jnp.sum(
            jnp.where(here, jnp.where(lane < LANES // 2, top, total), 0.0),
            axis=0,
            keepdims=True,
        )
        if has_earlier:
            line = line + earlier_stats_ref[0]
        for target in range(stats_ref.shape[0]):
            stats_ref[target, pl.ds(index, 1), :] = line
        return carry

    lax.fori_loop(0, rows_total // ROWS, block, 0)


def slice_kernel(scale, calls, by_distance, *refs):
    stats_ref, exps_own_ref, exps_other_ref = refs[:3]
    weighted_refs = (refs[3 : 3 + calls], refs[3 + calls : 3 + 2 * calls])
    out_hbm, best_hbm, log_hbm = refs[3 + 2 * calls : 6 + 2 * calls]
    best_ref, log_ref, posterior_ref, summed_ref, sems, number_sems = refs[6 + 2 * calls :]
    blocks, rows, block_rows = exps_own_ref.shape
    chips = stats_ref.shape[0]
    per_device = best_ref.shape[0]
    full = out_hbm.shape[1]
    index = lax.axis_index("blk")
    chip = index >> 1
    lane = lax.broadcasted_iota(jnp.int32, (1, LANES), 1)

    def combined(core, row):
        at = pl.ds(row, 1)
        lower = lane < LANES // 2
        lines = [stats_ref[source, core, at, :] for source in range(chips)]
        lines.append(stats_ref[chip, core, at, :])
        turned = [pltpu.roll(line, LANES // 2, 1) for line in lines]
        tops = [jnp.where(lower, one, two) for one, two in zip(lines, turned)]
        totals = [jnp.where(lower, two, one) for one, two in zip(lines, turned)]
        top = functools.reduce(jnp.maximum, tops)
        total = functools.reduce(
            jnp.add, [part * jnp.exp(high - top) for high, part in zip(tops[:-1], totals)]
        )
        return top, top + jnp.log(total), tops[-1]

    upper = (lane & ROWS) != 0
    for side, exps_ref in enumerate((exps_own_ref, exps_other_ref)):
        core = (index & 1) ^ side
        for block in range(blocks):
            if block == 0 or not by_distance:
                top, log_total, mine = combined(core, block)
                line = jnp.exp(mine - log_total)
                crossed = pltpu.roll(line, ROWS, 1)
            wanted = (chip // NEAR ^ block) != 0 if by_distance else False
            factor = jnp.where(upper == wanted, line, crossed)
            posterior_ref[side, block] = (exps_ref[block] * factor[:, :block_rows]).astype(
                jnp.bfloat16
            )

    width = 1024
    copies = []
    for number, start in enumerate(range(0, full, width)):
        at = pl.ds(start, width)
        products = []
        for side in range(2):
            for block in range(blocks):
                call, place = divmod(block, blocks // calls)
                products.append(
                    jnp.dot(
                        posterior_ref[side, block],
                        weighted_refs[side][call][pl.ds(place * block_rows, block_rows), at],
                        preferred_element_type=jnp.float32,
                    )
                )
        summed_ref[:, at] = functools.reduce(jnp.add, products) * scale
        copy = pltpu.make_async_copy(summed_ref.at[:, at], out_hbm.at[:, at], sems.at[number])
        copy.start()
        copies.append(copy)
        if number == 0:
            for row in range(per_device):
                particle = chip * per_device + row
                if by_distance:
                    top, log_total, mine = combined(index & 1, 0)
                    chosen = lane == particle
                else:
                    top, log_total, mine = combined(index & 1, particle // ROWS)
                    chosen = lane == particle % ROWS
                best_ref[row] = jnp.sum(jnp.where(chosen, jnp.exp(top - log_total), 0.0))
                log_ref[row] = jnp.sum(jnp.where(chosen, log_total, 0.0))
            copies.append(pltpu.make_async_copy(best_ref, best_hbm, number_sems.at[0]))
            copies.append(pltpu.make_async_copy(log_ref, log_hbm, number_sems.at[1]))
            copies[-2].start()
            copies[-1].start()
    for copy in copies:
        copy.wait()


def local(
    axis_size, projections, images, ctf_group, shift_offsets, shell_limit, ctf_table, noise_weight
):
    batch_count, orient_dev, full = projections.shape
    half = full // 2
    own_rows = batch_count * orient_dev
    candidates = 2 * own_rows
    per_device = images.shape[0]
    shifts = shift_offsets.shape[1]
    chips = axis_size // 2
    particles = chips * per_device
    blocks = particles // ROWS
    block_rows = shifts * ROWS
    megabytes = 12 + -(-2 * blocks * block_rows * full * 2 // 2**20)
    params = pltpu.CompilerParams(vmem_limit_bytes=megabytes * 2**20)

    def swap(value, mask):
        return lax.ppermute(value, "blk", [(i, i ^ mask) for i in range(axis_size)])

    numbers = pl.pallas_call(
        pack_kernel,
        out_shape=jax.ShapeDtypeStruct((1, per_device, LANES), jnp.bfloat16),
        in_specs=[HBM] * 3,
        out_specs=VMEM,
        scratch_shapes=[
            pltpu.SMEM((per_device,), jnp.int32),
            pltpu.SMEM((per_device,), jnp.int32),
            pltpu.SMEM((per_device, 2, shifts), jnp.int32),
            pltpu.SemaphoreType.DMA((3,)),
        ],
        compiler_params=pltpu.CompilerParams(vmem_limit_bytes=60 * 2**20),
        name="pack",
    )(ctf_group, shell_limit, shift_offsets.transpose(0, 2, 1))
    by_distance = chips == 2 * NEAR and per_device * NEAR == ROWS
    rows = images[None]
    if by_distance:
        received = swap(rows, 2)

    flat = projections.reshape(own_rows, full)
    other = swap(flat, 1)
    if by_distance:
        rows, numbers, other = lax.optimization_barrier((rows, numbers, other))
        received_numbers = swap(numbers, 2)
    groups = ctf_table.shape[0]
    both, high, low = pl.pallas_call(
        power_kernel,
        out_shape=(
            jax.ShapeDtypeStruct((candidates, full), jnp.bfloat16),
            jax.ShapeDtypeStruct((candidates, half), jnp.bfloat16),
            jax.ShapeDtypeStruct((candidates, half), jnp.bfloat16),
        ),
        in_specs=[VMEM] * 2,
        out_specs=(VMEM,) * 3,
        compiler_params=params,
        cost_estimate=pl.CostEstimate(
            flops=8 * candidates * full, bytes_accessed=4 * candidates * full, transcendentals=0
        ),
        name="power",
    )(flat, other)
    tables = pl.pallas_call(
        table_kernel,
        out_shape=jax.ShapeDtypeStruct((3 * groups, full), jnp.bfloat16),
        in_specs=[VMEM] * 2,
        out_specs=VMEM,
        compiler_params=params,
        cost_estimate=pl.CostEstimate(
            flops=6 * groups * full, bytes_accessed=10 * groups * full, transcendentals=0
        ),
        name="tables",
    )(ctf_table, noise_weight)
    if by_distance:
        pair = jnp.zeros((2, per_device, full + LANES), images.dtype)
        pair = lax.dynamic_update_slice(pair, rows, (0, 0, 0))
        pair = lax.dynamic_update_slice(pair, numbers, (0, 0, full))
        pair, received, received_numbers, both, high, low = lax.optimization_barrier(
            (pair, received, received_numbers, both, high, low)
        )
        pair = lax.dynamic_update_slice(pair, received, (1, 0, 0))
        pair = lax.dynamic_update_slice(pair, received_numbers, (1, 0, full))
        pieces = [pair] + [swap(pair, mask) for mask in range(4, axis_size, 4)]
        parts = [(pieces[:2], ((0, 1), (2, 3))), (pieces[2:], ((4, 5), (6, 7)))]
    else:
        same_core = [[2 * c + core for c in range(chips)] for core in range(2)]
        gathered = lax.all_gather(
            jnp.concatenate([rows, numbers], axis=2), "blk", axis=0, tiled=True, axis_index_groups=same_core
        )
        parts = [([gathered], (tuple(range(chips)),))]

    all_weighted = []
    earlier = ()
    for pieces, sources in parts:
        last = len(all_weighted) == len(parts) - 1
        own_blocks = blocks // len(parts)
        seen = blocks if last else own_blocks
        weighted, *earlier = pl.pallas_call(
            functools.partial(score_kernel, sources, by_distance, shifts, bool(earlier)),
            out_shape=(
                jax.ShapeDtypeStruct((own_blocks * block_rows, full), jnp.bfloat16),
                jax.ShapeDtypeStruct((seen, own_rows, block_rows), jnp.float32),
                jax.ShapeDtypeStruct((seen, own_rows, block_rows), jnp.float32),
                jax.ShapeDtypeStruct(
                    (axis_size if last else 1, 1 if by_distance else blocks, LANES), jnp.float32
                ),
            ),
            in_specs=[VMEM] * (len(pieces) + 4 + len(earlier)),
            out_specs=(VMEM,) * 4,
            scratch_shapes=[
                pltpu.VMEM((own_blocks * ROWS, full + LANES), jnp.float32),
                pltpu.VMEM((ROWS, half), jnp.float32),
                pltpu.VMEM((ROWS, half), jnp.float32),
                pltpu.VMEM((block_rows, candidates), jnp.float32),
                pltpu.VMEM((-(-block_rows // LANES) * LANES, LANES), jnp.float32),
            ],
            compiler_params=params,
            cost_estimate=pl.CostEstimate(
                flops=2 * own_blocks * block_rows * full * (candidates + 8),
                bytes_accessed=2 * own_blocks * block_rows * full,
                transcendentals=0,
            ),
            name="scores",
        )(*pieces, both, high, low, tables, *earlier)
        all_weighted.append(weighted)
    exps, exps_other, stats = earlier

    exchanged = [swap(weighted, 1) for weighted in all_weighted]
    exps_in = swap(exps_other, 1)
    gathered = lax.all_to_all(stats, "blk", 0, 0)
    gathered = gathered.reshape((chips, 2) + gathered.shape[1:])

    slices, best_posterior, log_total = pl.pallas_call(
        functools.partial(
            slice_kernel, own_rows / per_device, len(all_weighted), by_distance
        ),
        out_shape=(
            jax.ShapeDtypeStruct((own_rows, full), jnp.float32),
            jax.ShapeDtypeStruct((per_device,), jnp.float32),
            jax.ShapeDtypeStruct((per_device,), jnp.float32),
        ),
        in_specs=[VMEM] * (3 + 2 * len(all_weighted)),
        out_specs=(HBM, HBM, HBM),
        scratch_shapes=[
            pltpu.SMEM((per_device,), jnp.float32),
            pltpu.SMEM((per_device,), jnp.float32),
            pltpu.VMEM((2, blocks, own_rows, block_rows), jnp.bfloat16),
            pltpu.VMEM((own_rows, full), jnp.float32),
            pltpu.SemaphoreType.DMA((full // 1024,)),
            pltpu.SemaphoreType.DMA((2,)),
        ],
        compiler_params=params,
        name="slices",
    )(gathered, exps, exps_in, *all_weighted, *exchanged)
    return (slices.reshape(batch_count, orient_dev, full), best_posterior, log_total)


def solution(mesh):
    in_specs = (
        P(None, ("groups", "blk"), None),
        P(("groups", "blk"), None),
        P(("groups", "blk")),
        P(("groups", "blk"), None, None),
        P(("groups", "blk")),
        P("groups", None),
        P("groups", None),
    )
    out_specs = (P(None, ("groups", "blk"), None), P(("groups", "blk")), P(("groups", "blk")))
    return jax.shard_map(
        functools.partial(local, mesh.shape["blk"]),
        mesh=mesh,
        in_specs=in_specs,
        out_specs=out_specs,
        check_vma=False,
    )
```

```python
import functools
import math

import jax
import jax.numpy as jnp
from jax import lax
from jax.experimental import pallas as pl
from jax.experimental.pallas import tpu as pltpu
from jax.sharding import PartitionSpec as P

KY = 64
IMG = 256
LANES = 128
ROWS = 8
NEAR = 4
GROUP = 1024
LIMIT_AT = 1
X_AT = 16
Y_AT = 48

VMEM = pl.BlockSpec(memory_space=pltpu.VMEM)
HBM = pl.BlockSpec(memory_space=pltpu.HBM)
NT = (((1,), (1,)), ((), ()))


def sin_cos(turns):
    quarter = IMG // 4
    wrapped = (turns + quarter // 2) & (IMG - 1)
    quadrant = wrapped >> int(math.log2(quarter))
    angle = (wrapped - quadrant * quarter - quarter // 2).astype(jnp.float32) * (
        2.0 * math.pi / IMG
    )
    square = angle * angle
    even = 1.0 + square * (
        -1.0 / 2 + square * (1.0 / 24 + square * (-1.0 / 720 + square * (1.0 / 40320)))
    )
    odd = angle * (
        1.0
        + square
        * (-1.0 / 6 + square * (1.0 / 120 + square * (-1.0 / 5040 + square * (1.0 / 362880))))
    )
    swapped = (quadrant & 1) == 1
    cosine = jnp.where(swapped, odd, even)
    sine = jnp.where(swapped, even, odd)
    cosine = jnp.where((quadrant == 1) | (quadrant == 2), -cosine, cosine)
    sine = jnp.where(quadrant >= 2, -sine, sine)
    return cosine, sine


def split_halves(value):
    high = value.astype(jnp.bfloat16)
    return high, (value - high.astype(jnp.float32)).astype(jnp.bfloat16)


def pack_kernel(group_hbm, limit_hbm, offsets_hbm, packed_ref, group, limit, offsets, sems):
    per_device, _, shifts = offsets_hbm.shape
    copies = [
        pltpu.make_async_copy(group_hbm, group, sems.at[0]),
        pltpu.make_async_copy(limit_hbm, limit, sems.at[1]),
        pltpu.make_async_copy(offsets_hbm, offsets, sems.at[2]),
    ]
    for copy in copies:
        copy.start()
    for copy in copies:
        copy.wait()
    row = lax.broadcasted_iota(jnp.int32, (per_device, LANES), 0)
    lane = lax.broadcasted_iota(jnp.int32, (per_device, LANES), 1)
    numbers = jnp.zeros((per_device, LANES), jnp.int32)
    for particle in range(per_device):
        line = jnp.zeros((per_device, LANES), jnp.int32)
        line = jnp.where(lane == 0, group[particle], line)
        line = jnp.where(lane == LIMIT_AT, limit[particle], line)
        for shift in range(shifts):
            line = jnp.where(lane == X_AT + shift, offsets[particle, 0, shift], line)
            line = jnp.where(lane == Y_AT + shift, offsets[particle, 1, shift], line)
        numbers = jnp.where(row == particle, line, numbers)
    packed_ref[0] = numbers.astype(jnp.float32).astype(jnp.bfloat16)


def split_thirds(value):
    high = value.astype(jnp.bfloat16)
    rest = value - high.astype(jnp.float32)
    middle = rest.astype(jnp.bfloat16)
    return high, middle, (rest - middle.astype(jnp.float32)).astype(jnp.bfloat16)


def power_kernel(own_ref, other_ref, both_ref, high_ref, low_ref):
    rows, full = own_ref.shape
    half = full // 2
    for place, ref in enumerate((own_ref, other_ref)):
        at = pl.ds(place * rows, rows)
        both_ref[at, :] = ref[...]
        real = ref[:, :half].astype(jnp.float32)
        imag = ref[:, half:].astype(jnp.float32)
        high, low = split_halves(real * real + imag * imag)
        high_ref[at, :] = high
        low_ref[at, :] = low


def table_kernel(ctf_ref, noise_ref, table_ref):
    groups, half = ctf_ref.shape
    for place, ref in enumerate((ctf_ref, noise_ref)):
        for third, part in enumerate(split_thirds(ref[...])):
            table_ref[pl.ds(third * groups, groups), pl.ds(place * half, half)] = part


def score_kernel(sources, by_distance, shifts, has_earlier, *refs):
    pieces = refs[: len(sources)]
    refs = refs[len(sources) :]
    both_ref, high_ref, low_ref, table_ref = refs[:4]
    refs = refs[4:]
    if has_earlier:
        earlier_own_ref, earlier_other_ref, earlier_stats_ref = refs[:3]
        refs = refs[3:]
    weighted_ref, exps_ref, exps_other_ref, stats_ref = refs[:4]
    image_ref, real_ref, imag_ref, cross_ref, square_ref = refs[4:]
    full = both_ref.shape[1]
    half = full // 2
    groups = table_ref.shape[0] // 3
    candidates = both_ref.shape[0]
    rows_total = image_ref.shape[0]
    per_device = pieces[0].shape[1]
    scale = 0.5 / math.sqrt(half)
    chip = lax.axis_index("blk") >> 1
    for piece, places in zip(pieces, sources):
        for row, place in enumerate(places):
            if by_distance:
                place = (chip ^ place) & (NEAR - 1)
            values = piece[row].astype(jnp.float32)
            for sub in range(per_device):
                image_ref[pl.ds(place * per_device + sub, 1), :] = values[sub : sub + 1]

    block_rows = shifts * ROWS
    slot = 1 if has_earlier else 0
    if has_earlier:
        exps_ref[0] = earlier_own_ref[0]
        exps_other_ref[0] = earlier_other_ref[0]

    def block(index, carry):
        rows = pl.ds(pl.multiple_of(index * ROWS, ROWS), ROWS)
        first = pl.multiple_of(index * block_rows, ROWS)
        numbers = image_ref[rows, full:]
        column = lax.broadcasted_iota(jnp.int32, (ROWS, 3 * groups), 1) % groups
        one_hot = (numbers[:, :1].astype(jnp.int32) == column).astype(jnp.bfloat16)
        tables = jnp.dot(one_hot, table_ref[...], preferred_element_type=jnp.float32)
        ctf = tables[:, :half]
        noise = tables[:, half:]
        limit = numbers[:, LIMIT_AT : LIMIT_AT + 1].astype(jnp.int32)
        position = lax.broadcasted_iota(jnp.int32, (ROWS, half), 1)
        freq_x = position >> int(math.log2(KY))
        freq_y = (position & (KY - 1)) - KY // 2
        weight = jnp.where(freq_x * freq_x + freq_y * freq_y < limit * limit, noise, 0.0)
        ctf_weight = weight * ctf
        real = image_ref[rows, :half]
        imag = image_ref[rows, half:full]
        norm = jnp.sum(weight * (real * real + imag * imag), axis=1, keepdims=True)
        real_ref[...] = ctf_weight * real
        imag_ref[...] = ctf_weight * imag
        quad_high, quad_low = split_halves(ctf_weight * ctf)
        quad_weight = jnp.concatenate([quad_high, quad_low], axis=0)
        quad = lax.dot_general(
            quad_weight, high_ref[...], NT, preferred_element_type=jnp.float32
        ) + lax.dot_general(quad_weight, low_ref[...], NT, preferred_element_type=jnp.float32)
        quad = quad[:ROWS] + quad[ROWS:]

        numbers_int = numbers.astype(jnp.int32)
        step_cos, step_sin = sin_cos(numbers_int * (LANES // KY))
        phases = []
        for start in range(0, shifts, 2):
            members = range(start, min(start + 2, shifts))

            def stacked(value, base):
                return jnp.concatenate(
                    [value[:, base + shift : base + shift + 1] for shift in members], axis=0
                )

            height = len(members) * ROWS
            lane = lax.broadcasted_iota(jnp.int32, (height, LANES), 1)
            turns = (lane >> int(math.log2(KY))) * stacked(numbers_int, X_AT) + (
                (lane & (KY - 1)) - KY // 2
            ) * stacked(numbers_int, Y_AT)
            cosine, sine = sin_cos(turns)
            turn_cos = stacked(step_cos, X_AT)
            turn_sin = stacked(step_sin, X_AT)
            cosine_before = cosine * turn_cos + sine * turn_sin
            sine_before = sine * turn_cos - cosine * turn_sin
            double = jnp.broadcast_to(2.0 * turn_cos, (height, LANES))
            phases.append((cosine, cosine_before, sine, sine_before, double))

        cross = jnp.zeros(cross_ref.shape, jnp.float32)
        for group in range(0, half, GROUP):
            for number, phase in enumerate(phases):
                cosine, cosine_before, sine, sine_before, double = phase
                height = double.shape[0]
                out_rows = pl.ds(first + 2 * number * ROWS, height)
                for start in range(group, group + GROUP, LANES):
                    at = pl.ds(start, LANES)
                    real = jnp.concatenate([real_ref[:, at]] * (height // ROWS), axis=0)
                    imag = jnp.concatenate([imag_ref[:, at]] * (height // ROWS), axis=0)
                    weighted_ref[out_rows, at] = (real * cosine + imag * sine).astype(
                        jnp.bfloat16
                    )
                    weighted_ref[out_rows, pl.ds(half + start, LANES)] = (
                        imag * cosine - real * sine
                    ).astype(jnp.bfloat16)
                    cosine, cosine_before = double * cosine - cosine_before, cosine
                    sine, sine_before = double * sine - sine_before, sine
                phases[number] = (cosine, cosine_before, sine, sine_before, double)
            for base in (group, half + group):
                at = pl.ds(base, GROUP)
                cross = cross + lax.dot_general(
                    weighted_ref[pl.ds(first, block_rows), at],
                    both_ref[:, at],
                    NT,
                    preferred_element_type=jnp.float32,
                )
        cross_ref[...] = cross
        base = norm + quad
        scores = [
            -(base - 2.0 * cross_ref[pl.ds(shift * ROWS, ROWS), :]) * scale
            for shift in range(shifts)
        ]
        top = jnp.max(functools.reduce(jnp.maximum, scores), axis=1, keepdims=True)
        exps = [jnp.exp(score - top) for score in scores]
        total = jnp.sum(functools.reduce(jnp.add, exps), axis=1, keepdims=True)
        for shift in range(shifts):
            square_ref[pl.ds(shift * ROWS, ROWS), :candidates] = exps[shift]
        turned = square_ref[...].T
        exps_ref[index + slot] = turned[: candidates // 2, :block_rows]
        exps_other_ref[index + slot] = turned[candidates // 2 : candidates, :block_rows]
        row = lax.broadcasted_iota(jnp.int32, (ROWS, LANES), 0)
        lane = lax.broadcasted_iota(jnp.int32, (ROWS, LANES), 1)
        half_at = chip // NEAR ^ slot if by_distance else 0
        here = (lane & (2 * ROWS - 1)) == row + half_at * ROWS
        line = jnp.sum(
            jnp.where(here, jnp.where(lane < LANES // 2, top, total), 0.0),
            axis=0,
            keepdims=True,
        )
        if has_earlier:
            line = line + earlier_stats_ref[0]
        for target in range(stats_ref.shape[0]):
            stats_ref[target, pl.ds(index, 1), :] = line
        return carry

    lax.fori_loop(0, rows_total // ROWS, block, 0)


def slice_kernel(scale, calls, by_distance, *refs):
    stats_ref, exps_own_ref, exps_other_ref = refs[:3]
    weighted_refs = (refs[3 : 3 + calls], refs[3 + calls : 3 + 2 * calls])
    out_hbm, best_hbm, log_hbm = refs[3 + 2 * calls : 6 + 2 * calls]
    best_ref, log_ref, posterior_ref, summed_ref, sems, number_sems = refs[6 + 2 * calls :]
    blocks, rows, block_rows = exps_own_ref.shape
    chips = stats_ref.shape[0]
    per_device = best_ref.shape[0]
    full = out_hbm.shape[1]
    index = lax.axis_index("blk")
    chip = index >> 1
    lane = lax.broadcasted_iota(jnp.int32, (1, LANES), 1)

    def combined(core, row):
        at = pl.ds(row, 1)
        lower = lane < LANES // 2
        lines = [stats_ref[source, core, at, :] for source in range(chips)]
        lines.append(stats_ref[chip, core, at, :])
        turned = [pltpu.roll(line, LANES // 2, 1) for line in lines]
        tops = [jnp.where(lower, one, two) for one, two in zip(lines, turned)]
        totals = [jnp.where(lower, two, one) for one, two in zip(lines, turned)]
        top = functools.reduce(jnp.maximum, tops)
        total = functools.reduce(
            jnp.add, [part * jnp.exp(high - top) for high, part in zip(tops[:-1], totals)]
        )
        return top, top + jnp.log(total), tops[-1]

    upper = (lane & ROWS) != 0
    for side, exps_ref in enumerate((exps_own_ref, exps_other_ref)):
        core = (index & 1) ^ side
        for block in range(blocks):
            if block == 0 or not by_distance:
                top, log_total, mine = combined(core, block)
                line = jnp.exp(mine - log_total)
                crossed = pltpu.roll(line, ROWS, 1)
            wanted = (chip // NEAR ^ block) != 0 if by_distance else False
            factor = jnp.where(upper == wanted, line, crossed)
            posterior_ref[side, block] = (exps_ref[block] * factor[:, :block_rows]).astype(
                jnp.bfloat16
            )

    width = 1024
    copies = []
    for number, start in enumerate(range(0, full, width)):
        at = pl.ds(start, width)
        products = []
        for side in range(2):
            for block in range(blocks):
                call, place = divmod(block, blocks // calls)
                products.append(
                    jnp.dot(
                        posterior_ref[side, block],
                        weighted_refs[side][call][pl.ds(place * block_rows, block_rows), at],
                        preferred_element_type=jnp.float32,
                    )
                )
        summed_ref[:, at] = functools.reduce(jnp.add, products) * scale
        copy = pltpu.make_async_copy(summed_ref.at[:, at], out_hbm.at[:, at], sems.at[number])
        copy.start()
        copies.append(copy)
        if number == 0:
            for row in range(per_device):
                particle = chip * per_device + row
                if by_distance:
                    top, log_total, mine = combined(index & 1, 0)
                    chosen = lane == particle
                else:
                    top, log_total, mine = combined(index & 1, particle // ROWS)
                    chosen = lane == particle % ROWS
                best_ref[row] = jnp.sum(jnp.where(chosen, jnp.exp(top - log_total), 0.0))
                log_ref[row] = jnp.sum(jnp.where(chosen, log_total, 0.0))
            copies.append(pltpu.make_async_copy(best_ref, best_hbm, number_sems.at[0]))
            copies.append(pltpu.make_async_copy(log_ref, log_hbm, number_sems.at[1]))
            copies[-2].start()
            copies[-1].start()
    for copy in copies:
        copy.wait()


def local(
    axis_size, projections, images, ctf_group, shift_offsets, shell_limit, ctf_table, noise_weight
):
    batch_count, orient_dev, full = projections.shape
    half = full // 2
    own_rows = batch_count * orient_dev
    candidates = 2 * own_rows
    per_device = images.shape[0]
    shifts = shift_offsets.shape[1]
    chips = axis_size // 2
    particles = chips * per_device
    blocks = particles // ROWS
    block_rows = shifts * ROWS
    megabytes = 12 + -(-2 * blocks * block_rows * full * 2 // 2**20)
    params = pltpu.CompilerParams(vmem_limit_bytes=megabytes * 2**20)

    def swap(value, mask):
        return lax.ppermute(value, "blk", [(i, i ^ mask) for i in range(axis_size)])

    numbers = pl.pallas_call(
        pack_kernel,
        out_shape=jax.ShapeDtypeStruct((1, per_device, LANES), jnp.bfloat16),
        in_specs=[HBM] * 3,
        out_specs=VMEM,
        scratch_shapes=[
            pltpu.SMEM((per_device,), jnp.int32),
            pltpu.SMEM((per_device,), jnp.int32),
            pltpu.SMEM((per_device, 2, shifts), jnp.int32),
            pltpu.SemaphoreType.DMA((3,)),
        ],
        compiler_params=pltpu.CompilerParams(vmem_limit_bytes=60 * 2**20),
        name="pack",
    )(ctf_group, shell_limit, shift_offsets.transpose(0, 2, 1))
    by_distance = chips == 2 * NEAR and per_device * NEAR == ROWS
    rows = images[None]
    if by_distance:
        received = swap(rows, 2)

    flat = projections.reshape(own_rows, full)
    other = swap(flat, 1)
    if by_distance:
        rows, numbers, other = lax.optimization_barrier((rows, numbers, other))
        received_numbers = swap(numbers, 2)
    groups = ctf_table.shape[0]
    both, high, low = pl.pallas_call(
        power_kernel,
        out_shape=(
            jax.ShapeDtypeStruct((candidates, full), jnp.bfloat16),
            jax.ShapeDtypeStruct((candidates, half), jnp.bfloat16),
            jax.ShapeDtypeStruct((candidates, half), jnp.bfloat16),
        ),
        in_specs=[VMEM] * 2,
        out_specs=(VMEM,) * 3,
        compiler_params=params,
        cost_estimate=pl.CostEstimate(
            flops=8 * candidates * full, bytes_accessed=4 * candidates * full, transcendentals=0
        ),
        name="power",
    )(flat, other)
    tables = pl.pallas_call(
        table_kernel,
        out_shape=jax.ShapeDtypeStruct((3 * groups, full), jnp.bfloat16),
        in_specs=[VMEM] * 2,
        out_specs=VMEM,
        compiler_params=params,
        cost_estimate=pl.CostEstimate(
            flops=6 * groups * full, bytes_accessed=10 * groups * full, transcendentals=0
        ),
        name="tables",
    )(ctf_table, noise_weight)
    if by_distance:
        pair = jnp.zeros((2, per_device, full + LANES), images.dtype)
        pair = lax.dynamic_update_slice(pair, rows, (0, 0, 0))
        pair = lax.dynamic_update_slice(pair, numbers, (0, 0, full))
        pair = lax.dynamic_update_slice(pair, received, (1, 0, 0))
        pair = lax.dynamic_update_slice(pair, received_numbers, (1, 0, full))
        pieces = [pair] + [swap(pair, mask) for mask in range(4, axis_size, 4)]
        parts = [(pieces[:2], ((0, 1), (2, 3))), (pieces[2:], ((4, 5), (6, 7)))]
    else:
        same_core = [[2 * c + core for c in range(chips)] for core in range(2)]
        gathered = lax.all_gather(
            jnp.concatenate([rows, numbers], axis=2), "blk", axis=0, tiled=True, axis_index_groups=same_core
        )
        parts = [([gathered], (tuple(range(chips)),))]

    all_weighted = []
    earlier = ()
    for pieces, sources in parts:
        last = len(all_weighted) == len(parts) - 1
        own_blocks = blocks // len(parts)
        seen = blocks if last else own_blocks
        weighted, *earlier = pl.pallas_call(
            functools.partial(score_kernel, sources, by_distance, shifts, bool(earlier)),
            out_shape=(
                jax.ShapeDtypeStruct((own_blocks * block_rows, full), jnp.bfloat16),
                jax.ShapeDtypeStruct((seen, own_rows, block_rows), jnp.float32),
                jax.ShapeDtypeStruct((seen, own_rows, block_rows), jnp.float32),
                jax.ShapeDtypeStruct(
                    (axis_size if last else 1, 1 if by_distance else blocks, LANES), jnp.float32
                ),
            ),
            in_specs=[VMEM] * (len(pieces) + 4 + len(earlier)),
            out_specs=(VMEM,) * 4,
            scratch_shapes=[
                pltpu.VMEM((own_blocks * ROWS, full + LANES), jnp.float32),
                pltpu.VMEM((ROWS, half), jnp.float32),
                pltpu.VMEM((ROWS, half), jnp.float32),
                pltpu.VMEM((block_rows, candidates), jnp.float32),
                pltpu.VMEM((-(-block_rows // LANES) * LANES, LANES), jnp.float32),
            ],
            compiler_params=params,
            cost_estimate=pl.CostEstimate(
                flops=2 * own_blocks * block_rows * full * (candidates + 8),
                bytes_accessed=2 * own_blocks * block_rows * full,
                transcendentals=0,
            ),
            name="scores",
        )(*pieces, both, high, low, tables, *earlier)
        all_weighted.append(weighted)
    exps, exps_other, stats = earlier

    exchanged = [swap(weighted, 1) for weighted in all_weighted]
    exps_in = swap(exps_other, 1)
    gathered = lax.all_to_all(stats, "blk", 0, 0)
    gathered = gathered.reshape((chips, 2) + gathered.shape[1:])

    slices, best_posterior, log_total = pl.pallas_call(
        functools.partial(
            slice_kernel, own_rows / per_device, len(all_weighted), by_distance
        ),
        out_shape=(
            jax.ShapeDtypeStruct((own_rows, full), jnp.float32),
            jax.ShapeDtypeStruct((per_device,), jnp.float32),
            jax.ShapeDtypeStruct((per_device,), jnp.float32),
        ),
        in_specs=[VMEM] * (3 + 2 * len(all_weighted)),
        out_specs=(HBM, HBM, HBM),
        scratch_shapes=[
            pltpu.SMEM((per_device,), jnp.float32),
            pltpu.SMEM((per_device,), jnp.float32),
            pltpu.VMEM((2, blocks, own_rows, block_rows), jnp.bfloat16),
            pltpu.VMEM((own_rows, full), jnp.float32),
            pltpu.SemaphoreType.DMA((full // 1024,)),
            pltpu.SemaphoreType.DMA((2,)),
        ],
        compiler_params=params,
        name="slices",
    )(gathered, exps, exps_in, *all_weighted, *exchanged)
    return (slices.reshape(batch_count, orient_dev, full), best_posterior, log_total)


def solution(mesh):
    in_specs = (
        P(None, ("groups", "blk"), None),
        P(("groups", "blk"), None),
        P(("groups", "blk")),
        P(("groups", "blk"), None, None),
        P(("groups", "blk")),
        P("groups", None),
        P("groups", None),
    )
    out_specs = (P(None, ("groups", "blk"), None), P(("groups", "blk")), P(("groups", "blk")))
    return jax.shard_map(
        functools.partial(local, mesh.shape["blk"]),
        mesh=mesh,
        in_specs=in_specs,
        out_specs=out_specs,
        check_vma=False,
    )
```

```python
import functools
import math

import jax
import jax.numpy as jnp
from jax import lax
from jax.experimental import pallas as pl
from jax.experimental.pallas import tpu as pltpu
from jax.sharding import PartitionSpec as P

KY = 64
IMG = 256
LANES = 128
ROWS = 8
NEAR = 4
GROUP = 1024
LIMIT_AT = 1
X_AT = 16
Y_AT = 48

VMEM = pl.BlockSpec(memory_space=pltpu.VMEM)
HBM = pl.BlockSpec(memory_space=pltpu.HBM)
NT = (((1,), (1,)), ((), ()))


def sin_cos(turns):
    quarter = IMG // 4
    wrapped = (turns + quarter // 2) & (IMG - 1)
    quadrant = wrapped >> int(math.log2(quarter))
    angle = (wrapped - quadrant * quarter - quarter // 2).astype(jnp.float32) * (
        2.0 * math.pi / IMG
    )
    square = angle * angle
    even = 1.0 + square * (
        -1.0 / 2 + square * (1.0 / 24 + square * (-1.0 / 720 + square * (1.0 / 40320)))
    )
    odd = angle * (
        1.0
        + square
        * (-1.0 / 6 + square * (1.0 / 120 + square * (-1.0 / 5040 + square * (1.0 / 362880))))
    )
    swapped = (quadrant & 1) == 1
    cosine = jnp.where(swapped, odd, even)
    sine = jnp.where(swapped, even, odd)
    cosine = jnp.where((quadrant == 1) | (quadrant == 2), -cosine, cosine)
    sine = jnp.where(quadrant >= 2, -sine, sine)
    return cosine, sine


def split_halves(value):
    high = value.astype(jnp.bfloat16)
    return high, (value - high.astype(jnp.float32)).astype(jnp.bfloat16)


def pack_kernel(group_hbm, limit_hbm, offsets_hbm, packed_ref, group, limit, offsets, sems):
    per_device, _, shifts = offsets_hbm.shape
    copies = [
        pltpu.make_async_copy(group_hbm, group, sems.at[0]),
        pltpu.make_async_copy(limit_hbm, limit, sems.at[1]),
        pltpu.make_async_copy(offsets_hbm, offsets, sems.at[2]),
    ]
    for copy in copies:
        copy.start()
    for copy in copies:
        copy.wait()
    row = lax.broadcasted_iota(jnp.int32, (per_device, LANES), 0)
    lane = lax.broadcasted_iota(jnp.int32, (per_device, LANES), 1)
    numbers = jnp.zeros((per_device, LANES), jnp.int32)
    for particle in range(per_device):
        line = jnp.zeros((per_device, LANES), jnp.int32)
        line = jnp.where(lane == 0, group[particle], line)
        line = jnp.where(lane == LIMIT_AT, limit[particle], line)
        for shift in range(shifts):
            line = jnp.where(lane == X_AT + shift, offsets[particle, 0, shift], line)
            line = jnp.where(lane == Y_AT + shift, offsets[particle, 1, shift], line)
        numbers = jnp.where(row == particle, line, numbers)
    packed_ref[0] = numbers.astype(jnp.float32).astype(jnp.bfloat16)


def split_thirds(value):
    high = value.astype(jnp.bfloat16)
    rest = value - high.astype(jnp.float32)
    middle = rest.astype(jnp.bfloat16)
    return high, middle, (rest - middle.astype(jnp.float32)).astype(jnp.bfloat16)


def power_kernel(own_ref, other_ref, both_ref, high_ref, low_ref):
    rows, full = own_ref.shape
    half = full // 2
    for place, ref in enumerate((own_ref, other_ref)):
        at = pl.ds(place * rows, rows)
        both_ref[at, :] = ref[...]
        real = ref[:, :half].astype(jnp.float32)
        imag = ref[:, half:].astype(jnp.float32)
        high, low = split_halves(real * real + imag * imag)
        high_ref[at, :] = high
        low_ref[at, :] = low


def table_kernel(ctf_ref, noise_ref, table_ref):
    groups, half = ctf_ref.shape
    for place, ref in enumerate((ctf_ref, noise_ref)):
        for third, part in enumerate(split_thirds(ref[...])):
            table_ref[pl.ds(third * groups, groups), pl.ds(place * half, half)] = part


def score_kernel(sources, by_distance, shifts, has_earlier, *refs):
    pieces = refs[: len(sources)]
    refs = refs[len(sources) :]
    both_ref, high_ref, low_ref, table_ref = refs[:4]
    refs = refs[4:]
    if has_earlier:
        earlier_own_ref, earlier_other_ref, earlier_stats_ref = refs[:3]
        refs = refs[3:]
    weighted_ref, exps_ref, *exps_other_refs, stats_ref = refs[:-5]
    image_ref, real_ref, imag_ref, cross_ref, square_ref = refs[-5:]
    full = both_ref.shape[1]
    half = full // 2
    groups = table_ref.shape[0] // 3
    candidates = both_ref.shape[0]
    rows_total = image_ref.shape[0]

    def put_exps(slot, values):
        for ref in exps_other_refs:
            ref[slot] = values
        if has_earlier:
            for third, part in enumerate(split_thirds(values)):
                at = pl.ds(full + (3 * slot + third) * LANES, values.shape[1])
                weighted_ref[pl.ds(0, values.shape[0]), at] = part

    per_device = pieces[0].shape[1]
    scale = 0.5 / math.sqrt(half)
    chip = lax.axis_index("blk") >> 1
    for piece, places in zip(pieces, sources):
        for row, place in enumerate(places):
            if by_distance:
                place = (chip ^ place) & (NEAR - 1)
            values = piece[row].astype(jnp.float32)
            for sub in range(per_device):
                image_ref[pl.ds(place * per_device + sub, 1), :] = values[sub : sub + 1]

    block_rows = shifts * ROWS
    slot = 1 if has_earlier else 0
    if has_earlier:
        exps_ref[0] = earlier_own_ref[0]
        put_exps(0, earlier_other_ref[0])

    def block(index, carry):
        rows = pl.ds(pl.multiple_of(index * ROWS, ROWS), ROWS)
        first = pl.multiple_of(index * block_rows, ROWS)
        numbers = image_ref[rows, full:]
        column = lax.broadcasted_iota(jnp.int32, (ROWS, 3 * groups), 1) % groups
        one_hot = (numbers[:, :1].astype(jnp.int32) == column).astype(jnp.bfloat16)
        tables = jnp.dot(one_hot, table_ref[...], preferred_element_type=jnp.float32)
        ctf = tables[:, :half]
        noise = tables[:, half:]
        limit = numbers[:, LIMIT_AT : LIMIT_AT + 1].astype(jnp.int32)
        position = lax.broadcasted_iota(jnp.int32, (ROWS, half), 1)
        freq_x = position >> int(math.log2(KY))
        freq_y = (position & (KY - 1)) - KY // 2
        weight = jnp.where(freq_x * freq_x + freq_y * freq_y < limit * limit, noise, 0.0)
        ctf_weight = weight * ctf
        real = image_ref[rows, :half]
        imag = image_ref[rows, half:full]
        norm = jnp.sum(weight * (real * real + imag * imag), axis=1, keepdims=True)
        real_ref[...] = ctf_weight * real
        imag_ref[...] = ctf_weight * imag
        quad_high, quad_low = split_halves(ctf_weight * ctf)
        quad_weight = jnp.concatenate([quad_high, quad_low], axis=0)
        quad = lax.dot_general(
            quad_weight, high_ref[...], NT, preferred_element_type=jnp.float32
        ) + lax.dot_general(quad_weight, low_ref[...], NT, preferred_element_type=jnp.float32)
        quad = quad[:ROWS] + quad[ROWS:]

        numbers_int = numbers.astype(jnp.int32)
        step_cos, step_sin = sin_cos(numbers_int * (LANES // KY))
        phases = []
        for start in range(0, shifts, 2):
            members = range(start, min(start + 2, shifts))

            def stacked(value, base):
                return jnp.concatenate(
                    [value[:, base + shift : base + shift + 1] for shift in members], axis=0
                )

            height = len(members) * ROWS
            lane = lax.broadcasted_iota(jnp.int32, (height, LANES), 1)
            turns = (lane >> int(math.log2(KY))) * stacked(numbers_int, X_AT) + (
                (lane & (KY - 1)) - KY // 2
            ) * stacked(numbers_int, Y_AT)
            cosine, sine = sin_cos(turns)
            turn_cos = stacked(step_cos, X_AT)
            turn_sin = stacked(step_sin, X_AT)
            cosine_before = cosine * turn_cos + sine * turn_sin
            sine_before = sine * turn_cos - cosine * turn_sin
            double = jnp.broadcast_to(2.0 * turn_cos, (height, LANES))
            phases.append((cosine, cosine_before, sine, sine_before, double))

        cross = jnp.zeros(cross_ref.shape, jnp.float32)
        for group in range(0, half, GROUP):
            for number, phase in enumerate(phases):
                cosine, cosine_before, sine, sine_before, double = phase
                height = double.shape[0]
                out_rows = pl.ds(first + 2 * number * ROWS, height)
                for start in range(group, group + GROUP, LANES):
                    at = pl.ds(start, LANES)
                    real = jnp.concatenate([real_ref[:, at]] * (height // ROWS), axis=0)
                    imag = jnp.concatenate([imag_ref[:, at]] * (height // ROWS), axis=0)
                    weighted_ref[out_rows, at] = (real * cosine + imag * sine).astype(
                        jnp.bfloat16
                    )
                    weighted_ref[out_rows, pl.ds(half + start, LANES)] = (
                        imag * cosine - real * sine
                    ).astype(jnp.bfloat16)
                    cosine, cosine_before = double * cosine - cosine_before, cosine
                    sine, sine_before = double * sine - sine_before, sine
                phases[number] = (cosine, cosine_before, sine, sine_before, double)
            for base in (group, half + group):
                at = pl.ds(base, GROUP)
                cross = cross + lax.dot_general(
                    weighted_ref[pl.ds(first, block_rows), at],
                    both_ref[:, at],
                    NT,
                    preferred_element_type=jnp.float32,
                )
        cross_ref[...] = cross
        base = norm + quad
        scores = [
            -(base - 2.0 * cross_ref[pl.ds(shift * ROWS, ROWS), :]) * scale
            for shift in range(shifts)
        ]
        top = jnp.max(functools.reduce(jnp.maximum, scores), axis=1, keepdims=True)
        exps = [jnp.exp(score - top) for score in scores]
        total = jnp.sum(functools.reduce(jnp.add, exps), axis=1, keepdims=True)
        for shift in range(shifts):
            square_ref[pl.ds(shift * ROWS, ROWS), :candidates] = exps[shift]
        turned = square_ref[...].T
        exps_ref[index + slot] = turned[: candidates // 2, :block_rows]
        put_exps(index + slot, turned[candidates // 2 : candidates, :block_rows])
        row = lax.broadcasted_iota(jnp.int32, (ROWS, LANES), 0)
        lane = lax.broadcasted_iota(jnp.int32, (ROWS, LANES), 1)
        half_at = chip // NEAR ^ slot if by_distance else 0
        here = (lane & (2 * ROWS - 1)) == row + half_at * ROWS
        line = jnp.sum(
            jnp.where(here, jnp.where(lane < LANES // 2, top, total), 0.0),
            axis=0,
            keepdims=True,
        )
        if has_earlier:
            line = line + earlier_stats_ref[0]
        for target in range(stats_ref.shape[0]):
            stats_ref[target, pl.ds(index, 1), :] = line
        return carry

    lax.fori_loop(0, rows_total // ROWS, block, 0)


def slice_kernel(scale, calls, by_distance, *refs):
    stats_ref, exps_own_ref = refs[:2]
    refs = refs[2:]
    if not by_distance:
        exps_other_ref, *refs = refs
    weighted_refs = (refs[:calls], refs[calls : 2 * calls])
    out_hbm, best_hbm, log_hbm = refs[2 * calls : 2 * calls + 3]
    best_ref, log_ref, posterior_ref, summed_ref, sems, number_sems = refs[2 * calls + 3 :]
    blocks, rows, block_rows = exps_own_ref.shape
    chips = stats_ref.shape[0]
    per_device = best_ref.shape[0]
    full = out_hbm.shape[1]
    index = lax.axis_index("blk")
    chip = index >> 1
    lane = lax.broadcasted_iota(jnp.int32, (1, LANES), 1)

    def combined(core, row):
        at = pl.ds(row, 1)
        lower = lane < LANES // 2
        lines = [stats_ref[source, core, at, :] for source in range(chips)]
        lines.append(stats_ref[chip, core, at, :])
        turned = [pltpu.roll(line, LANES // 2, 1) for line in lines]
        tops = [jnp.where(lower, one, two) for one, two in zip(lines, turned)]
        totals = [jnp.where(lower, two, one) for one, two in zip(lines, turned)]
        top = functools.reduce(jnp.maximum, tops)
        total = functools.reduce(
            jnp.add, [part * jnp.exp(high - top) for high, part in zip(tops[:-1], totals)]
        )
        return top, top + jnp.log(total), tops[-1]

    upper = (lane & ROWS) != 0
    def exps_of(side, block):
        if side == 0:
            return exps_own_ref[block]
        if not by_distance:
            return exps_other_ref[block]
        parts = [
            weighted_refs[1][-1][
                pl.ds(0, rows), pl.ds(full + (3 * block + third) * LANES, block_rows)
            ].astype(jnp.float32)
            for third in range(3)
        ]
        return parts[0] + (parts[1] + parts[2])

    for side in range(2):
        core = (index & 1) ^ side
        for block in range(blocks):
            if block == 0 or not by_distance:
                top, log_total, mine = combined(core, block)
                line = jnp.exp(mine - log_total)
                crossed = pltpu.roll(line, ROWS, 1)
            wanted = (chip // NEAR ^ block) != 0 if by_distance else False
            factor = jnp.where(upper == wanted, line, crossed)
            posterior_ref[side, block] = (exps_of(side, block) * factor[:, :block_rows]).astype(
                jnp.bfloat16
            )

    width = 1024
    copies = []
    for number, start in enumerate(range(0, full, width)):
        at = pl.ds(start, width)
        products = []
        for side in range(2):
            for block in range(blocks):
                call, place = divmod(block, blocks // calls)
                products.append(
                    jnp.dot(
                        posterior_ref[side, block],
                        weighted_refs[side][call][pl.ds(place * block_rows, block_rows), at],
                        preferred_element_type=jnp.float32,
                    )
                )
        summed_ref[:, at] = functools.reduce(jnp.add, products) * scale
        copy = pltpu.make_async_copy(summed_ref.at[:, at], out_hbm.at[:, at], sems.at[number])
        copy.start()
        copies.append(copy)
        if number == 0:
            for row in range(per_device):
                particle = chip * per_device + row
                if by_distance:
                    top, log_total, mine = combined(index & 1, 0)
                    chosen = lane == particle
                else:
                    top, log_total, mine = combined(index & 1, particle // ROWS)
                    chosen = lane == particle % ROWS
                best_ref[row] = jnp.sum(jnp.where(chosen, jnp.exp(top - log_total), 0.0))
                log_ref[row] = jnp.sum(jnp.where(chosen, log_total, 0.0))
            copies.append(pltpu.make_async_copy(best_ref, best_hbm, number_sems.at[0]))
            copies.append(pltpu.make_async_copy(log_ref, log_hbm, number_sems.at[1]))
            copies[-2].start()
            copies[-1].start()
    for copy in copies:
        copy.wait()


def local(
    axis_size, projections, images, ctf_group, shift_offsets, shell_limit, ctf_table, noise_weight
):
    batch_count, orient_dev, full = projections.shape
    half = full // 2
    own_rows = batch_count * orient_dev
    candidates = 2 * own_rows
    per_device = images.shape[0]
    shifts = shift_offsets.shape[1]
    chips = axis_size // 2
    particles = chips * per_device
    blocks = particles // ROWS
    block_rows = shifts * ROWS
    megabytes = 12 + -(-2 * blocks * block_rows * full * 2 // 2**20)
    params = pltpu.CompilerParams(vmem_limit_bytes=megabytes * 2**20)

    def swap(value, mask):
        return lax.ppermute(value, "blk", [(i, i ^ mask) for i in range(axis_size)])

    numbers = pl.pallas_call(
        pack_kernel,
        out_shape=jax.ShapeDtypeStruct((1, per_device, LANES), jnp.bfloat16),
        in_specs=[HBM] * 3,
        out_specs=VMEM,
        scratch_shapes=[
            pltpu.SMEM((per_device,), jnp.int32),
            pltpu.SMEM((per_device,), jnp.int32),
            pltpu.SMEM((per_device, 2, shifts), jnp.int32),
            pltpu.SemaphoreType.DMA((3,)),
        ],
        compiler_params=pltpu.CompilerParams(vmem_limit_bytes=60 * 2**20),
        name="pack",
    )(ctf_group, shell_limit, shift_offsets.transpose(0, 2, 1))
    by_distance = chips == 2 * NEAR and per_device * NEAR == ROWS
    rows = images[None]
    if by_distance:
        received = swap(rows, 2)

    flat = projections.reshape(own_rows, full)
    other = swap(flat, 1)
    if by_distance:
        rows, numbers = lax.optimization_barrier((rows, numbers))
        received_numbers = swap(numbers, 2)
    groups = ctf_table.shape[0]
    both, high, low = pl.pallas_call(
        power_kernel,
        out_shape=(
            jax.ShapeDtypeStruct((candidates, full), jnp.bfloat16),
            jax.ShapeDtypeStruct((candidates, half), jnp.bfloat16),
            jax.ShapeDtypeStruct((candidates, half), jnp.bfloat16),
        ),
        in_specs=[VMEM] * 2,
        out_specs=(VMEM,) * 3,
        compiler_params=params,
        cost_estimate=pl.CostEstimate(
            flops=8 * candidates * full, bytes_accessed=4 * candidates * full, transcendentals=0
        ),
        name="power",
    )(flat, other)
    tables = pl.pallas_call(
        table_kernel,
        out_shape=jax.ShapeDtypeStruct((3 * groups, full), jnp.bfloat16),
        in_specs=[VMEM] * 2,
        out_specs=VMEM,
        compiler_params=params,
        cost_estimate=pl.CostEstimate(
            flops=6 * groups * full, bytes_accessed=10 * groups * full, transcendentals=0
        ),
        name="tables",
    )(ctf_table, noise_weight)
    if by_distance:
        pair = jnp.zeros((2, per_device, full + LANES), images.dtype)
        pair = lax.dynamic_update_slice(pair, rows, (0, 0, 0))
        pair = lax.dynamic_update_slice(pair, numbers, (0, 0, full))
        pair = lax.dynamic_update_slice(pair, received, (1, 0, 0))
        pair = lax.dynamic_update_slice(pair, received_numbers, (1, 0, full))
        pieces = [pair] + [swap(pair, mask) for mask in range(4, axis_size, 4)]
        parts = [(pieces[:2], ((0, 1), (2, 3))), (pieces[2:], ((4, 5), (6, 7)))]
    else:
        same_core = [[2 * c + core for c in range(chips)] for core in range(2)]
        gathered = lax.all_gather(
            jnp.concatenate([rows, numbers], axis=2), "blk", axis=0, tiled=True, axis_index_groups=same_core
        )
        parts = [([gathered], (tuple(range(chips)),))]

    all_weighted = []
    earlier = ()
    for pieces, sources in parts:
        last = len(all_weighted) == len(parts) - 1
        own_blocks = blocks // len(parts)
        seen = blocks if last else own_blocks
        exps_shape = jax.ShapeDtypeStruct((seen, own_rows, block_rows), jnp.float32)
        weighted, *earlier = pl.pallas_call(
            functools.partial(score_kernel, sources, by_distance, shifts, bool(earlier)),
            out_shape=(
                jax.ShapeDtypeStruct(
                    (own_blocks * block_rows, full + (3 * blocks * LANES if earlier else 0)),
                    jnp.bfloat16,
                ),
                *([exps_shape] if earlier else [exps_shape] * 2),
                jax.ShapeDtypeStruct(
                    (axis_size if last else 1, 1 if by_distance else blocks, LANES), jnp.float32
                ),
            ),
            in_specs=[VMEM] * (len(pieces) + 4 + len(earlier)),
            out_specs=(VMEM,) * (3 if earlier else 4),
            scratch_shapes=[
                pltpu.VMEM((own_blocks * ROWS, full + LANES), jnp.float32),
                pltpu.VMEM((ROWS, half), jnp.float32),
                pltpu.VMEM((ROWS, half), jnp.float32),
                pltpu.VMEM((block_rows, candidates), jnp.float32),
                pltpu.VMEM((-(-block_rows // LANES) * LANES, LANES), jnp.float32),
            ],
            compiler_params=params,
            cost_estimate=pl.CostEstimate(
                flops=2 * own_blocks * block_rows * full * (candidates + 8),
                bytes_accessed=2 * own_blocks * block_rows * full,
                transcendentals=0,
            ),
            name="scores",
        )(*pieces, both, high, low, tables, *earlier)
        all_weighted.append(weighted)
    exps, *exps_other, stats = earlier

    exchanged = [swap(weighted, 1) for weighted in all_weighted]
    exps_in = [swap(part, 1) for part in exps_other]
    gathered = lax.all_to_all(stats, "blk", 0, 0)
    gathered = gathered.reshape((chips, 2) + gathered.shape[1:])

    slices, best_posterior, log_total = pl.pallas_call(
        functools.partial(
            slice_kernel, own_rows / per_device, len(all_weighted), by_distance
        ),
        out_shape=(
            jax.ShapeDtypeStruct((own_rows, full), jnp.float32),
            jax.ShapeDtypeStruct((per_device,), jnp.float32),
            jax.ShapeDtypeStruct((per_device,), jnp.float32),
        ),
        in_specs=[VMEM] * (2 + len(exps_in) + 2 * len(all_weighted)),
        out_specs=(HBM, HBM, HBM),
        scratch_shapes=[
            pltpu.SMEM((per_device,), jnp.float32),
            pltpu.SMEM((per_device,), jnp.float32),
            pltpu.VMEM((2, blocks, own_rows, block_rows), jnp.bfloat16),
            pltpu.VMEM((own_rows, full), jnp.float32),
            pltpu.SemaphoreType.DMA((full // 1024,)),
            pltpu.SemaphoreType.DMA((2,)),
        ],
        compiler_params=params,
        name="slices",
    )(gathered, exps, *exps_in, *all_weighted, *exchanged)
    return (slices.reshape(batch_count, orient_dev, full), best_posterior, log_total)


def solution(mesh):
    in_specs = (
        P(None, ("groups", "blk"), None),
        P(("groups", "blk"), None),
        P(("groups", "blk")),
        P(("groups", "blk"), None, None),
        P(("groups", "blk")),
        P("groups", None),
        P("groups", None),
    )
    out_specs = (P(None, ("groups", "blk"), None), P(("groups", "blk")), P(("groups", "blk")))
    return jax.shard_map(
        functools.partial(local, mesh.shape["blk"]),
        mesh=mesh,
        in_specs=in_specs,
        out_specs=out_specs,
        check_vma=False,
    )
```

```python
import functools
import math

import jax
import jax.numpy as jnp
from jax import lax
from jax.experimental import pallas as pl
from jax.experimental.pallas import tpu as pltpu
from jax.sharding import PartitionSpec as P

KY = 64
IMG = 256
LANES = 128
ROWS = 8
NEAR = 4
GROUP = 1024
LIMIT_AT = 1
X_AT = 16
Y_AT = 48

VMEM = pl.BlockSpec(memory_space=pltpu.VMEM)
HBM = pl.BlockSpec(memory_space=pltpu.HBM)
NT = (((1,), (1,)), ((), ()))


def sin_cos(turns):
    quarter = IMG // 4
    wrapped = (turns + quarter // 2) & (IMG - 1)
    quadrant = wrapped >> int(math.log2(quarter))
    angle = (wrapped - quadrant * quarter - quarter // 2).astype(jnp.float32) * (
        2.0 * math.pi / IMG
    )
    square = angle * angle
    even = 1.0 + square * (
        -1.0 / 2 + square * (1.0 / 24 + square * (-1.0 / 720 + square * (1.0 / 40320)))
    )
    odd = angle * (
        1.0
        + square
        * (-1.0 / 6 + square * (1.0 / 120 + square * (-1.0 / 5040 + square * (1.0 / 362880))))
    )
    swapped = (quadrant & 1) == 1
    cosine = jnp.where(swapped, odd, even)
    sine = jnp.where(swapped, even, odd)
    cosine = jnp.where((quadrant == 1) | (quadrant == 2), -cosine, cosine)
    sine = jnp.where(quadrant >= 2, -sine, sine)
    return cosine, sine


def split_halves(value):
    high = value.astype(jnp.bfloat16)
    return high, (value - high.astype(jnp.float32)).astype(jnp.bfloat16)


def pack_kernel(group_hbm, limit_hbm, offsets_hbm, packed_ref, group, limit, offsets, sems):
    per_device, _, shifts = offsets_hbm.shape
    copies = [
        pltpu.make_async_copy(group_hbm, group, sems.at[0]),
        pltpu.make_async_copy(limit_hbm, limit, sems.at[1]),
        pltpu.make_async_copy(offsets_hbm, offsets, sems.at[2]),
    ]
    for copy in copies:
        copy.start()
    for copy in copies:
        copy.wait()
    row = lax.broadcasted_iota(jnp.int32, (per_device, LANES), 0)
    lane = lax.broadcasted_iota(jnp.int32, (per_device, LANES), 1)
    numbers = jnp.zeros((per_device, LANES), jnp.int32)
    for particle in range(per_device):
        line = jnp.zeros((per_device, LANES), jnp.int32)
        line = jnp.where(lane == 0, group[particle], line)
        line = jnp.where(lane == LIMIT_AT, limit[particle], line)
        for shift in range(shifts):
            line = jnp.where(lane == X_AT + shift, offsets[particle, 0, shift], line)
            line = jnp.where(lane == Y_AT + shift, offsets[particle, 1, shift], line)
        numbers = jnp.where(row == particle, line, numbers)
    packed_ref[0] = numbers.astype(jnp.float32).astype(jnp.bfloat16)


def split_thirds(value):
    high = value.astype(jnp.bfloat16)
    rest = value - high.astype(jnp.float32)
    middle = rest.astype(jnp.bfloat16)
    return high, middle, (rest - middle.astype(jnp.float32)).astype(jnp.bfloat16)


def power_kernel(own_ref, other_ref, both_ref, high_ref, low_ref):
    rows, full = own_ref.shape
    half = full // 2
    for place, ref in enumerate((own_ref, other_ref)):
        at = pl.ds(place * rows, rows)
        both_ref[at, :] = ref[...]
        real = ref[:, :half].astype(jnp.float32)
        imag = ref[:, half:].astype(jnp.float32)
        high, low = split_halves(real * real + imag * imag)
        high_ref[at, :] = high
        low_ref[at, :] = low


def table_kernel(ctf_ref, noise_ref, table_ref):
    groups, half = ctf_ref.shape
    for place, ref in enumerate((ctf_ref, noise_ref)):
        for third, part in enumerate(split_thirds(ref[...])):
            table_ref[pl.ds(third * groups, groups), pl.ds(place * half, half)] = part


def score_kernel(sources, by_distance, shifts, has_earlier, *refs):
    pieces = refs[: len(sources)]
    refs = refs[len(sources) :]
    both_ref, high_ref, low_ref, table_ref = refs[:4]
    refs = refs[4:]
    if has_earlier:
        earlier_own_ref, earlier_other_ref, earlier_stats_ref = refs[:3]
        refs = refs[3:]
    weighted_ref, exps_ref, exps_other_ref, stats_ref = refs[:4]
    image_ref, real_ref, imag_ref, cross_ref, square_ref = refs[4:]
    full = both_ref.shape[1]
    half = full // 2
    groups = table_ref.shape[0] // 3
    candidates = both_ref.shape[0]
    rows_total = image_ref.shape[0]
    per_device = pieces[0].shape[1]
    scale = 0.5 / math.sqrt(half)
    chip = lax.axis_index("blk") >> 1
    for piece, places in zip(pieces, sources):
        for row, place in enumerate(places):
            if by_distance:
                place = (chip ^ place) & (NEAR - 1)
            values = piece[row].astype(jnp.float32)
            for sub in range(per_device):
                image_ref[pl.ds(place * per_device + sub, 1), :] = values[sub : sub + 1]

    block_rows = shifts * ROWS
    slot = 1 if has_earlier else 0
    if has_earlier:
        exps_ref[0] = earlier_own_ref[0]
        exps_other_ref[0] = earlier_other_ref[0]

    def block(index, carry):
        rows = pl.ds(pl.multiple_of(index * ROWS, ROWS), ROWS)
        first = pl.multiple_of(index * block_rows, ROWS)
        numbers = image_ref[rows, full:]
        column = lax.broadcasted_iota(jnp.int32, (ROWS, 3 * groups), 1) % groups
        one_hot = (numbers[:, :1].astype(jnp.int32) == column).astype(jnp.bfloat16)
        tables = jnp.dot(one_hot, table_ref[...], preferred_element_type=jnp.float32)
        ctf = tables[:, :half]
        noise = tables[:, half:]
        limit = numbers[:, LIMIT_AT : LIMIT_AT + 1].astype(jnp.int32)
        position = lax.broadcasted_iota(jnp.int32, (ROWS, half), 1)
        freq_x = position >> int(math.log2(KY))
        freq_y = (position & (KY - 1)) - KY // 2
        weight = jnp.where(freq_x * freq_x + freq_y * freq_y < limit * limit, noise, 0.0)
        ctf_weight = weight * ctf
        real = image_ref[rows, :half]
        imag = image_ref[rows, half:full]
        norm = jnp.sum(weight * (real * real + imag * imag), axis=1, keepdims=True)
        real_ref[...] = ctf_weight * real
        imag_ref[...] = ctf_weight * imag
        quad_high, quad_low = split_halves(ctf_weight * ctf)
        quad_weight = jnp.concatenate([quad_high, quad_low], axis=0)
        quad = lax.dot_general(
            quad_weight, high_ref[...], NT, preferred_element_type=jnp.float32
        ) + lax.dot_general(quad_weight, low_ref[...], NT, preferred_element_type=jnp.float32)
        quad = quad[:ROWS] + quad[ROWS:]

        numbers_int = numbers.astype(jnp.int32)
        step_cos, step_sin = sin_cos(numbers_int * (LANES // KY))
        phases = []
        for start in range(0, shifts, 2):
            members = range(start, min(start + 2, shifts))

            def stacked(value, base):
                return jnp.concatenate(
                    [value[:, base + shift : base + shift + 1] for shift in members], axis=0
                )

            height = len(members) * ROWS
            lane = lax.broadcasted_iota(jnp.int32, (height, LANES), 1)
            turns = (lane >> int(math.log2(KY))) * stacked(numbers_int, X_AT) + (
                (lane & (KY - 1)) - KY // 2
            ) * stacked(numbers_int, Y_AT)
            cosine, sine = sin_cos(turns)
            turn_cos = stacked(step_cos, X_AT)
            turn_sin = stacked(step_sin, X_AT)
            cosine_before = cosine * turn_cos + sine * turn_sin
            sine_before = sine * turn_cos - cosine * turn_sin
            double = jnp.broadcast_to(2.0 * turn_cos, (height, LANES))
            phases.append((cosine, cosine_before, sine, sine_before, double))

        cross = jnp.zeros(cross_ref.shape, jnp.float32)
        for group in range(0, half, GROUP):
            for number, phase in enumerate(phases):
                cosine, cosine_before, sine, sine_before, double = phase
                height = double.shape[0]
                out_rows = pl.ds(first + 2 * number * ROWS, height)
                for start in range(group, group + GROUP, LANES):
                    at = pl.ds(start, LANES)
                    real = jnp.concatenate([real_ref[:, at]] * (height // ROWS), axis=0)
                    imag = jnp.concatenate([imag_ref[:, at]] * (height // ROWS), axis=0)
                    weighted_ref[out_rows, at] = (real * cosine + imag * sine).astype(
                        jnp.bfloat16
                    )
                    weighted_ref[out_rows, pl.ds(half + start, LANES)] = (
                        imag * cosine - real * sine
                    ).astype(jnp.bfloat16)
                    cosine, cosine_before = double * cosine - cosine_before, cosine
                    sine, sine_before = double * sine - sine_before, sine
                phases[number] = (cosine, cosine_before, sine, sine_before, double)
            for base in (group, half + group):
                at = pl.ds(base, GROUP)
                cross = cross + lax.dot_general(
                    weighted_ref[pl.ds(first, block_rows), at],
                    both_ref[:, at],
                    NT,
                    preferred_element_type=jnp.float32,
                )
        cross_ref[...] = cross
        base = norm + quad
        scores = [
            -(base - 2.0 * cross_ref[pl.ds(shift * ROWS, ROWS), :]) * scale
            for shift in range(shifts)
        ]
        top = jnp.max(functools.reduce(jnp.maximum, scores), axis=1, keepdims=True)
        exps = [jnp.exp(score - top) for score in scores]
        total = jnp.sum(functools.reduce(jnp.add, exps), axis=1, keepdims=True)
        for shift in range(shifts):
            square_ref[pl.ds(shift * ROWS, ROWS), :candidates] = exps[shift]
        turned = square_ref[...].T
        exps_ref[index + slot] = turned[: candidates // 2, :block_rows]
        exps_other_ref[index + slot] = turned[candidates // 2 : candidates, :block_rows]
        row = lax.broadcasted_iota(jnp.int32, (ROWS, LANES), 0)
        lane = lax.broadcasted_iota(jnp.int32, (ROWS, LANES), 1)
        half_at = chip // NEAR ^ slot if by_distance else 0
        here = (lane & (2 * ROWS - 1)) == row + half_at * ROWS
        line = jnp.sum(
            jnp.where(here, jnp.where(lane < LANES // 2, top, total), 0.0),
            axis=0,
            keepdims=True,
        )
        if has_earlier:
            line = line + earlier_stats_ref[0]
        for target in range(stats_ref.shape[0]):
            stats_ref[target, pl.ds(index, 1), :] = line
        return carry

    lax.fori_loop(0, rows_total // ROWS, block, 0)


def slice_kernel(scale, calls, by_distance, *refs):
    stats_ref, exps_own_ref, exps_other_ref = refs[:3]
    weighted_refs = (refs[3 : 3 + calls], refs[3 + calls : 3 + 2 * calls])
    out_hbm, best_hbm, log_hbm = refs[3 + 2 * calls : 6 + 2 * calls]
    best_ref, log_ref, posterior_ref, summed_ref, sems, number_sems = refs[6 + 2 * calls :]
    blocks, rows, block_rows = exps_own_ref.shape
    chips = stats_ref.shape[0]
    per_device = best_ref.shape[0]
    full = out_hbm.shape[1]
    index = lax.axis_index("blk")
    chip = index >> 1
    lane = lax.broadcasted_iota(jnp.int32, (1, LANES), 1)

    def combined(core, row):
        at = pl.ds(row, 1)
        lower = lane < LANES // 2
        lines = [stats_ref[source, core, at, :] for source in range(chips)]
        lines.append(stats_ref[chip, core, at, :])
        turned = [pltpu.roll(line, LANES // 2, 1) for line in lines]
        tops = [jnp.where(lower, one, two) for one, two in zip(lines, turned)]
        totals = [jnp.where(lower, two, one) for one, two in zip(lines, turned)]
        top = functools.reduce(jnp.maximum, tops)
        total = functools.reduce(
            jnp.add, [part * jnp.exp(high - top) for high, part in zip(tops[:-1], totals)]
        )
        return top, top + jnp.log(total), tops[-1]

    upper = (lane & ROWS) != 0
    for side, exps_ref in enumerate((exps_own_ref, exps_other_ref)):
        core = (index & 1) ^ side
        for block in range(blocks):
            if block == 0 or not by_distance:
                top, log_total, mine = combined(core, block)
                line = jnp.exp(mine - log_total)
                crossed = pltpu.roll(line, ROWS, 1)
            wanted = (chip // NEAR ^ block) != 0 if by_distance else False
            factor = jnp.where(upper == wanted, line, crossed)
            posterior_ref[side, block] = (exps_ref[block] * factor[:, :block_rows]).astype(
                jnp.bfloat16
            )

    width = 1024
    copies = []
    for number, start in enumerate(range(0, full, width)):
        at = pl.ds(start, width)
        products = []
        for side in range(2):
            for block in range(blocks):
                call, place = divmod(block, blocks // calls)
                products.append(
                    jnp.dot(
                        posterior_ref[side, block],
                        weighted_refs[side][call][pl.ds(place * block_rows, block_rows), at],
                        preferred_element_type=jnp.float32,
                    )
                )
        summed_ref[:, at] = functools.reduce(jnp.add, products) * scale
        copy = pltpu.make_async_copy(summed_ref.at[:, at], out_hbm.at[:, at], sems.at[number])
        copy.start()
        copies.append(copy)
        if number == 0:
            for row in range(per_device):
                particle = chip * per_device + row
                if by_distance:
                    top, log_total, mine = combined(index & 1, 0)
                    chosen = lane == particle
                else:
                    top, log_total, mine = combined(index & 1, particle // ROWS)
                    chosen = lane == particle % ROWS
                best_ref[row] = jnp.sum(jnp.where(chosen, jnp.exp(top - log_total), 0.0))
                log_ref[row] = jnp.sum(jnp.where(chosen, log_total, 0.0))
            copies.append(pltpu.make_async_copy(best_ref, best_hbm, number_sems.at[0]))
            copies.append(pltpu.make_async_copy(log_ref, log_hbm, number_sems.at[1]))
            copies[-2].start()
            copies[-1].start()
    for copy in copies:
        copy.wait()


def local(
    axis_size, projections, images, ctf_group, shift_offsets, shell_limit, ctf_table, noise_weight
):
    batch_count, orient_dev, full = projections.shape
    half = full // 2
    own_rows = batch_count * orient_dev
    candidates = 2 * own_rows
    per_device = images.shape[0]
    shifts = shift_offsets.shape[1]
    chips = axis_size // 2
    particles = chips * per_device
    blocks = particles // ROWS
    block_rows = shifts * ROWS
    megabytes = 12 + -(-2 * blocks * block_rows * full * 2 // 2**20)
    params = pltpu.CompilerParams(vmem_limit_bytes=megabytes * 2**20)

    def swap(value, mask):
        return lax.ppermute(value, "blk", [(i, i ^ mask) for i in range(axis_size)])

    numbers = pl.pallas_call(
        pack_kernel,
        out_shape=jax.ShapeDtypeStruct((1, per_device, LANES), jnp.bfloat16),
        in_specs=[HBM] * 3,
        out_specs=VMEM,
        scratch_shapes=[
            pltpu.SMEM((per_device,), jnp.int32),
            pltpu.SMEM((per_device,), jnp.int32),
            pltpu.SMEM((per_device, 2, shifts), jnp.int32),
            pltpu.SemaphoreType.DMA((3,)),
        ],
        compiler_params=pltpu.CompilerParams(vmem_limit_bytes=60 * 2**20),
        name="pack",
    )(ctf_group, shell_limit, shift_offsets.transpose(0, 2, 1))
    by_distance = chips == 2 * NEAR and per_device * NEAR == ROWS
    rows = images[None]
    if by_distance:
        received = swap(rows, 2)

    flat = projections.reshape(own_rows, full)
    other = swap(flat, 1)
    if by_distance:
        rows, numbers = lax.optimization_barrier((rows, numbers))
        received_numbers = swap(numbers, 2)
    groups = ctf_table.shape[0]
    both, high, low = pl.pallas_call(
        power_kernel,
        out_shape=(
            jax.ShapeDtypeStruct((candidates, full), jnp.bfloat16),
            jax.ShapeDtypeStruct((candidates, half), jnp.bfloat16),
            jax.ShapeDtypeStruct((candidates, half), jnp.bfloat16),
        ),
        in_specs=[VMEM] * 2,
        out_specs=(VMEM,) * 3,
        compiler_params=params,
        cost_estimate=pl.CostEstimate(
            flops=8 * candidates * full, bytes_accessed=4 * candidates * full, transcendentals=0
        ),
        name="power",
    )(flat, other)
    tables = pl.pallas_call(
        table_kernel,
        out_shape=jax.ShapeDtypeStruct((3 * groups, full), jnp.bfloat16),
        in_specs=[VMEM] * 2,
        out_specs=VMEM,
        compiler_params=params,
        cost_estimate=pl.CostEstimate(
            flops=6 * groups * full, bytes_accessed=10 * groups * full, transcendentals=0
        ),
        name="tables",
    )(ctf_table, noise_weight)
    if by_distance:
        pair = jnp.zeros((2, per_device, full + LANES), images.dtype)
        pair = lax.dynamic_update_slice(pair, rows, (0, 0, 0))
        pair = lax.dynamic_update_slice(pair, numbers, (0, 0, full))
        pair = lax.dynamic_update_slice(pair, received, (1, 0, 0))
        pair = lax.dynamic_update_slice(pair, received_numbers, (1, 0, full))
        pieces = [pair] + [swap(pair, mask) for mask in range(4, axis_size, 4)]
        parts = [(pieces[:2], ((0, 1), (2, 3))), (pieces[2:], ((4, 5), (6, 7)))]
    else:
        same_core = [[2 * c + core for c in range(chips)] for core in range(2)]
        gathered = lax.all_gather(
            jnp.concatenate([rows, numbers], axis=2), "blk", axis=0, tiled=True, axis_index_groups=same_core
        )
        parts = [([gathered], (tuple(range(chips)),))]

    all_weighted = []
    earlier = ()
    for pieces, sources in parts:
        last = len(all_weighted) == len(parts) - 1
        own_blocks = blocks // len(parts)
        seen = blocks if last else own_blocks
        weighted, *earlier = pl.pallas_call(
            functools.partial(score_kernel, sources, by_distance, shifts, bool(earlier)),
            out_shape=(
                jax.ShapeDtypeStruct((own_blocks * block_rows, full), jnp.bfloat16),
                jax.ShapeDtypeStruct((seen, own_rows, block_rows), jnp.float32),
                jax.ShapeDtypeStruct((seen, own_rows, block_rows), jnp.float32),
                jax.ShapeDtypeStruct(
                    (axis_size if last else 1, 1 if by_distance else blocks, LANES), jnp.float32
                ),
            ),
            in_specs=[VMEM] * (len(pieces) + 4 + len(earlier)),
            out_specs=(VMEM,) * 4,
            scratch_shapes=[
                pltpu.VMEM((own_blocks * ROWS, full + LANES), jnp.float32),
                pltpu.VMEM((ROWS, half), jnp.float32),
                pltpu.VMEM((ROWS, half), jnp.float32),
                pltpu.VMEM((block_rows, candidates), jnp.float32),
                pltpu.VMEM((-(-block_rows // LANES) * LANES, LANES), jnp.float32),
            ],
            compiler_params=params,
            cost_estimate=pl.CostEstimate(
                flops=2 * own_blocks * block_rows * full * (candidates + 8),
                bytes_accessed=2 * own_blocks * block_rows * full,
                transcendentals=0,
            ),
            name="scores",
        )(*pieces, both, high, low, tables, *earlier)
        all_weighted.append(weighted)
    exps, exps_other, stats = earlier

    exchanged = [swap(weighted, 1) for weighted in all_weighted]
    exps_in = swap(exps_other, 1)
    gathered = lax.all_to_all(stats, "blk", 0, 0)
    gathered = gathered.reshape((chips, 2) + gathered.shape[1:])

    slices, best_posterior, log_total = pl.pallas_call(
        functools.partial(
            slice_kernel, own_rows / per_device, len(all_weighted), by_distance
        ),
        out_shape=(
            jax.ShapeDtypeStruct((own_rows, full), jnp.float32),
            jax.ShapeDtypeStruct((per_device,), jnp.float32),
            jax.ShapeDtypeStruct((per_device,), jnp.float32),
        ),
        in_specs=[VMEM] * (3 + 2 * len(all_weighted)),
        out_specs=(HBM, HBM, HBM),
        scratch_shapes=[
            pltpu.SMEM((per_device,), jnp.float32),
            pltpu.SMEM((per_device,), jnp.float32),
            pltpu.VMEM((2, blocks, own_rows, block_rows), jnp.bfloat16),
            pltpu.VMEM((own_rows, full), jnp.float32),
            pltpu.SemaphoreType.DMA((full // 1024,)),
            pltpu.SemaphoreType.DMA((2,)),
        ],
        compiler_params=params,
        name="slices",
    )(gathered, exps, exps_in, *all_weighted, *exchanged)
    return (slices.reshape(batch_count, orient_dev, full), best_posterior, log_total)


def solution(mesh):
    in_specs = (
        P(None, ("groups", "blk"), None),
        P(("groups", "blk"), None),
        P(("groups", "blk")),
        P(("groups", "blk"), None, None),
        P(("groups", "blk")),
        P("groups", None),
        P("groups", None),
    )
    out_specs = (P(None, ("groups", "blk"), None), P(("groups", "blk")), P(("groups", "blk")))
    return jax.shard_map(
        functools.partial(local, mesh.shape["blk"]),
        mesh=mesh,
        in_specs=in_specs,
        out_specs=out_specs,
        check_vma=False,
    )
```

```python
import functools
import math

import jax
import jax.numpy as jnp
from jax import lax
from jax.experimental import pallas as pl
from jax.experimental.pallas import tpu as pltpu
from jax.sharding import PartitionSpec as P

KY = 64
IMG = 256
LANES = 128
ROWS = 8
NEAR = 4
GROUP = 1024
LIMIT_AT = 1
X_AT = 16
Y_AT = 48

VMEM = pl.BlockSpec(memory_space=pltpu.VMEM)
HBM = pl.BlockSpec(memory_space=pltpu.HBM)
NT = (((1,), (1,)), ((), ()))


def sin_cos(turns):
    quarter = IMG // 4
    wrapped = (turns + quarter // 2) & (IMG - 1)
    quadrant = wrapped >> int(math.log2(quarter))
    angle = (wrapped - quadrant * quarter - quarter // 2).astype(jnp.float32) * (
        2.0 * math.pi / IMG
    )
    square = angle * angle
    even = 1.0 + square * (
        -1.0 / 2 + square * (1.0 / 24 + square * (-1.0 / 720 + square * (1.0 / 40320)))
    )
    odd = angle * (
        1.0
        + square
        * (-1.0 / 6 + square * (1.0 / 120 + square * (-1.0 / 5040 + square * (1.0 / 362880))))
    )
    swapped = (quadrant & 1) == 1
    cosine = jnp.where(swapped, odd, even)
    sine = jnp.where(swapped, even, odd)
    cosine = jnp.where((quadrant == 1) | (quadrant == 2), -cosine, cosine)
    sine = jnp.where(quadrant >= 2, -sine, sine)
    return cosine, sine


def split_halves(value):
    high = value.astype(jnp.bfloat16)
    return high, (value - high.astype(jnp.float32)).astype(jnp.bfloat16)


def pack_kernel(group_hbm, limit_hbm, offsets_hbm, packed_ref, group, limit, offsets, sems):
    per_device, _, shifts = offsets_hbm.shape
    copies = [
        pltpu.make_async_copy(group_hbm, group, sems.at[0]),
        pltpu.make_async_copy(limit_hbm, limit, sems.at[1]),
        pltpu.make_async_copy(offsets_hbm, offsets, sems.at[2]),
    ]
    for copy in copies:
        copy.start()
    for copy in copies:
        copy.wait()
    row = lax.broadcasted_iota(jnp.int32, (per_device, LANES), 0)
    lane = lax.broadcasted_iota(jnp.int32, (per_device, LANES), 1)
    numbers = jnp.zeros((per_device, LANES), jnp.int32)
    for particle in range(per_device):
        line = jnp.zeros((per_device, LANES), jnp.int32)
        line = jnp.where(lane == 0, group[particle], line)
        line = jnp.where(lane == LIMIT_AT, limit[particle], line)
        for shift in range(shifts):
            line = jnp.where(lane == X_AT + shift, offsets[particle, 0, shift], line)
            line = jnp.where(lane == Y_AT + shift, offsets[particle, 1, shift], line)
        numbers = jnp.where(row == particle, line, numbers)
    packed_ref[0] = numbers.astype(jnp.float32).astype(jnp.bfloat16)


def split_thirds(value):
    high = value.astype(jnp.bfloat16)
    rest = value - high.astype(jnp.float32)
    middle = rest.astype(jnp.bfloat16)
    return high, middle, (rest - middle.astype(jnp.float32)).astype(jnp.bfloat16)


def power_kernel(own_ref, other_ref, both_ref, high_ref, low_ref):
    rows, full = own_ref.shape
    half = full // 2
    for place, ref in enumerate((own_ref, other_ref)):
        at = pl.ds(place * rows, rows)
        both_ref[at, :] = ref[...]
        real = ref[:, :half].astype(jnp.float32)
        imag = ref[:, half:].astype(jnp.float32)
        high, low = split_halves(real * real + imag * imag)
        high_ref[at, :] = high
        low_ref[at, :] = low


def table_kernel(ctf_ref, noise_ref, table_ref):
    groups, half = ctf_ref.shape
    for place, ref in enumerate((ctf_ref, noise_ref)):
        for third, part in enumerate(split_thirds(ref[...])):
            table_ref[pl.ds(third * groups, groups), pl.ds(place * half, half)] = part


def score_kernel(sources, by_distance, shifts, has_earlier, *refs):
    pieces = refs[: len(sources)]
    refs = refs[len(sources) :]
    both_ref, high_ref, low_ref, table_ref = refs[:4]
    refs = refs[4:]
    if has_earlier:
        _, earlier_own_ref, earlier_other_ref, earlier_stats_ref = refs[:4]
        refs = refs[4:]
    weighted_ref, exps_ref, *exps_other_refs, stats_ref = refs[:-5]
    image_ref, real_ref, imag_ref, cross_ref, square_ref = refs[-5:]
    full = both_ref.shape[1]
    half = full // 2
    groups = table_ref.shape[0] // 3
    candidates = both_ref.shape[0]
    rows_total = image_ref.shape[0]

    def put_exps(slot, values):
        for ref in exps_other_refs:
            ref[slot] = values
        if has_earlier:
            for third, part in enumerate(split_thirds(values)):
                at = pl.ds(full + (3 * slot + third) * LANES, values.shape[1])
                weighted_ref[pl.ds(0, values.shape[0]), at] = part

    per_device = pieces[0].shape[1]
    scale = 0.5 / math.sqrt(half)
    chip = lax.axis_index("blk") >> 1
    for piece, places in zip(pieces, sources):
        for row, place in enumerate(places):
            if by_distance:
                place = (chip ^ place) & (NEAR - 1)
            values = piece[row].astype(jnp.float32)
            for sub in range(per_device):
                image_ref[pl.ds(place * per_device + sub, 1), :] = values[sub : sub + 1]

    block_rows = shifts * ROWS
    slot = 1 if has_earlier else 0
    if has_earlier:
        exps_ref[0] = earlier_own_ref[0]
        put_exps(0, earlier_other_ref[0])

    def block(index, carry):
        rows = pl.ds(pl.multiple_of(index * ROWS, ROWS), ROWS)
        first = pl.multiple_of((index + slot) * block_rows, ROWS)
        numbers = image_ref[rows, full:]
        column = lax.broadcasted_iota(jnp.int32, (ROWS, 3 * groups), 1) % groups
        one_hot = (numbers[:, :1].astype(jnp.int32) == column).astype(jnp.bfloat16)
        tables = jnp.dot(one_hot, table_ref[...], preferred_element_type=jnp.float32)
        ctf = tables[:, :half]
        noise = tables[:, half:]
        limit = numbers[:, LIMIT_AT : LIMIT_AT + 1].astype(jnp.int32)
        position = lax.broadcasted_iota(jnp.int32, (ROWS, half), 1)
        freq_x = position >> int(math.log2(KY))
        freq_y = (position & (KY - 1)) - KY // 2
        weight = jnp.where(freq_x * freq_x + freq_y * freq_y < limit * limit, noise, 0.0)
        ctf_weight = weight * ctf
        real = image_ref[rows, :half]
        imag = image_ref[rows, half:full]
        norm = jnp.sum(weight * (real * real + imag * imag), axis=1, keepdims=True)
        real_ref[...] = ctf_weight * real
        imag_ref[...] = ctf_weight * imag
        quad_high, quad_low = split_halves(ctf_weight * ctf)
        quad_weight = jnp.concatenate([quad_high, quad_low], axis=0)
        quad = lax.dot_general(
            quad_weight, high_ref[...], NT, preferred_element_type=jnp.float32
        ) + lax.dot_general(quad_weight, low_ref[...], NT, preferred_element_type=jnp.float32)
        quad = quad[:ROWS] + quad[ROWS:]

        numbers_int = numbers.astype(jnp.int32)
        step_cos, step_sin = sin_cos(numbers_int * (LANES // KY))
        phases = []
        for start in range(0, shifts, 2):
            members = range(start, min(start + 2, shifts))

            def stacked(value, base):
                return jnp.concatenate(
                    [value[:, base + shift : base + shift + 1] for shift in members], axis=0
                )

            height = len(members) * ROWS
            lane = lax.broadcasted_iota(jnp.int32, (height, LANES), 1)
            turns = (lane >> int(math.log2(KY))) * stacked(numbers_int, X_AT) + (
                (lane & (KY - 1)) - KY // 2
            ) * stacked(numbers_int, Y_AT)
            cosine, sine = sin_cos(turns)
            turn_cos = stacked(step_cos, X_AT)
            turn_sin = stacked(step_sin, X_AT)
            cosine_before = cosine * turn_cos + sine * turn_sin
            sine_before = sine * turn_cos - cosine * turn_sin
            double = jnp.broadcast_to(2.0 * turn_cos, (height, LANES))
            phases.append((cosine, cosine_before, sine, sine_before, double))

        cross = jnp.zeros(cross_ref.shape, jnp.float32)
        for group in range(0, half, GROUP):
            for number, phase in enumerate(phases):
                cosine, cosine_before, sine, sine_before, double = phase
                height = double.shape[0]
                out_rows = pl.ds(first + 2 * number * ROWS, height)
                for start in range(group, group + GROUP, LANES):
                    at = pl.ds(start, LANES)
                    real = jnp.concatenate([real_ref[:, at]] * (height // ROWS), axis=0)
                    imag = jnp.concatenate([imag_ref[:, at]] * (height // ROWS), axis=0)
                    weighted_ref[out_rows, at] = (real * cosine + imag * sine).astype(
                        jnp.bfloat16
                    )
                    weighted_ref[out_rows, pl.ds(half + start, LANES)] = (
                        imag * cosine - real * sine
                    ).astype(jnp.bfloat16)
                    cosine, cosine_before = double * cosine - cosine_before, cosine
                    sine, sine_before = double * sine - sine_before, sine
                phases[number] = (cosine, cosine_before, sine, sine_before, double)
            for base in (group, half + group):
                at = pl.ds(base, GROUP)
                cross = cross + lax.dot_general(
                    weighted_ref[pl.ds(first, block_rows), at],
                    both_ref[:, at],
                    NT,
                    preferred_element_type=jnp.float32,
                )
        cross_ref[...] = cross
        base = norm + quad
        scores = [
            -(base - 2.0 * cross_ref[pl.ds(shift * ROWS, ROWS), :]) * scale
            for shift in range(shifts)
        ]
        top = jnp.max(functools.reduce(jnp.maximum, scores), axis=1, keepdims=True)
        exps = [jnp.exp(score - top) for score in scores]
        total = jnp.sum(functools.reduce(jnp.add, exps), axis=1, keepdims=True)
        for shift in range(shifts):
            square_ref[pl.ds(shift * ROWS, ROWS), :candidates] = exps[shift]
        turned = square_ref[...].T
        exps_ref[index + slot] = turned[: candidates // 2, :block_rows]
        put_exps(index + slot, turned[candidates // 2 : candidates, :block_rows])
        row = lax.broadcasted_iota(jnp.int32, (ROWS, LANES), 0)
        lane = lax.broadcasted_iota(jnp.int32, (ROWS, LANES), 1)
        half_at = chip // NEAR ^ slot if by_distance else 0
        here = (lane & (2 * ROWS - 1)) == row + half_at * ROWS
        line = jnp.sum(
            jnp.where(here, jnp.where(lane < LANES // 2, top, total), 0.0),
            axis=0,
            keepdims=True,
        )
        if has_earlier:
            line = line + earlier_stats_ref[0]
        for target in range(stats_ref.shape[0]):
            stats_ref[target, pl.ds(index, 1), :] = line
        return carry

    lax.fori_loop(0, rows_total // ROWS, block, 0)


def slice_kernel(scale, calls, by_distance, *refs):
    stats_ref, exps_own_ref = refs[:2]
    refs = refs[2:]
    if not by_distance:
        exps_other_ref, *refs = refs
    weighted_refs = (refs[:calls], refs[calls : 2 * calls])
    out_hbm, best_hbm, log_hbm = refs[2 * calls : 2 * calls + 3]
    best_ref, log_ref, posterior_ref, summed_ref, sems, number_sems = refs[2 * calls + 3 :]
    blocks, rows, block_rows = exps_own_ref.shape
    chips = stats_ref.shape[0]
    per_device = best_ref.shape[0]
    full = out_hbm.shape[1]
    index = lax.axis_index("blk")
    chip = index >> 1
    lane = lax.broadcasted_iota(jnp.int32, (1, LANES), 1)

    def combined(core, row):
        at = pl.ds(row, 1)
        lower = lane < LANES // 2
        lines = [stats_ref[source, core, at, :] for source in range(chips)]
        lines.append(stats_ref[chip, core, at, :])
        turned = [pltpu.roll(line, LANES // 2, 1) for line in lines]
        tops = [jnp.where(lower, one, two) for one, two in zip(lines, turned)]
        totals = [jnp.where(lower, two, one) for one, two in zip(lines, turned)]
        top = functools.reduce(jnp.maximum, tops)
        total = functools.reduce(
            jnp.add, [part * jnp.exp(high - top) for high, part in zip(tops[:-1], totals)]
        )
        return top, top + jnp.log(total), tops[-1]

    upper = (lane & ROWS) != 0
    def exps_of(side, block):
        if side == 0:
            return exps_own_ref[block]
        if not by_distance:
            return exps_other_ref[block]
        parts = [
            weighted_refs[1][-1][
                pl.ds(0, rows), pl.ds(full + (3 * block + third) * LANES, block_rows)
            ].astype(jnp.float32)
            for third in range(3)
        ]
        return parts[0] + (parts[1] + parts[2])

    for side in range(2):
        core = (index & 1) ^ side
        for block in range(blocks):
            if block == 0 or not by_distance:
                top, log_total, mine = combined(core, block)
                line = jnp.exp(mine - log_total)
                crossed = pltpu.roll(line, ROWS, 1)
            wanted = (chip // NEAR ^ block) != 0 if by_distance else False
            factor = jnp.where(upper == wanted, line, crossed)
            posterior_ref[side, block] = (exps_of(side, block) * factor[:, :block_rows]).astype(
                jnp.bfloat16
            )

    width = 1024
    copies = []
    for number, start in enumerate(range(0, full, width)):
        at = pl.ds(start, width)
        products = []
        for side in range(2):
            for block in range(blocks):
                call, place = divmod(block, blocks // calls)
                products.append(
                    jnp.dot(
                        posterior_ref[side, block],
                        weighted_refs[side][call][pl.ds(place * block_rows, block_rows), at],
                        preferred_element_type=jnp.float32,
                    )
                )
        summed_ref[:, at] = functools.reduce(jnp.add, products) * scale
        copy = pltpu.make_async_copy(summed_ref.at[:, at], out_hbm.at[:, at], sems.at[number])
        copy.start()
        copies.append(copy)
        if number == 0:
            for row in range(per_device):
                particle = chip * per_device + row
                if by_distance:
                    top, log_total, mine = combined(index & 1, 0)
                    chosen = lane == particle
                else:
                    top, log_total, mine = combined(index & 1, particle // ROWS)
                    chosen = lane == particle % ROWS
                best_ref[row] = jnp.sum(jnp.where(chosen, jnp.exp(top - log_total), 0.0))
                log_ref[row] = jnp.sum(jnp.where(chosen, log_total, 0.0))
            copies.append(pltpu.make_async_copy(best_ref, best_hbm, number_sems.at[0]))
            copies.append(pltpu.make_async_copy(log_ref, log_hbm, number_sems.at[1]))
            copies[-2].start()
            copies[-1].start()
    for copy in copies:
        copy.wait()


def local(
    axis_size, projections, images, ctf_group, shift_offsets, shell_limit, ctf_table, noise_weight
):
    batch_count, orient_dev, full = projections.shape
    half = full // 2
    own_rows = batch_count * orient_dev
    candidates = 2 * own_rows
    per_device = images.shape[0]
    shifts = shift_offsets.shape[1]
    chips = axis_size // 2
    particles = chips * per_device
    blocks = particles // ROWS
    block_rows = shifts * ROWS
    megabytes = 12 + -(-2 * blocks * block_rows * full * 2 // 2**20)
    params = pltpu.CompilerParams(vmem_limit_bytes=megabytes * 2**20)

    def swap(value, mask):
        return lax.ppermute(value, "blk", [(i, i ^ mask) for i in range(axis_size)])

    numbers = pl.pallas_call(
        pack_kernel,
        out_shape=jax.ShapeDtypeStruct((1, per_device, LANES), jnp.bfloat16),
        in_specs=[HBM] * 3,
        out_specs=VMEM,
        scratch_shapes=[
            pltpu.SMEM((per_device,), jnp.int32),
            pltpu.SMEM((per_device,), jnp.int32),
            pltpu.SMEM((per_device, 2, shifts), jnp.int32),
            pltpu.SemaphoreType.DMA((3,)),
        ],
        compiler_params=pltpu.CompilerParams(vmem_limit_bytes=60 * 2**20),
        name="pack",
    )(ctf_group, shell_limit, shift_offsets.transpose(0, 2, 1))
    by_distance = chips == 2 * NEAR and per_device * NEAR == ROWS
    rows = images[None]
    if by_distance:
        received = swap(rows, 2)

    flat = projections.reshape(own_rows, full)
    other = swap(flat, 1)
    if by_distance:
        rows, numbers, other = lax.optimization_barrier((rows, numbers, other))
        received_numbers = swap(numbers, 2)
    groups = ctf_table.shape[0]
    both, high, low = pl.pallas_call(
        power_kernel,
        out_shape=(
            jax.ShapeDtypeStruct((candidates, full), jnp.bfloat16),
            jax.ShapeDtypeStruct((candidates, half), jnp.bfloat16),
            jax.ShapeDtypeStruct((candidates, half), jnp.bfloat16),
        ),
        in_specs=[VMEM] * 2,
        out_specs=(VMEM,) * 3,
        compiler_params=params,
        cost_estimate=pl.CostEstimate(
            flops=8 * candidates * full, bytes_accessed=4 * candidates * full, transcendentals=0
        ),
        name="power",
    )(flat, other)
    tables = pl.pallas_call(
        table_kernel,
        out_shape=jax.ShapeDtypeStruct((3 * groups, full), jnp.bfloat16),
        in_specs=[VMEM] * 2,
        out_specs=VMEM,
        compiler_params=params,
        cost_estimate=pl.CostEstimate(
            flops=6 * groups * full, bytes_accessed=10 * groups * full, transcendentals=0
        ),
        name="tables",
    )(ctf_table, noise_weight)
    if by_distance:
        pair = jnp.zeros((2, per_device, full + LANES), images.dtype)
        pair = lax.dynamic_update_slice(pair, rows, (0, 0, 0))
        pair = lax.dynamic_update_slice(pair, numbers, (0, 0, full))
        pair = lax.dynamic_update_slice(pair, received, (1, 0, 0))
        pair = lax.dynamic_update_slice(pair, received_numbers, (1, 0, full))
        pieces = [pair] + [swap(pair, mask) for mask in range(4, axis_size, 4)]
        parts = [(pieces[:2], ((0, 1), (2, 3))), (pieces[2:], ((4, 5), (6, 7)))]
    else:
        same_core = [[2 * c + core for c in range(chips)] for core in range(2)]
        gathered = lax.all_gather(
            jnp.concatenate([rows, numbers], axis=2), "blk", axis=0, tiled=True, axis_index_groups=same_core
        )
        parts = [([gathered], (tuple(range(chips)),))]

    earlier = ()
    for number, (pieces, sources) in enumerate(parts):
        last = number == len(parts) - 1
        own_blocks = blocks // len(parts)
        seen = blocks if last else own_blocks
        exps_shape = jax.ShapeDtypeStruct((seen, own_rows, block_rows), jnp.float32)
        earlier = pl.pallas_call(
            functools.partial(score_kernel, sources, by_distance, shifts, bool(earlier)),
            out_shape=(
                jax.ShapeDtypeStruct(
                    (blocks * block_rows, full + (3 * blocks * LANES if by_distance else 0)),
                    jnp.bfloat16,
                ),
                *([exps_shape] if earlier else [exps_shape] * 2),
                jax.ShapeDtypeStruct(
                    (axis_size if last else 1, 1 if by_distance else blocks, LANES), jnp.float32
                ),
            ),
            in_specs=[VMEM] * (len(pieces) + 4 + len(earlier)),
            out_specs=(VMEM,) * (3 if earlier else 4),
            scratch_shapes=[
                pltpu.VMEM((own_blocks * ROWS, full + LANES), jnp.float32),
                pltpu.VMEM((ROWS, half), jnp.float32),
                pltpu.VMEM((ROWS, half), jnp.float32),
                pltpu.VMEM((block_rows, candidates), jnp.float32),
                pltpu.VMEM((-(-block_rows // LANES) * LANES, LANES), jnp.float32),
            ],
            input_output_aliases={len(pieces) + 4: 0} if earlier else {},
            compiler_params=params,
            cost_estimate=pl.CostEstimate(
                flops=2 * own_blocks * block_rows * full * (candidates + 8),
                bytes_accessed=2 * own_blocks * block_rows * full,
                transcendentals=0,
            ),
            name="scores",
        )(*pieces, both, high, low, tables, *earlier)
    weighted, exps, *exps_other, stats = earlier

    all_weighted = [weighted]
    exchanged = [swap(weighted, 1)]
    exps_in = [swap(part, 1) for part in exps_other]
    gathered = lax.all_to_all(stats, "blk", 0, 0)
    gathered = gathered.reshape((chips, 2) + gathered.shape[1:])

    slices, best_posterior, log_total = pl.pallas_call(
        functools.partial(
            slice_kernel, own_rows / per_device, len(all_weighted), by_distance
        ),
        out_shape=(
            jax.ShapeDtypeStruct((own_rows, full), jnp.float32),
            jax.ShapeDtypeStruct((per_device,), jnp.float32),
            jax.ShapeDtypeStruct((per_device,), jnp.float32),
        ),
        in_specs=[VMEM] * (2 + len(exps_in) + 2 * len(all_weighted)),
        out_specs=(HBM, HBM, HBM),
        scratch_shapes=[
            pltpu.SMEM((per_device,), jnp.float32),
            pltpu.SMEM((per_device,), jnp.float32),
            pltpu.VMEM((2, blocks, own_rows, block_rows), jnp.bfloat16),
            pltpu.VMEM((own_rows, full), jnp.float32),
            pltpu.SemaphoreType.DMA((full // 1024,)),
            pltpu.SemaphoreType.DMA((2,)),
        ],
        compiler_params=params,
        name="slices",
    )(gathered, exps, *exps_in, *all_weighted, *exchanged)
    return (slices.reshape(batch_count, orient_dev, full), best_posterior, log_total)


def solution(mesh):
    in_specs = (
        P(None, ("groups", "blk"), None),
        P(("groups", "blk"), None),
        P(("groups", "blk")),
        P(("groups", "blk"), None, None),
        P(("groups", "blk")),
        P("groups", None),
        P("groups", None),
    )
    out_specs = (P(None, ("groups", "blk"), None), P(("groups", "blk")), P(("groups", "blk")))
    return jax.shard_map(
        functools.partial(local, mesh.shape["blk"]),
        mesh=mesh,
        in_specs=in_specs,
        out_specs=out_specs,
        check_vma=False,
    )
```

```python
import functools
import math

import jax
import jax.numpy as jnp
from jax import lax
from jax.experimental import pallas as pl
from jax.experimental.pallas import tpu as pltpu
from jax.sharding import PartitionSpec as P

KY = 64
IMG = 256
LANES = 128
ROWS = 8
NEAR = 4
GROUP = 1024
LIMIT_AT = 1
X_AT = 16
Y_AT = 48

VMEM = pl.BlockSpec(memory_space=pltpu.VMEM)
HBM = pl.BlockSpec(memory_space=pltpu.HBM)
NT = (((1,), (1,)), ((), ()))


def sin_cos(turns):
    quarter = IMG // 4
    wrapped = (turns + quarter // 2) & (IMG - 1)
    quadrant = wrapped >> int(math.log2(quarter))
    angle = (wrapped - quadrant * quarter - quarter // 2).astype(jnp.float32) * (
        2.0 * math.pi / IMG
    )
    square = angle * angle
    even = 1.0 + square * (
        -1.0 / 2 + square * (1.0 / 24 + square * (-1.0 / 720 + square * (1.0 / 40320)))
    )
    odd = angle * (
        1.0
        + square
        * (-1.0 / 6 + square * (1.0 / 120 + square * (-1.0 / 5040 + square * (1.0 / 362880))))
    )
    swapped = (quadrant & 1) == 1
    cosine = jnp.where(swapped, odd, even)
    sine = jnp.where(swapped, even, odd)
    cosine = jnp.where((quadrant == 1) | (quadrant == 2), -cosine, cosine)
    sine = jnp.where(quadrant >= 2, -sine, sine)
    return cosine, sine


def split_halves(value):
    high = value.astype(jnp.bfloat16)
    return high, (value - high.astype(jnp.float32)).astype(jnp.bfloat16)


def pack_kernel(group_hbm, limit_hbm, offsets_hbm, packed_ref, group, limit, offsets, sems):
    per_device, _, shifts = offsets_hbm.shape
    copies = [
        pltpu.make_async_copy(group_hbm, group, sems.at[0]),
        pltpu.make_async_copy(limit_hbm, limit, sems.at[1]),
        pltpu.make_async_copy(offsets_hbm, offsets, sems.at[2]),
    ]
    for copy in copies:
        copy.start()
    for copy in copies:
        copy.wait()
    row = lax.broadcasted_iota(jnp.int32, (per_device, LANES), 0)
    lane = lax.broadcasted_iota(jnp.int32, (per_device, LANES), 1)
    numbers = jnp.zeros((per_device, LANES), jnp.int32)
    for particle in range(per_device):
        line = jnp.zeros((per_device, LANES), jnp.int32)
        line = jnp.where(lane == 0, group[particle], line)
        line = jnp.where(lane == LIMIT_AT, limit[particle], line)
        for shift in range(shifts):
            line = jnp.where(lane == X_AT + shift, offsets[particle, 0, shift], line)
            line = jnp.where(lane == Y_AT + shift, offsets[particle, 1, shift], line)
        numbers = jnp.where(row == particle, line, numbers)
    packed_ref[0] = numbers.astype(jnp.float32).astype(jnp.bfloat16)


def split_thirds(value):
    high = value.astype(jnp.bfloat16)
    rest = value - high.astype(jnp.float32)
    middle = rest.astype(jnp.bfloat16)
    return high, middle, (rest - middle.astype(jnp.float32)).astype(jnp.bfloat16)


def power_kernel(own_ref, other_ref, both_ref, high_ref, low_ref):
    rows, full = own_ref.shape
    half = full // 2
    for place, ref in enumerate((own_ref, other_ref)):
        at = pl.ds(place * rows, rows)
        both_ref[at, :] = ref[...]
        real = ref[:, :half].astype(jnp.float32)
        imag = ref[:, half:].astype(jnp.float32)
        high, low = split_halves(real * real + imag * imag)
        high_ref[at, :] = high
        low_ref[at, :] = low


def table_kernel(values_ref, table_ref):
    groups = values_ref.shape[0]
    for third, part in enumerate(split_thirds(values_ref[...])):
        table_ref[pl.ds(third * groups, groups), :] = part


def score_kernel(sources, by_distance, shifts, has_earlier, *refs):
    pieces = refs[: len(sources)]
    refs = refs[len(sources) :]
    both_ref, high_ref, low_ref, ctf_ref, noise_ref = refs[:5]
    refs = refs[5:]
    if has_earlier:
        _, earlier_own_ref, earlier_other_ref, earlier_stats_ref = refs[:4]
        refs = refs[4:]
    weighted_ref, exps_ref, *exps_other_refs, stats_ref = refs[:-5]
    image_ref, real_ref, imag_ref, cross_ref, square_ref = refs[-5:]
    full = both_ref.shape[1]
    half = full // 2
    groups = ctf_ref.shape[0] // 3
    candidates = both_ref.shape[0]
    rows_total = image_ref.shape[0]

    def put_exps(slot, values):
        for ref in exps_other_refs:
            ref[slot] = values
        if has_earlier:
            for third, part in enumerate(split_thirds(values)):
                at = pl.ds(full + (3 * slot + third) * LANES, values.shape[1])
                weighted_ref[pl.ds(0, values.shape[0]), at] = part

    per_device = pieces[0].shape[1]
    scale = 0.5 / math.sqrt(half)
    chip = lax.axis_index("blk") >> 1
    for piece, places in zip(pieces, sources):
        for row, place in enumerate(places):
            if by_distance:
                place = (chip ^ place) & (NEAR - 1)
            values = piece[row].astype(jnp.float32)
            for sub in range(per_device):
                image_ref[pl.ds(place * per_device + sub, 1), :] = values[sub : sub + 1]

    block_rows = shifts * ROWS
    slot = 1 if has_earlier else 0
    if has_earlier:
        exps_ref[0] = earlier_own_ref[0]
        put_exps(0, earlier_other_ref[0])

    def block(index, carry):
        rows = pl.ds(pl.multiple_of(index * ROWS, ROWS), ROWS)
        first = pl.multiple_of((index + slot) * block_rows, ROWS)
        numbers = image_ref[rows, full:]
        column = lax.broadcasted_iota(jnp.int32, (ROWS, 3 * groups), 1) % groups
        one_hot = (numbers[:, :1].astype(jnp.int32) == column).astype(jnp.bfloat16)
        ctf = jnp.dot(one_hot, ctf_ref[...], preferred_element_type=jnp.float32)
        noise = jnp.dot(one_hot, noise_ref[...], preferred_element_type=jnp.float32)
        limit = numbers[:, LIMIT_AT : LIMIT_AT + 1].astype(jnp.int32)
        position = lax.broadcasted_iota(jnp.int32, (ROWS, half), 1)
        freq_x = position >> int(math.log2(KY))
        freq_y = (position & (KY - 1)) - KY // 2
        weight = jnp.where(freq_x * freq_x + freq_y * freq_y < limit * limit, noise, 0.0)
        ctf_weight = weight * ctf
        real = image_ref[rows, :half]
        imag = image_ref[rows, half:full]
        norm = jnp.sum(weight * (real * real + imag * imag), axis=1, keepdims=True)
        real_ref[...] = ctf_weight * real
        imag_ref[...] = ctf_weight * imag
        quad_high, quad_low = split_halves(ctf_weight * ctf)
        quad_weight = jnp.concatenate([quad_high, quad_low], axis=0)
        quad = lax.dot_general(
            quad_weight, high_ref[...], NT, preferred_element_type=jnp.float32
        ) + lax.dot_general(quad_weight, low_ref[...], NT, preferred_element_type=jnp.float32)
        quad = quad[:ROWS] + quad[ROWS:]

        numbers_int = numbers.astype(jnp.int32)
        step_cos, step_sin = sin_cos(numbers_int * (LANES // KY))
        phases = []
        for start in range(0, shifts, 2):
            members = range(start, min(start + 2, shifts))

            def stacked(value, base):
                return jnp.concatenate(
                    [value[:, base + shift : base + shift + 1] for shift in members], axis=0
                )

            height = len(members) * ROWS
            lane = lax.broadcasted_iota(jnp.int32, (height, LANES), 1)
            turns = (lane >> int(math.log2(KY))) * stacked(numbers_int, X_AT) + (
                (lane & (KY - 1)) - KY // 2
            ) * stacked(numbers_int, Y_AT)
            cosine, sine = sin_cos(turns)
            turn_cos = stacked(step_cos, X_AT)
            turn_sin = stacked(step_sin, X_AT)
            cosine_before = cosine * turn_cos + sine * turn_sin
            sine_before = sine * turn_cos - cosine * turn_sin
            double = jnp.broadcast_to(2.0 * turn_cos, (height, LANES))
            phases.append((cosine, cosine_before, sine, sine_before, double))

        cross = jnp.zeros(cross_ref.shape, jnp.float32)
        for group in range(0, half, GROUP):
            for number, phase in enumerate(phases):
                cosine, cosine_before, sine, sine_before, double = phase
                height = double.shape[0]
                out_rows = pl.ds(first + 2 * number * ROWS, height)
                for start in range(group, group + GROUP, LANES):
                    at = pl.ds(start, LANES)
                    real = jnp.concatenate([real_ref[:, at]] * (height // ROWS), axis=0)
                    imag = jnp.concatenate([imag_ref[:, at]] * (height // ROWS), axis=0)
                    weighted_ref[out_rows, at] = (real * cosine + imag * sine).astype(
                        jnp.bfloat16
                    )
                    weighted_ref[out_rows, pl.ds(half + start, LANES)] = (
                        imag * cosine - real * sine
                    ).astype(jnp.bfloat16)
                    cosine, cosine_before = double * cosine - cosine_before, cosine
                    sine, sine_before = double * sine - sine_before, sine
                phases[number] = (cosine, cosine_before, sine, sine_before, double)
            for base in (group, half + group):
                at = pl.ds(base, GROUP)
                cross = cross + lax.dot_general(
                    weighted_ref[pl.ds(first, block_rows), at],
                    both_ref[:, at],
                    NT,
                    preferred_element_type=jnp.float32,
                )
        cross_ref[...] = cross
        base = norm + quad
        scores = [
            -(base - 2.0 * cross_ref[pl.ds(shift * ROWS, ROWS), :]) * scale
            for shift in range(shifts)
        ]
        top = jnp.max(functools.reduce(jnp.maximum, scores), axis=1, keepdims=True)
        exps = [jnp.exp(score - top) for score in scores]
        total = jnp.sum(functools.reduce(jnp.add, exps), axis=1, keepdims=True)
        for shift in range(shifts):
            square_ref[pl.ds(shift * ROWS, ROWS), :candidates] = exps[shift]
        turned = square_ref[...].T
        exps_ref[index + slot] = turned[: candidates // 2, :block_rows]
        put_exps(index + slot, turned[candidates // 2 : candidates, :block_rows])
        row = lax.broadcasted_iota(jnp.int32, (ROWS, LANES), 0)
        lane = lax.broadcasted_iota(jnp.int32, (ROWS, LANES), 1)
        half_at = chip // NEAR ^ slot if by_distance else 0
        here = (lane & (2 * ROWS - 1)) == row + half_at * ROWS
        line = jnp.sum(
            jnp.where(here, jnp.where(lane < LANES // 2, top, total), 0.0),
            axis=0,
            keepdims=True,
        )
        if has_earlier:
            line = line + earlier_stats_ref[0]
        for target in range(stats_ref.shape[0]):
            stats_ref[target, pl.ds(index, 1), :] = line
        return carry

    lax.fori_loop(0, rows_total // ROWS, block, 0)


def slice_kernel(scale, calls, by_distance, *refs):
    stats_ref, exps_own_ref = refs[:2]
    refs = refs[2:]
    if not by_distance:
        exps_other_ref, *refs = refs
    weighted_refs = (refs[:calls], refs[calls : 2 * calls])
    out_hbm, best_hbm, log_hbm = refs[2 * calls : 2 * calls + 3]
    best_ref, log_ref, posterior_ref, summed_ref, sems, number_sems = refs[2 * calls + 3 :]
    blocks, rows, block_rows = exps_own_ref.shape
    chips = stats_ref.shape[0]
    per_device = best_ref.shape[0]
    full = out_hbm.shape[1]
    index = lax.axis_index("blk")
    chip = index >> 1
    lane = lax.broadcasted_iota(jnp.int32, (1, LANES), 1)

    def combined(core, row):
        at = pl.ds(row, 1)
        lower = lane < LANES // 2
        lines = [stats_ref[source, core, at, :] for source in range(chips)]
        lines.append(stats_ref[chip, core, at, :])
        turned = [pltpu.roll(line, LANES // 2, 1) for line in lines]
        tops = [jnp.where(lower, one, two) for one, two in zip(lines, turned)]
        totals = [jnp.where(lower, two, one) for one, two in zip(lines, turned)]
        top = functools.reduce(jnp.maximum, tops)
        total = functools.reduce(
            jnp.add, [part * jnp.exp(high - top) for high, part in zip(tops[:-1], totals)]
        )
        return top, top + jnp.log(total), tops[-1]

    upper = (lane & ROWS) != 0
    def exps_of(side, block):
        if side == 0:
            return exps_own_ref[block]
        if not by_distance:
            return exps_other_ref[block]
        parts = [
            weighted_refs[1][-1][
                pl.ds(0, rows), pl.ds(full + (3 * block + third) * LANES, block_rows)
            ].astype(jnp.float32)
            for third in range(3)
        ]
        return parts[0] + (parts[1] + parts[2])

    for side in range(2):
        core = (index & 1) ^ side
        for block in range(blocks):
            if block == 0 or not by_distance:
                top, log_total, mine = combined(core, block)
                line = jnp.exp(mine - log_total)
                crossed = pltpu.roll(line, ROWS, 1)
            wanted = (chip // NEAR ^ block) != 0 if by_distance else False
            factor = jnp.where(upper == wanted, line, crossed)
            posterior_ref[side, block] = (exps_of(side, block) * factor[:, :block_rows]).astype(
                jnp.bfloat16
            )

    width = 1024
    copies = []
    for number, start in enumerate(range(0, full, width)):
        at = pl.ds(start, width)
        products = []
        for side in range(2):
            for block in range(blocks):
                call, place = divmod(block, blocks // calls)
                products.append(
                    jnp.dot(
                        posterior_ref[side, block],
                        weighted_refs[side][call][pl.ds(place * block_rows, block_rows), at],
                        preferred_element_type=jnp.float32,
                    )
                )
        summed_ref[:, at] = functools.reduce(jnp.add, products) * scale
        copy = pltpu.make_async_copy(summed_ref.at[:, at], out_hbm.at[:, at], sems.at[number])
        copy.start()
        copies.append(copy)
        if number == 0:
            for row in range(per_device):
                particle = chip * per_device + row
                if by_distance:
                    top, log_total, mine = combined(index & 1, 0)
                    chosen = lane == particle
                else:
                    top, log_total, mine = combined(index & 1, particle // ROWS)
                    chosen = lane == particle % ROWS
                best_ref[row] = jnp.sum(jnp.where(chosen, jnp.exp(top - log_total), 0.0))
                log_ref[row] = jnp.sum(jnp.where(chosen, log_total, 0.0))
            copies.append(pltpu.make_async_copy(best_ref, best_hbm, number_sems.at[0]))
            copies.append(pltpu.make_async_copy(log_ref, log_hbm, number_sems.at[1]))
            copies[-2].start()
            copies[-1].start()
    for copy in copies:
        copy.wait()


def local(
    axis_size, projections, images, ctf_group, shift_offsets, shell_limit, ctf_table, noise_weight
):
    batch_count, orient_dev, full = projections.shape
    half = full // 2
    own_rows = batch_count * orient_dev
    candidates = 2 * own_rows
    per_device = images.shape[0]
    shifts = shift_offsets.shape[1]
    chips = axis_size // 2
    particles = chips * per_device
    blocks = particles // ROWS
    block_rows = shifts * ROWS
    megabytes = 12 + -(-2 * blocks * block_rows * full * 2 // 2**20)
    params = pltpu.CompilerParams(vmem_limit_bytes=megabytes * 2**20)

    def swap(value, mask):
        return lax.ppermute(value, "blk", [(i, i ^ mask) for i in range(axis_size)])

    numbers = pl.pallas_call(
        pack_kernel,
        out_shape=jax.ShapeDtypeStruct((1, per_device, LANES), jnp.bfloat16),
        in_specs=[HBM] * 3,
        out_specs=VMEM,
        scratch_shapes=[
            pltpu.SMEM((per_device,), jnp.int32),
            pltpu.SMEM((per_device,), jnp.int32),
            pltpu.SMEM((per_device, 2, shifts), jnp.int32),
            pltpu.SemaphoreType.DMA((3,)),
        ],
        compiler_params=pltpu.CompilerParams(vmem_limit_bytes=60 * 2**20),
        name="pack",
    )(ctf_group, shell_limit, shift_offsets.transpose(0, 2, 1))
    by_distance = chips == 2 * NEAR and per_device * NEAR == ROWS
    rows = images[None]
    if by_distance:
        received = swap(rows, 2)

    flat = projections.reshape(own_rows, full)
    other = swap(flat, 1)
    if by_distance:
        rows, numbers, other = lax.optimization_barrier((rows, numbers, other))
        received_numbers = swap(numbers, 2)
    groups = ctf_table.shape[0]
    both, high, low = pl.pallas_call(
        power_kernel,
        out_shape=(
            jax.ShapeDtypeStruct((candidates, full), jnp.bfloat16),
            jax.ShapeDtypeStruct((candidates, half), jnp.bfloat16),
            jax.ShapeDtypeStruct((candidates, half), jnp.bfloat16),
        ),
        in_specs=[VMEM] * 2,
        out_specs=(VMEM,) * 3,
        compiler_params=params,
        cost_estimate=pl.CostEstimate(
            flops=8 * candidates * full, bytes_accessed=4 * candidates * full, transcendentals=0
        ),
        name="power",
    )(flat, other)
    def in_thirds(values, name):
        return pl.pallas_call(
            table_kernel,
            out_shape=jax.ShapeDtypeStruct((3 * groups, half), jnp.bfloat16),
            in_specs=[VMEM],
            out_specs=VMEM,
            compiler_params=params,
            cost_estimate=pl.CostEstimate(
                flops=6 * groups * half, bytes_accessed=10 * groups * half, transcendentals=0
            ),
            name=name,
        )(values)

    noise_thirds = in_thirds(noise_weight, "noise")
    if by_distance:
        pair = jnp.zeros((2, per_device, full + LANES), images.dtype)
        pair = lax.dynamic_update_slice(pair, rows, (0, 0, 0))
        pair = lax.dynamic_update_slice(pair, numbers, (0, 0, full))
        pair, ctf_late = lax.optimization_barrier((pair, ctf_table))
        ctf_thirds = in_thirds(ctf_late, "ctf")
        pair = lax.dynamic_update_slice(pair, received, (1, 0, 0))
        received_numbers, ctf_thirds = lax.optimization_barrier(
            (received_numbers, ctf_thirds)
        )
        pair = lax.dynamic_update_slice(pair, received_numbers, (1, 0, full))
        pieces = [pair] + [swap(pair, mask) for mask in range(4, axis_size, 4)]
        parts = [(pieces[:2], ((0, 1), (2, 3))), (pieces[2:], ((4, 5), (6, 7)))]
    else:
        same_core = [[2 * c + core for c in range(chips)] for core in range(2)]
        ctf_thirds = in_thirds(ctf_table, "ctf")
        gathered = lax.all_gather(
            jnp.concatenate([rows, numbers], axis=2), "blk", axis=0, tiled=True, axis_index_groups=same_core
        )
        parts = [([gathered], (tuple(range(chips)),))]

    earlier = ()
    for number, (pieces, sources) in enumerate(parts):
        last = number == len(parts) - 1
        own_blocks = blocks // len(parts)
        seen = blocks if last else own_blocks
        exps_shape = jax.ShapeDtypeStruct((seen, own_rows, block_rows), jnp.float32)
        earlier = pl.pallas_call(
            functools.partial(score_kernel, sources, by_distance, shifts, bool(earlier)),
            out_shape=(
                jax.ShapeDtypeStruct(
                    (blocks * block_rows, full + (3 * blocks * LANES if by_distance else 0)),
                    jnp.bfloat16,
                ),
                *([exps_shape] if earlier else [exps_shape] * 2),
                jax.ShapeDtypeStruct(
                    (axis_size if last else 1, 1 if by_distance else blocks, LANES), jnp.float32
                ),
            ),
            in_specs=[VMEM] * (len(pieces) + 5 + len(earlier)),
            out_specs=(VMEM,) * (3 if earlier else 4),
            scratch_shapes=[
                pltpu.VMEM((own_blocks * ROWS, full + LANES), jnp.float32),
                pltpu.VMEM((ROWS, half), jnp.float32),
                pltpu.VMEM((ROWS, half), jnp.float32),
                pltpu.VMEM((block_rows, candidates), jnp.float32),
                pltpu.VMEM((-(-block_rows // LANES) * LANES, LANES), jnp.float32),
            ],
            input_output_aliases={len(pieces) + 5: 0} if earlier else {},
            compiler_params=params,
            cost_estimate=pl.CostEstimate(
                flops=2 * own_blocks * block_rows * full * (candidates + 8),
                bytes_accessed=2 * own_blocks * block_rows * full,
                transcendentals=0,
            ),
            name="scores",
        )(*pieces, both, high, low, ctf_thirds, noise_thirds, *earlier)
    weighted, exps, *exps_other, stats = earlier

    all_weighted = [weighted]
    exchanged = [swap(weighted, 1)]
    exps_in = [swap(part, 1) for part in exps_other]
    gathered = lax.all_to_all(stats, "blk", 0, 0)
    gathered = gathered.reshape((chips, 2) + gathered.shape[1:])

    slices, best_posterior, log_total = pl.pallas_call(
        functools.partial(
            slice_kernel, own_rows / per_device, len(all_weighted), by_distance
        ),
        out_shape=(
            jax.ShapeDtypeStruct((own_rows, full), jnp.float32),
            jax.ShapeDtypeStruct((per_device,), jnp.float32),
            jax.ShapeDtypeStruct((per_device,), jnp.float32),
        ),
        in_specs=[VMEM] * (2 + len(exps_in) + 2 * len(all_weighted)),
        out_specs=(HBM, HBM, HBM),
        scratch_shapes=[
            pltpu.SMEM((per_device,), jnp.float32),
            pltpu.SMEM((per_device,), jnp.float32),
            pltpu.VMEM((2, blocks, own_rows, block_rows), jnp.bfloat16),
            pltpu.VMEM((own_rows, full), jnp.float32),
            pltpu.SemaphoreType.DMA((full // 1024,)),
            pltpu.SemaphoreType.DMA((2,)),
        ],
        compiler_params=params,
        name="slices",
    )(gathered, exps, *exps_in, *all_weighted, *exchanged)
    return (slices.reshape(batch_count, orient_dev, full), best_posterior, log_total)


def solution(mesh):
    in_specs = (
        P(None, ("groups", "blk"), None),
        P(("groups", "blk"), None),
        P(("groups", "blk")),
        P(("groups", "blk"), None, None),
        P(("groups", "blk")),
        P("groups", None),
        P("groups", None),
    )
    out_specs = (P(None, ("groups", "blk"), None), P(("groups", "blk")), P(("groups", "blk")))
    return jax.shard_map(
        functools.partial(local, mesh.shape["blk"]),
        mesh=mesh,
        in_specs=in_specs,
        out_specs=out_specs,
        check_vma=False,
    )
```
